256 devices in a mesh: span: 4 (over x), tile: 64 (over y, z, core).
Axes of the slice: x: 4, y: 4, z: 8, core: 2. Of those that a mesh axis runs over, the one named last changes fastest.
Arguments:
- latents: bfloat16 [8, 128, 64, 384], P('span', 'tile'), may hold values from -6 to 6
- gain_first: float32 [384], replicated, may hold values from 0.1 to 1.9
- conv_first: bfloat16 [3, 3, 3, 384, 384], P(None, None, None, 'tile'), may hold values from -0.0625 to 0.0625
- bias_first: float32 [384], replicated, may hold values from -3 to 3
- gain_second: float32 [384], replicated, may hold values from 0.1 to 1.9
- conv_second: bfloat16 [3, 3, 3, 384, 384], P(None, None, None, 'tile'), may hold values from -0.0625 to 0.0625
- bias_second: float32 [384], replicated, may hold values from -3 to 3
Outputs:
- decoded: bfloat16 [8, 128, 64, 384], P('span', 'tile')
The draws below stay inside these ranges and needn't reach their ends.
All inputs are finite; a program needn't handle non-finite values.
Results may differ from the reference program's by a relative error of at most 0.0034.
Values may be sent and summed in bfloat16 or wider, within the bound.
A program may use at most 128 MiB of HBM per device.

```python
import jax
import jax.numpy as jnp
from jax import lax

C = 384
W = 64
FRAMES = 8
H = 128


def levels(key, extent, split, smallest, high):
    def one(position, parts):
        draws = jax.random.uniform(jax.random.fold_in(jax.random.fold_in(key, 6), position), (parts,), jnp.float32, smallest / len(split), high / len(split))
        return jnp.repeat(jnp.exp(draws), extent[position] // parts).reshape((-1,) + (1,) * (len(extent) - position - 1))

    level = one(*split[0])
    for cut in split[1:]:
        level = level * one(*cut)
    return level


def noise(key, shape, width, limit, cuts=(), kind=jnp.bfloat16):
    loudness = levels(key, shape, cuts, -0.22, 0.18) if cuts else 1.0
    drawn = jax.random.normal(key, shape, jnp.float32) * width * loudness
    return jnp.minimum(jnp.maximum(drawn, -limit), limit).astype(kind)


def setup_inputs(seed: int = 0) -> dict:
    key_list = jax.random.split(jax.random.key(seed), 8)
    return {
        "latents": noise(key_list[0], (FRAMES, H, W, C), 1.0, 6.0, ((0, 4), (1, 64))),
        "gain_first": jnp.clip(1.0 + 0.18 * jax.random.normal(key_list[1], (C,), jnp.float32), 0.1, 1.9),
        "conv_first": noise(key_list[2], (3, 3, 3, C, C), (27 * C) ** -0.5, 0.0625, ((3, 64),)),
        "bias_first": noise(key_list[3], (C,), 0.5, 3.0, (), jnp.float32),
        "gain_second": jnp.clip(1.0 + 0.18 * jax.random.normal(key_list[4], (C,), jnp.float32), 0.1, 1.9),
        "conv_second": noise(key_list[5], (3, 3, 3, C, C), (27 * C) ** -0.5, 0.0625, ((3, 64),)),
        "bias_second": noise(key_list[6], (C,), 0.5, 3.0, (), jnp.float32),
    }


def activate(values, gain):
    mean_square = lax.optimization_barrier(jnp.mean(values * values, axis=-1, keepdims=True))
    scaled = values * lax.rsqrt(mean_square + 1e-06) * gain
    return jax.nn.silu(scaled).astype(jnp.bfloat16)

def convolve(active, kernel, bias):
    frames, rows, cols, channels = active.shape
    padded = jnp.pad(active, ((2, 0), (1, 1), (1, 1), (0, 0)))
    kernel_wide = kernel.astype(jnp.float32)

    def one_frame(index):
        total = jnp.zeros((rows * cols, channels), jnp.float32)
        for depth in range(3):
            plane = lax.dynamic_index_in_dim(padded, index + depth, 0, keepdims=False)
            for lift in range(3):
                for slide in range(3):
                    view = plane[lift:lift + rows, slide:slide + cols, :].reshape(rows * cols, channels)
                    total = total + jnp.dot(view.astype(jnp.float32), kernel_wide[depth, lift, slide], precision=lax.Precision.HIGHEST)
        return total + bias
    result = lax.map(one_frame, jnp.arange(frames, dtype=jnp.int32))
    return result.reshape(frames, rows, cols, channels)

def reference(latents, gain_first, conv_first, bias_first, gain_second, conv_second, bias_second):
    base = latents.astype(jnp.float32)
    active_first = activate(base, gain_first)
    hidden_first = convolve(active_first, conv_first, bias_first)
    active_second = activate(hidden_first, gain_second)
    hidden_second = convolve(active_second, conv_second, bias_second)
    return (base + hidden_second).astype(jnp.bfloat16)
```

```python
import jax
import jax.numpy as jnp
import numpy as np
from jax import lax
from jax.experimental import pallas as pl
from jax.experimental.pallas import tpu as pltpu
from jax.sharding import PartitionSpec as P

MESH = pl.DeviceIdType.MESH
F32 = jnp.float32
BF16 = jnp.bfloat16

SLOTS = ((0, 1), (0, 0), (0, 2), (2, 0), (1, 1), (1, 0), (1, 2), (2, 2), (2, 1))


def one_hot_first():
    pick = np.zeros((144, 256), np.float32)
    for dy in range(3):
        for member in range(8):
            for channel in range(6):
                pick[dy * 48 + member * 6 + channel, member * 32 + dy * 6 + channel] = 1
    return pick


def one_hot_second():
    pick = np.zeros((48, 128), np.float32)
    for member in range(8):
        for channel in range(6):
            pick[member * 6 + channel, member * 16 + channel] = 1
    return pick


def silu(u):
    return u / (1.0 + jnp.exp(-u))


def kernel(
    lat, gain1, bias1, gain2, bias2, s1, s2, pick1, pick2, out,
    r1, r2, w1, w2, abuf, pbuf, hbuf, ssbuf, a2s, a2h, sendb, recvb,
    st1s, st1r, st2s, st2r, loc,
    ysend, yrecv, rsend, rrecv, bsend, brecv,
    xs, xr, ups, upr, dns, dnr, sss, ssr, h2s, h2r, fs, fr,
):
    x = lax.axis_index("span")
    t = lax.axis_index("tile")
    c = lax.rem(t, 2)
    z = lax.rem(lax.div(t, 2), 8)
    y = lax.div(t, 16)
    zi = lax.rem(z, 4)
    h = lax.div(z, 4)
    j = lax.rem(t, 8)
    g = lax.div(t, 8)

    def dev(yy, zz, cc):
        return (x, yy * 16 + zz * 2 + cc)

    def rc(src, dst, ssem, rsem, device):
        return pltpu.make_async_remote_copy(
            src_ref=src, dst_ref=dst, send_sem=ssem, recv_sem=rsem,
            device_id=device, device_id_type=MESH,
        )

    barrier = pltpu.get_barrier_semaphore()

    def hail(device):
        pl.semaphore_signal(barrier, inc=1, device_id=device, device_id_type=MESH)

    for d in range(1, 8):
        hail((x, g * 8 + lax.rem(j + d, 8)))

    @pl.when(x != y)
    def _():
        for d in range(8):
            hail((y, x * 16 + h * 8 + lax.rem(j + d, 8)))

    for d in range(1, 4):
        hail((lax.rem(x + d, 4), t))
    for d in range(1, 4):
        hail(dev(lax.rem(y + d, 4), z, c))
    zr = lax.rem(z + 1, 8)
    zl = lax.rem(z + 7, 8)
    hail(dev(y, zr, c))
    hail(dev(y, zl, c))

    @pl.when(t > 0)
    def _():
        hail((x, t - 1))

    @pl.when(t < 63)
    def _():
        hail((x, t + 1))

    w2[:, :, :, 96:128, :] = jnp.zeros((4, 4, 2, 32, 384), BF16)
    a2s[:, 0:2] = jnp.zeros((3, 2, 4, 64, 128), BF16)

    def zero_p(i, carry):
        pbuf[i, 0:2] = jnp.zeros((2, 2, 64, 256), F32)
        return carry

    lax.fori_loop(0, 4, zero_p, 0)

    def act1(i, carry):
        v = lat[i].reshape(128, 384).astype(F32)
        ms = jnp.mean(v * v, axis=-1, keepdims=True)
        u = v * lax.rsqrt(ms + 1e-6) * gain1[...]
        abuf[x, i, 1:3] = silu(u).astype(BF16).reshape(2, 64, 384)
        return carry

    lax.fori_loop(0, 2, act1, 0)

    many = jnp.where(x != y, 8, 0) + jnp.where(t > 0, 1, 0) + jnp.where(t < 63, 1, 0) + 15
    pl.semaphore_wait(barrier, many)

    def st1(d):
        jj = lax.rem(j + d, 8)
        return rc(s1.at[jj], r1.at[j], st1s.at[d], st1r.at[d], (x, g * 8 + jj))

    def st2(d):
        jj = lax.rem(j + d, 8)
        return rc(s2.at[jj], r2.at[j], st2s.at[d], st2r.at[d], (y, x * 16 + h * 8 + jj))

    def own2():
        return pltpu.make_async_copy(s2.at[j], r2.at[j], loc.at[1])

    for d in range(1, 8):
        st1(d).start()
    own1 = pltpu.make_async_copy(s1.at[j], r1.at[j], loc.at[0])
    own1.start()

    def xsend(d):
        return rc(
            abuf.at[x, :, 1:3], abuf.at[x, :, 1:3], xs.at[d], xr.at[d], (lax.rem(x + d, 4), t)
        )

    def up(src, d):
        return rc(abuf.at[src, :, 1], abuf.at[src, :, 3], ups.at[d], upr.at[d], (x, t - 1))

    def down(src, d):
        return rc(abuf.at[src, :, 2], abuf.at[src, :, 0], dns.at[d], dnr.at[d], (x, t + 1))

    def halo_send(d):
        src = lax.rem(x + 4 - d, 4)

        @pl.when(t > 0)
        def _():
            up(src, d).start()

        @pl.when(t < 63)
        def _():
            down(src, d).start()

    def xstep(d):
        src = lax.rem(x + 4 - d, 4)
        land = abuf.at[src, :, 1:3]
        rc(land, land, xs.at[d], xr.at[d], (x, t)).wait_recv()
        halo_send(d)

    def halo_wait():
        for d in range(4):
            src = lax.rem(x + 4 - d, 4)

            @pl.when(t > 0)
            def _():
                land = abuf.at[src, :, 0]
                rc(land, land, dns.at[d], dnr.at[d], (x, t)).wait_recv()

            @pl.when(t < 63)
            def _():
                land = abuf.at[src, :, 3]
                rc(land, land, ups.at[d], upr.at[d], (x, t)).wait_recv()

        @pl.when(t == 0)
        def _():
            abuf[:, :, 0] = jnp.zeros((4, 2, 64, 384), BF16)

        @pl.when(t == 63)
        def _():
            abuf[:, :, 3] = jnp.zeros((4, 2, 64, 384), BF16)

    for d in range(1, 4):
        xsend(d).start()
    for d in range(8):
        if d == 0:

            @pl.when(x != y)
            def _():
                st2(0).start()

            @pl.when(x == y)
            def _():
                own2().start()
        else:
            st2(d).start()
    halo_send(0)

    def own_slice(k):
        if k == 0:
            return w1.at[c, zi, :, y, h]
        return w2.at[y, zi, c, pl.ds(pl.multiple_of(48 * h, 16), 48), :]

    def blk(k, yy, zz, cc):
        if k == 0:
            return w1.at[cc, lax.rem(zz, 4), :, yy, lax.div(zz, 4)]
        return w2.at[yy, lax.rem(zz, 4), cc, pl.ds(pl.multiple_of(48 * lax.div(zz, 4), 16), 48), :]

    def half(k, zz, hf):
        if k == 0:
            return w1.at[0, lax.rem(zz, 4), :, 2 * hf:2 * hf + 2, lax.div(zz, 4)]
        return w2.at[2 * hf:2 * hf + 2, lax.rem(zz, 4), 0, pl.ds(pl.multiple_of(48 * lax.div(zz, 4), 16), 48), :]

    def zset(k, zz):
        if k == 0:
            return w1.at[0, lax.rem(zz, 4), :, :, lax.div(zz, 4)]
        return w2.at[:, lax.rem(zz, 4), 0, pl.ds(pl.multiple_of(48 * lax.div(zz, 4), 16), 48), :]

    def yset(k, yy):
        if k == 0:
            return w1.at[1, :, :, yy]
        return w2.at[yy, :, 1, 0:96, :]

    def yhalf(k, yy, a):
        if k == 0:
            return w1.at[1, 2 * a:2 * a + 2, :, yy]
        return w2.at[yy, 2 * a:2 * a + 2, 1, 0:96, :]

    sent_a, sent_b = [], []

    def go(group, make):
        make().start()
        group.append(make)

    def got(ref, rsem):
        rc(ref, ref, loc.at[2], rsem, (x, t)).wait_recv()

    def zz(s):
        return lax.rem(z + 8 + s, 8)

    ring_dev = (dev(y, zr, c), dev(y, zl, c))

    def a_ring(k, way, s, hf, origin):
        def make():
            ref = half(k, zz(origin), hf)
            return rc(ref, ref, rsend.at[k, way, s, hf], rrecv.at[k, way, s + 1, hf], ring_dev[way])

        go(sent_a, make)

    def a_sib(k, idx, origin):
        def make():
            ref = zset(k, zz(origin))
            return rc(ref, ref, bsend.at[k, idx], brecv.at[k, idx], dev(y, z, 1))

        go(sent_a, make)

    def b_ring(k, way, s, origin):
        def make():
            ref = blk(k, y, zz(origin), 1)
            return rc(ref, ref, rsend.at[k, way, s, 0], rrecv.at[k, way, s + 1, 0], ring_dev[way])

        go(sent_b, make)

    def b_sib(k, d):
        def make():
            ref = yset(k, lax.rem(y + d, 4))
            return rc(ref, ref, bsend.at[k, d], brecv.at[k, d], dev(y, z, 0))

        go(sent_b, make)

    def a_y(k, d):
        def make():
            ref = blk(k, y, z, 0)
            return rc(ref, ref, ysend.at[k, d], yrecv.at[k, d], dev(lax.rem(y + d, 4), z, 0))

        go(sent_a, make)

    def b_y(k, idx, origin, a, to):
        def make():
            ref = yhalf(k, lax.rem(y + origin, 4), a)
            return rc(ref, ref, ysend.at[k, idx], yrecv.at[k, idx], dev(lax.rem(y + to, 4), z, 1))

        go(sent_b, make)

    def step(k, n):
        @pl.when(c == 0)
        def _():
            if n == 0:
                for d in range(1, 4):
                    a_y(k, d)
            if n == 1:
                for d in range(1, 4):
                    got(blk(k, lax.rem(y + 4 - d, 4), z, 0), yrecv.at[k, d])
                for hf in range(2):
                    for way in range(2):
                        a_ring(k, way, 0, hf, 0)
                a_sib(k, 0, 0)
            if n in (2, 3, 4):
                s = n - 1
                for hf in range(2):
                    for way, origin in ((0, -s), (1, s)):
                        got(half(k, zz(origin), hf), rrecv.at[k, way, s, hf])
                        if s < 3 or hf == way:
                            a_ring(k, way, s, hf, origin)
                a_sib(k, 2 * s - 1, -s)
                a_sib(k, 2 * s, s)
            if n == 5:
                for way in range(2):
                    got(half(k, zz(4), way), rrecv.at[k, way, 4, way])
                a_sib(k, 7, 4)
            if n == 7:
                for d in range(4):
                    got(yset(k, lax.rem(y + d, 4)), brecv.at[k, d])

        @pl.when(c == 1)
        def _():
            if n == 0:
                for way in range(2):
                    b_ring(k, way, 0, 0)
            if n in (1, 2, 3):
                s = n
                for way, origin in ((0, -s), (1, s)):
                    got(blk(k, y, zz(origin), 1), rrecv.at[k, way, s, 0])
                    if s < 3 or way == 0:
                        b_ring(k, way, s, origin)
            if n == 4:
                got(blk(k, y, zz(4), 1), rrecv.at[k, 0, 4, 0])
                for a in range(2):
                    b_y(k, a, 0, a, 1)
                    b_y(k, 3 - a, 0, 1 - a, 3)
                b_sib(k, 0)
            if n == 5:
                below, above = lax.rem(y + 3, 4), lax.rem(y + 1, 4)
                got(yhalf(k, below, 0), yrecv.at[k, 0])
                b_y(k, 4, 3, 0, 1)
                got(yhalf(k, above, 1), yrecv.at[k, 3])
                b_y(k, 5, 1, 1, 3)
                got(yhalf(k, below, 1), yrecv.at[k, 1])
                got(yhalf(k, above, 0), yrecv.at[k, 2])
                b_sib(k, 3)
                b_sib(k, 1)
            if n == 6:
                got(yhalf(k, lax.rem(y + 2, 4), 0), yrecv.at[k, 4])
                got(yhalf(k, lax.rem(y + 2, 4), 1), yrecv.at[k, 5])
                b_sib(k, 2)
            if n == 7:
                for idx, s in enumerate((0, -1, 1, -2, 2, -3, 3, 4)):
                    got(zset(k, zz(s)), brecv.at[k, idx])

    own1.wait()
    for d in range(1, 8):
        got(r1.at[lax.rem(j + 8 - d, 8)], st1r.at[d])
    chunk = jnp.dot(pick1[...], r1[...].reshape(256, 128), preferred_element_type=F32).astype(BF16)
    for dy in range(3):
        w1[c, zi, dy, y, h] = chunk[dy * 48:dy * 48 + 48]
    step(0, 0)

    @pl.when(x != y)
    def _():
        got(r2.at[j], st2r.at[0])

    @pl.when(x == y)
    def _():
        own2().wait()

    for d in range(1, 8):
        got(r2.at[lax.rem(j + 8 - d, 8)], st2r.at[d])
    chunk2 = jnp.dot(pick2[...], r2[...].reshape(128, 384), preferred_element_type=F32).astype(BF16)
    w2[y, zi, c, pl.ds(pl.multiple_of(48 * h, 16), 48), :] = chunk2
    step(0, 1)
    step(1, 0)
    xstep(1)
    step(0, 2)
    xstep(3)
    step(0, 3)
    xstep(2)
    step(0, 4)
    step(0, 5)
    step(1, 1)
    step(0, 6)
    step(0, 7)
    halo_wait()

    def conv1(fp):
        rows = []
        for yy in range(2):
            rows.append(jnp.concatenate(
                [abuf[fp, :, yy + dy].reshape(128, 384) for dy in range(3)], axis=1))
        lhs = jnp.concatenate(rows, axis=0)

        def tile(n, carry):
            rhs = jnp.concatenate(
                [w1[0, n].reshape(1152, 128), w1[1, n].reshape(1152, 128)], axis=1)
            res = jnp.dot(lhs, rhs, preferred_element_type=F32)
            for yy in range(2):
                pbuf[n, 2 + 2 * fp:4 + 2 * fp, yy] = res[yy * 128:yy * 128 + 128].reshape(2, 64, 256)
            return carry

        lax.fori_loop(0, 4, tile, 0)

    for fp in range(4):
        conv1(fp)
        step(1, 2 + fp)

    lane = lax.broadcasted_iota(jnp.int32, (64, 128), 1)
    row = lax.broadcasted_iota(jnp.int32, (64, 128), 0)

    def shift_down(v):
        return jnp.where(row > 0, pltpu.roll(v, 1, 0), 0.0)

    def shift_up(v):
        return jnp.where(row < 63, pltpu.roll(v, 63, 0), 0.0)

    def combine(f, carry):
        for yy in range(2):
            def p(dt, n):
                return pbuf[n // 2, f + dt, yy, :, (n % 2) * 128:(n % 2) * 128 + 128]

            m1 = p(0, 0) + p(1, 3) + p(2, 6)
            a_lo = p(0, 0) + p(1, 3)
            mid = p(0, 1) + p(1, 4)
            b_hi = p(0, 2) + p(1, 5)
            m0 = pltpu.roll(jnp.where(lane >= 96, a_lo, mid), 32, 1) + pltpu.roll(p(2, 2), 96, 1)
            m2 = pltpu.roll(jnp.where(lane >= 64, mid, b_hi), 64, 1) + pltpu.roll(p(2, 5), 96, 1)
            hid = m1 + shift_down(m0) + shift_up(m2) + bias1[...]
            hbuf[f, yy] = jnp.where(lane < 96, hid, 0.0)
        return carry

    lax.fori_loop(0, 8, combine, 0)

    hv = hbuf[...].reshape(1024, 128)
    ssbuf[0] = lax.dot_general(
        jnp.ones((8, 128), F32), hv * hv, (((1,), (1,)), ((), ())),
        precision=lax.Precision.HIGHEST, preferred_element_type=F32,
    )

    def ss_send(d):
        return rc(ssbuf.at[0], ssbuf.at[d], sss.at[d], ssr.at[d], (lax.rem(x + d, 4), t))

    for d in range(1, 4):
        ss_send(d).start()
    step(1, 6)
    for d in range(1, 4):
        got(ssbuf.at[d], ssr.at[d])
    total = ssbuf[0] + ssbuf[1] + ssbuf[2] + ssbuf[3]
    ms = lax.dot_general(
        total, jnp.full((8, 128), 0.125, F32), (((0,), (0,)), ((), ())),
        precision=lax.Precision.HIGHEST, preferred_element_type=F32,
    ) * (1.0 / 384.0)
    hv = hbuf[...].reshape(1024, 128)
    hbuf[...] = (hv * lax.rsqrt(ms + 1e-6) * gain2[...]).reshape(8, 2, 64, 128)

    def spread(f, where, v):
        a2s[0, f + 2, where] = shift_down(v).astype(BF16)
        a2s[1, f + 2, where] = v.astype(BF16)
        a2s[2, f + 2, where] = shift_up(v).astype(BF16)

    def act2(f, carry):
        for yy in range(2):
            spread(f, 1 + yy, silu(hbuf[f, yy]))
        return carry

    lax.fori_loop(0, 8, act2, 0)

    def h2up():
        return rc(a2s.at[1, 2:10, 1], a2h.at[1], h2s.at[0], h2r.at[0], (x, t - 1))

    def h2down():
        return rc(a2s.at[1, 2:10, 2], a2h.at[0], h2s.at[1], h2r.at[1], (x, t + 1))

    @pl.when(t > 0)
    def _():
        h2up().start()

    @pl.when(t < 63)
    def _():
        h2down().start()

    step(1, 7)

    @pl.when(t > 0)
    def _():
        got(a2h.at[0], h2r.at[1])

    @pl.when(t == 0)
    def _():
        a2h[0] = jnp.zeros((8, 64, 128), BF16)

    @pl.when(t < 63)
    def _():
        got(a2h.at[1], h2r.at[0])

    @pl.when(t == 63)
    def _():
        a2h[1] = jnp.zeros((8, 64, 128), BF16)

    def halo2(f, carry):
        spread(f, 0, a2h[0, f].astype(F32))
        spread(f, 3, a2h[1, f].astype(F32))
        return carry

    lax.fori_loop(0, 8, halo2, 0)

    def conv2(q):
        acc = None
        for dt in range(3):
            lhs, rhs = [], []
            for dy in range(3):
                for dx in range(3):
                    tap = dt * 9 + dy * 3 + dx
                    lhs.append(a2s[dx, pl.ds(2 * q + dt, 2), dy:dy + 2].reshape(256, 128))
                    rhs.append(w2[tap // 8, (tap % 8) // 2, tap % 2])
            part = jnp.dot(
                jnp.concatenate(lhs, axis=1), jnp.concatenate(rhs, axis=0),
                preferred_element_type=F32,
            )
            acc = part if acc is None else acc + part
        return acc

    def out_send(d):
        return rc(sendb.at[d - 1], recvb.at[d - 1], fs.at[d], fr.at[d], (lax.rem(x + d, 4), t))

    for d in (2, 1, 3):
        sendb[d - 1] = conv2(lax.rem(x + d, 4)).astype(BF16).reshape(2, 2, 64, 384)
        out_send(d).start()
    mine = conv2(x) + bias2[...] + lat[...].reshape(256, 384).astype(F32)
    for d in (2, 1, 3):
        got(recvb.at[d - 1], fr.at[d])
        mine = mine + recvb[d - 1].reshape(256, 384).astype(F32)
    out[...] = mine.astype(BF16).reshape(2, 2, 64, 384)

    for d in range(1, 8):
        st1(d).wait_send()
        st2(d).wait_send()

    @pl.when(x != y)
    def _():
        st2(0).wait_send()

    for d in range(1, 4):
        xsend(d).wait_send()
        ss_send(d).wait_send()
        out_send(d).wait_send()

    @pl.when(t > 0)
    def _():
        for d in range(4):
            up(lax.rem(x + 4 - d, 4), d).wait_send()
        h2up().wait_send()

    @pl.when(t < 63)
    def _():
        for d in range(4):
            down(lax.rem(x + 4 - d, 4), d).wait_send()
        h2down().wait_send()

    @pl.when(c == 0)
    def _():
        for make in sent_a:
            make().wait_send()

    @pl.when(c == 1)
    def _():
        for make in sent_b:
            make().wait_send()


def per_device(latents, gain_first, conv_first, bias_first, gain_second, conv_second, bias_second):
    x = lax.axis_index("span")
    w = lax.dynamic_slice_in_dim(conv_first, 96 * x, 96, axis=4)
    w = jnp.stack([w[dt, :, dx] for dt, dx in SLOTS], axis=2)
    w = w.reshape(18, 864)
    w = jnp.pad(w, ((0, 14), (0, 160))).reshape(32, 8, 128)
    s1 = jnp.transpose(w, (1, 0, 2))
    v = jnp.pad(conv_second.reshape(27, 6, 384), ((0, 5), (0, 10), (0, 0)))
    s2 = lax.dynamic_slice_in_dim(v, 8 * x, 8, axis=0)

    def part(vec):
        return jnp.pad(lax.dynamic_slice_in_dim(vec, 96 * x, 96), (0, 32)).reshape(1, 128)

    vm = pl.BlockSpec(memory_space=pltpu.VMEM)
    dma = pltpu.SemaphoreType.DMA
    return pl.pallas_call(
        kernel,
        out_shape=jax.ShapeDtypeStruct((2, 2, 64, 384), BF16),
        in_specs=[vm] * 9,
        out_specs=vm,
        scratch_shapes=[
            pltpu.VMEM((8, 32, 128), BF16),
            pltpu.VMEM((8, 16, 384), BF16),
            pltpu.VMEM((2, 4, 3, 4, 2, 48, 128), BF16),
            pltpu.VMEM((4, 4, 2, 128, 384), BF16),
            pltpu.VMEM((4, 2, 4, 64, 384), BF16),
            pltpu.VMEM((4, 10, 2, 64, 256), F32),
            pltpu.VMEM((8, 2, 64, 128), F32),
            pltpu.VMEM((4, 8, 1024), F32),
            pltpu.VMEM((3, 10, 4, 64, 128), BF16),
            pltpu.VMEM((2, 8, 64, 128), BF16),
            pltpu.VMEM((3, 2, 2, 64, 384), BF16),
            pltpu.VMEM((3, 2, 2, 64, 384), BF16),
            dma((8,)), dma((8,)), dma((8,)), dma((8,)), dma((3,)),
            dma((2, 6)), dma((2, 6)), dma((2, 2, 4, 2)), dma((2, 2, 5, 2)), dma((2, 8)), dma((2, 8)),
            dma((4,)), dma((4,)), dma((4,)), dma((4,)), dma((4,)), dma((4,)),
            dma((4,)), dma((4,)), dma((2,)), dma((2,)), dma((4,)), dma((4,)),
        ],
        compiler_params=pltpu.CompilerParams(
            collective_id=0, has_side_effects=True, vmem_limit_bytes=48 * 1024 * 1024
        ),
        cost_estimate=pl.CostEstimate(flops=4_000_000_000, bytes_accessed=8_000_000, transcendentals=400_000),
    )(
        latents, gain_first.reshape(1, 384), part(bias_first), part(gain_second),
        bias_second.reshape(1, 384), s1, s2,
        jnp.asarray(one_hot_first(), BF16), jnp.asarray(one_hot_second(), BF16),
    )


def solution(mesh):
    in_specs = (
        P("span", "tile", None, None),
        P(),
        P(None, None, None, "tile", None),
        P(),
        P(),
        P(None, None, None, "tile", None),
        P(),
    )
    out_specs = P("span", "tile", None, None)
    return jax.shard_map(
        per_device, mesh=mesh, in_specs=in_specs, out_specs=out_specs, check_vma=False
    )
```

```python
import jax
import jax.numpy as jnp
from jax import lax
from jax.experimental import pallas as pl
from jax.experimental.pallas import tpu as pltpu
from jax.sharding import PartitionSpec as P

MESH = pl.DeviceIdType.MESH
F32 = jnp.float32
BF16 = jnp.bfloat16

SLOTS = ((0, 1), (0, 0), (0, 2), (2, 0), (1, 1), (1, 0), (1, 2), (2, 2), (2, 1))


def silu(u):
    return u / (1.0 + jnp.exp(-u))


def kernel(
    lat_hbm, gain1_hbm, bias1_hbm, gain2_hbm, bias2_hbm, k1_hbm, k2_hbm, out,
    lat, vec, k1, k2, s1, s2, stack,
    r1, r2, w1, w2, abuf, pbuf, hbuf, ssbuf, a2s, a2h, sendb, recvb,
    ins, st1s, st1r, st2s, st2r, loc,
    ysend, yrecv, rsend, rrecv, bsend, brecv,
    xs, xr, ups, upr, dns, dnr, sss, ssr, h2s, h2r, fs, fr,
):
    x = lax.axis_index("span")
    t = lax.axis_index("tile")
    c = lax.rem(t, 2)
    z = lax.rem(lax.div(t, 2), 8)
    y = lax.div(t, 16)
    zi = lax.rem(z, 4)
    h = lax.div(z, 4)
    j = lax.rem(t, 8)
    g = lax.div(t, 8)

    def dev(yy, zz, cc):
        return (x, yy * 16 + zz * 2 + cc)

    def rc(src, dst, ssem, rsem, device):
        return pltpu.make_async_remote_copy(
            src_ref=src, dst_ref=dst, send_sem=ssem, recv_sem=rsem,
            device_id=device, device_id_type=MESH,
        )

    loads = [
        pltpu.make_async_copy(k1_hbm, k1, ins.at[0]),
        pltpu.make_async_copy(lat_hbm, lat, ins.at[1]),
        pltpu.make_async_copy(k2_hbm, k2, ins.at[2]),
        pltpu.make_async_copy(gain1_hbm, vec.at[0], ins.at[3]),
        pltpu.make_async_copy(bias1_hbm, vec.at[1], ins.at[4]),
        pltpu.make_async_copy(gain2_hbm, vec.at[2], ins.at[5]),
        pltpu.make_async_copy(bias2_hbm, vec.at[3], ins.at[6]),
    ]
    for load in loads:
        load.start()

    barrier = pltpu.get_barrier_semaphore()

    def hail(device):
        pl.semaphore_signal(barrier, inc=1, device_id=device, device_id_type=MESH)

    for d in range(1, 8):
        hail((x, g * 8 + lax.rem(j + d, 8)))

    @pl.when(x != y)
    def _():
        for d in range(8):
            hail((y, x * 16 + h * 8 + lax.rem(j + d, 8)))

    for d in range(1, 4):
        hail((lax.rem(x + d, 4), t))
    for d in range(1, 4):
        hail(dev(lax.rem(y + d, 4), z, c))
    for d in (1, 2, 6, 7):
        hail(dev(y, lax.rem(z + d, 8), c))

    @pl.when(t > 0)
    def _():
        hail((x, t - 1))

    @pl.when(t < 63)
    def _():
        hail((x, t + 1))

    lane8 = lax.broadcasted_iota(jnp.int32, (8, 128), 1)
    turn = lax.rem(384 - 96 * x, 384)

    def mine96(v):
        return pltpu.roll(v, turn, 1)[:, 0:128]

    loads[0].wait()
    pad2 = jnp.zeros((2, 384), F32)
    tiles = []
    for dy in range(3):
        got_slots = []
        for dt, dx in SLOTS:
            got_slots.append(mine96(jnp.concatenate([k1[dt * 9 + dy * 3 + dx].astype(F32), pad2], axis=0)))

        def at(n, by):
            return pltpu.roll(got_slots[n], by, 1) if by else got_slots[n]

        row = [
            jnp.where(lane8 < 96, at(0, 0), at(1, 96)),
            jnp.where(lane8 < 64, at(1, 96), at(2, 64)),
            jnp.where(lane8 < 32, at(2, 64), at(3, 32)),
            jnp.where(lane8 < 96, at(4, 0), at(5, 96)),
            jnp.where(lane8 < 64, at(5, 96), at(6, 64)),
            jnp.where(lane8 < 32, at(6, 64), at(7, 32)),
            jnp.where(lane8 < 96, at(8, 0), 0.0),
            jnp.zeros((8, 128), F32),
        ]
        tiles.append(row)
    for n in range(8):
        s1[n, 0:16] = jnp.concatenate([tiles[0][n], tiles[1][n]], axis=0).astype(BF16)
        s1[n, 16:32] = jnp.concatenate([tiles[2][n], jnp.zeros((8, 128), F32)], axis=0).astype(BF16)
    loads[2].wait()
    for n in range(8):
        tap = jnp.minimum(8 * x + n, 26)
        s2[n] = jnp.concatenate([k2[tap].astype(F32), jnp.zeros((10, 384), F32)], axis=0).astype(BF16)
    for load in loads[3:]:
        load.wait()
    loads[1].wait()
    gain1 = vec[0:1]
    bias2 = vec[3:4]
    bias1 = jnp.where(lane8[0:1] < 96, mine96(jnp.broadcast_to(vec[1:2], (8, 384)))[0:1], 0.0)
    gain2 = jnp.where(lane8[0:1] < 96, mine96(jnp.broadcast_to(vec[2:3], (8, 384)))[0:1], 0.0)

    w2[:, :, :, 96:128, :] = jnp.zeros((4, 4, 2, 32, 384), BF16)
    a2s[:, 0:2] = jnp.zeros((3, 2, 4, 64, 128), BF16)

    def zero_p(i, carry):
        pbuf[i, 0:2] = jnp.zeros((2, 2, 64, 256), F32)
        return carry

    lax.fori_loop(0, 4, zero_p, 0)

    def act1(i, carry):
        v = lat[i].reshape(128, 384).astype(F32)
        ms = jnp.mean(v * v, axis=-1, keepdims=True)
        u = v * lax.rsqrt(ms + 1e-6) * gain1
        abuf[x, i, 1:3] = silu(u).astype(BF16).reshape(2, 64, 384)
        return carry

    lax.fori_loop(0, 2, act1, 0)

    many = jnp.where(x != y, 8, 0) + jnp.where(t > 0, 1, 0) + jnp.where(t < 63, 1, 0) + 17
    pl.semaphore_wait(barrier, many)

    def st1(d):
        jj = lax.rem(j + d, 8)
        return rc(s1.at[jj], r1.at[j], st1s.at[d], st1r.at[d], (x, g * 8 + jj))

    def st2(d):
        jj = lax.rem(j + d, 8)
        return rc(s2.at[jj], r2.at[j], st2s.at[d], st2r.at[d], (y, x * 16 + h * 8 + jj))

    def own2():
        return pltpu.make_async_copy(s2.at[j], r2.at[j], loc.at[1])

    for d in range(1, 8):
        st1(d).start()
    own1 = pltpu.make_async_copy(s1.at[j], r1.at[j], loc.at[0])
    own1.start()

    def xsend(d):
        return rc(
            abuf.at[x, :, 1:3], abuf.at[x, :, 1:3], xs.at[d], xr.at[d], (lax.rem(x + d, 4), t)
        )

    def up(src, d):
        return rc(abuf.at[src, :, 1], abuf.at[src, :, 3], ups.at[d], upr.at[d], (x, t - 1))

    def down(src, d):
        return rc(abuf.at[src, :, 2], abuf.at[src, :, 0], dns.at[d], dnr.at[d], (x, t + 1))

    def halo_send(d):
        src = lax.rem(x + 4 - d, 4)

        @pl.when(t > 0)
        def _():
            up(src, d).start()

        @pl.when(t < 63)
        def _():
            down(src, d).start()

    def xstep(d):
        src = lax.rem(x + 4 - d, 4)
        land = abuf.at[src, :, 1:3]
        rc(land, land, xs.at[d], xr.at[d], (x, t)).wait_recv()
        halo_send(d)

    def halo_wait():
        for d in range(4):
            src = lax.rem(x + 4 - d, 4)

            @pl.when(t > 0)
            def _():
                land = abuf.at[src, :, 0]
                rc(land, land, dns.at[d], dnr.at[d], (x, t)).wait_recv()

            @pl.when(t < 63)
            def _():
                land = abuf.at[src, :, 3]
                rc(land, land, ups.at[d], upr.at[d], (x, t)).wait_recv()

        @pl.when(t == 0)
        def _():
            abuf[:, :, 0] = jnp.zeros((4, 2, 64, 384), BF16)

        @pl.when(t == 63)
        def _():
            abuf[:, :, 3] = jnp.zeros((4, 2, 64, 384), BF16)

    for d in range(1, 4):
        xsend(d).start()
    for d in range(8):
        if d == 0:

            @pl.when(x != y)
            def _():
                st2(0).start()

            @pl.when(x == y)
            def _():
                own2().start()
        else:
            st2(d).start()
    halo_send(0)

    def own_slice(k):
        if k == 0:
            return w1.at[c, zi, :, y, h]
        return w2.at[y, zi, c, pl.ds(pl.multiple_of(48 * h, 16), 48), :]

    def blk(k, yy, zz, cc):
        if k == 0:
            return w1.at[cc, lax.rem(zz, 4), :, yy, lax.div(zz, 4)]
        return w2.at[yy, lax.rem(zz, 4), cc, pl.ds(pl.multiple_of(48 * lax.div(zz, 4), 16), 48), :]

    def half(k, zz, hf):
        if k == 0:
            return w1.at[0, lax.rem(zz, 4), :, 2 * hf:2 * hf + 2, lax.div(zz, 4)]
        return w2.at[2 * hf:2 * hf + 2, lax.rem(zz, 4), 0, pl.ds(pl.multiple_of(48 * lax.div(zz, 4), 16), 48), :]

    def zset(k, zz):
        if k == 0:
            return w1.at[0, lax.rem(zz, 4), :, :, lax.div(zz, 4)]
        return w2.at[:, lax.rem(zz, 4), 0, pl.ds(pl.multiple_of(48 * lax.div(zz, 4), 16), 48), :]

    def yset(k, yy):
        if k == 0:
            return w1.at[1, :, :, yy]
        return w2.at[yy, :, 1, 0:96, :]

    def yhalf(k, yy, a):
        if k == 0:
            return w1.at[1, 2 * a:2 * a + 2, :, yy]
        return w2.at[yy, 2 * a:2 * a + 2, 1, 0:96, :]

    sent_a, sent_b = [], []

    def go(group, make):
        make().start()
        group.append(make)

    def got(ref, rsem):
        rc(ref, ref, loc.at[2], rsem, (x, t)).wait_recv()

    def zz(s):
        return lax.rem(z + 8 + s, 8)

    def a_y(k, d):
        def make():
            ref = blk(k, y, z, 0)
            return rc(ref, ref, ysend.at[k, d - 1], yrecv.at[k, d - 1], dev(lax.rem(y + d, 4), z, 0))

        go(sent_a, make)

    WAY = {1: 0, -1: 1, 2: 2, -2: 3, 3: 4, -3: 5, 4: 6, -4: 7, 0: 8}

    def a_z(k, origin, total, hf=None):
        def make():
            ref = zset(k, zz(origin)) if hf is None else half(k, zz(origin), hf)
            i = WAY[total]
            return rc(ref, ref, rsend.at[k, i], rrecv.at[k, i], dev(y, zz(origin + total), c))

        go(sent_a, make)

    def a_sib(k, s):
        def make():
            ref = zset(k, zz(s))
            return rc(ref, ref, bsend.at[k, WAY[s] % 9], brecv.at[k, WAY[s] % 9], dev(y, z, 1))

        go(sent_a, make)

    def b_z(k, origin, total):
        def make():
            ref = blk(k, y, zz(origin), 1)
            i = WAY[total]
            return rc(ref, ref, rsend.at[k, i], rrecv.at[k, i], dev(y, zz(origin + total), c))

        go(sent_b, make)

    def b_y(k, s):
        for d in range(1, 4):
            def make(d=d):
                ref = blk(k, y, zz(s), 1)
                i = (d - 1) * 9 + WAY[s]
                return rc(ref, ref, ysend.at[k, i], yrecv.at[k, i], dev(lax.rem(y + d, 4), z, 1))

            go(sent_b, make)

    def b_sib(k, d):
        def make():
            ref = yset(k, lax.rem(y + d, 4))
            return rc(ref, ref, bsend.at[k, d], brecv.at[k, d], dev(y, z, 0))

        go(sent_b, make)

    def step(k, n):
        @pl.when(c == 0)
        def _():
            if n == 0:
                for d in range(1, 4):
                    a_y(k, d)
            if n == 1:
                for d in range(1, 4):
                    got(blk(k, lax.rem(y + 4 - d, 4), z, 0), yrecv.at[k, d - 1])
                for total in (2, -2, 1, -1):
                    a_z(k, 0, total)
                a_sib(k, 0)
            if n == 2:
                got(zset(k, zz(-2)), rrecv.at[k, WAY[2]])
                a_z(k, -2, 4, 0)
                a_z(k, -2, 3)
                got(zset(k, zz(2)), rrecv.at[k, WAY[-2]])
                a_z(k, 2, -4, 1)
                a_z(k, 2, -3)
                a_sib(k, -2)
                a_sib(k, 2)
            if n == 3:
                for s in (1, -1):
                    got(zset(k, zz(-s)), rrecv.at[k, WAY[s]])
                    a_sib(k, -s)
            if n == 4:
                for s in (3, -3):
                    got(zset(k, zz(-s)), rrecv.at[k, WAY[s]])
                    a_sib(k, -s)
                got(half(k, zz(4), 0), rrecv.at[k, WAY[4]])
                got(half(k, zz(4), 1), rrecv.at[k, WAY[-4]])
                a_sib(k, 4)
            if n == 5:
                for d in range(4):
                    got(yset(k, lax.rem(y + d, 4)), brecv.at[k, d])

        @pl.when(c == 1)
        def _():
            far = 4 if k == 0 else -4
            if n == 0:
                for total in (2, -2, 1, -1):
                    b_z(k, 0, total)
                b_y(k, 0)
            if n == 1:
                for s in (2, -2):
                    got(blk(k, y, zz(-s), 1), rrecv.at[k, WAY[s]])
                    if far * s > 0:
                        b_z(k, -s, far)
                    b_z(k, -s, 3 if s > 0 else -3)
                b_y(k, -2)
                b_y(k, 2)
            if n == 2:
                for s in (1, -1):
                    got(blk(k, y, zz(-s), 1), rrecv.at[k, WAY[s]])
                    b_y(k, -s)
            if n == 3:
                for s in (3, -3):
                    got(blk(k, y, zz(-s), 1), rrecv.at[k, WAY[s]])
                    b_y(k, -s)
                got(blk(k, y, zz(4), 1), rrecv.at[k, WAY[far]])
                b_y(k, 4)
                b_sib(k, 0)
            if n == 4:
                for d in range(1, 4):
                    for s in (0, 2, -2, 1, -1, 3, -3, 4):
                        got(blk(k, lax.rem(y + 4 - d, 4), zz(s), 1), yrecv.at[k, (d - 1) * 9 + WAY[s]])
                    b_sib(k, 4 - d)
            if n == 5:
                for s in (0, 2, -2, 1, -1, 3, -3, 4):
                    got(zset(k, zz(s)), brecv.at[k, WAY[s]])

    own1.wait()
    for d in range(1, 8):
        got(r1.at[lax.rem(j + 8 - d, 8)], st1r.at[d])
    for dy in range(3):
        for m in range(8):
            two = r1[m, 16 * (dy // 2):16 * (dy // 2) + 16].astype(F32)
            stack[m * 6:m * 6 + 6, 0:128] = two[(dy % 2) * 8:(dy % 2) * 8 + 6]
        w1[c, zi, dy, y, h] = stack[:, 0:128].astype(BF16)
    step(0, 0)
    @pl.when(x != y)
    def _():
        got(r2.at[j], st2r.at[0])

    @pl.when(x == y)
    def _():
        own2().wait()

    for d in range(1, 8):
        got(r2.at[lax.rem(j + 8 - d, 8)], st2r.at[d])
    for m in range(8):
        stack[m * 6:m * 6 + 6] = r2[m].astype(F32)[0:6]
    w2[y, zi, c, pl.ds(pl.multiple_of(48 * h, 16), 48), :] = stack[...].astype(BF16)
    step(1, 0)
    step(0, 1)
    xstep(1)
    xstep(3)
    step(0, 2)
    xstep(2)
    step(0, 3)
    step(1, 1)
    step(0, 4)
    step(1, 2)
    step(1, 3)
    step(0, 5)
    halo_wait()

    def conv1(fp):
        rows = []
        for yy in range(2):
            rows.append(jnp.concatenate(
                [abuf[fp, :, yy + dy].reshape(128, 384) for dy in range(3)], axis=1))
        lhs = jnp.concatenate(rows, axis=0)

        def tile(n, carry):
            rhs = jnp.concatenate(
                [w1[0, n].reshape(1152, 128), w1[1, n].reshape(1152, 128)], axis=1)
            res = jnp.dot(lhs, rhs, preferred_element_type=F32)
            for yy in range(2):
                pbuf[n, 2 + 2 * fp:4 + 2 * fp, yy] = res[yy * 128:yy * 128 + 128].reshape(2, 64, 256)
            return carry

        lax.fori_loop(0, 4, tile, 0)

    for fp in range(4):
        conv1(fp)
        if fp == 1:
            step(1, 4)

    lane = lax.broadcasted_iota(jnp.int32, (64, 128), 1)
    row = lax.broadcasted_iota(jnp.int32, (64, 128), 0)

    def shift_down(v):
        return jnp.where(row > 0, pltpu.roll(v, 1, 0), 0.0)

    def shift_up(v):
        return jnp.where(row < 63, pltpu.roll(v, 63, 0), 0.0)

    def combine(f, carry):
        for yy in range(2):
            def p(dt, n):
                return pbuf[n // 2, f + dt, yy, :, (n % 2) * 128:(n % 2) * 128 + 128]

            m1 = p(0, 0) + p(1, 3) + p(2, 6)
            a_lo = p(0, 0) + p(1, 3)
            mid = p(0, 1) + p(1, 4)
            b_hi = p(0, 2) + p(1, 5)
            m0 = pltpu.roll(jnp.where(lane >= 96, a_lo, mid), 32, 1) + pltpu.roll(p(2, 2), 96, 1)
            m2 = pltpu.roll(jnp.where(lane >= 64, mid, b_hi), 64, 1) + pltpu.roll(p(2, 5), 96, 1)
            hid = m1 + shift_down(m0) + shift_up(m2) + bias1
            hbuf[f, yy] = jnp.where(lane < 96, hid, 0.0)
        return carry

    lax.fori_loop(0, 8, combine, 0)

    hv = hbuf[...].reshape(1024, 128)
    ssbuf[0] = lax.dot_general(
        jnp.ones((8, 128), F32), hv * hv, (((1,), (1,)), ((), ())),
        precision=lax.Precision.HIGHEST, preferred_element_type=F32,
    )

    def ss_send(d):
        return rc(ssbuf.at[0], ssbuf.at[d], sss.at[d], ssr.at[d], (lax.rem(x + d, 4), t))

    for d in range(1, 4):
        ss_send(d).start()
    for d in range(1, 4):
        got(ssbuf.at[d], ssr.at[d])
    total = ssbuf[0] + ssbuf[1] + ssbuf[2] + ssbuf[3]
    ms = lax.dot_general(
        total, jnp.full((8, 128), 0.125, F32), (((0,), (0,)), ((), ())),
        precision=lax.Precision.HIGHEST, preferred_element_type=F32,
    ) * (1.0 / 384.0)
    hv = hbuf[...].reshape(1024, 128)
    hbuf[...] = (hv * lax.rsqrt(ms + 1e-6) * gain2).reshape(8, 2, 64, 128)

    def spread(f, where, v):
        a2s[0, f + 2, where] = shift_down(v).astype(BF16)
        a2s[1, f + 2, where] = v.astype(BF16)
        a2s[2, f + 2, where] = shift_up(v).astype(BF16)

    def act2(f, carry):
        for yy in range(2):
            spread(f, 1 + yy, silu(hbuf[f, yy]))
        return carry

    lax.fori_loop(0, 8, act2, 0)

    def h2up():
        return rc(a2s.at[1, 2:10, 1], a2h.at[1], h2s.at[0], h2r.at[0], (x, t - 1))

    def h2down():
        return rc(a2s.at[1, 2:10, 2], a2h.at[0], h2s.at[1], h2r.at[1], (x, t + 1))

    @pl.when(t > 0)
    def _():
        h2up().start()

    @pl.when(t < 63)
    def _():
        h2down().start()

    step(1, 5)

    @pl.when(t > 0)
    def _():
        got(a2h.at[0], h2r.at[1])

    @pl.when(t == 0)
    def _():
        a2h[0] = jnp.zeros((8, 64, 128), BF16)

    @pl.when(t < 63)
    def _():
        got(a2h.at[1], h2r.at[0])

    @pl.when(t == 63)
    def _():
        a2h[1] = jnp.zeros((8, 64, 128), BF16)

    def halo2(f, carry):
        spread(f, 0, a2h[0, f].astype(F32))
        spread(f, 3, a2h[1, f].astype(F32))
        return carry

    lax.fori_loop(0, 8, halo2, 0)

    def conv2(q):
        acc = None
        for dt in range(3):
            lhs, rhs = [], []
            for dy in range(3):
                for dx in range(3):
                    tap = dt * 9 + dy * 3 + dx
                    lhs.append(a2s[dx, pl.ds(2 * q + dt, 2), dy:dy + 2].reshape(256, 128))
                    rhs.append(w2[tap // 8, (tap % 8) // 2, tap % 2])
            part = jnp.dot(
                jnp.concatenate(lhs, axis=1), jnp.concatenate(rhs, axis=0),
                preferred_element_type=F32,
            )
            acc = part if acc is None else acc + part
        return acc

    def out_send(d):
        return rc(sendb.at[d - 1], recvb.at[d - 1], fs.at[d], fr.at[d], (lax.rem(x + d, 4), t))

    for d in (2, 1, 3):
        sendb[d - 1] = conv2(lax.rem(x + d, 4)).astype(BF16).reshape(2, 2, 64, 384)
        out_send(d).start()
    mine = conv2(x) + bias2 + lat[...].reshape(256, 384).astype(F32)
    for d in (2, 1, 3):
        got(recvb.at[d - 1], fr.at[d])
        mine = mine + recvb[d - 1].reshape(256, 384).astype(F32)
    out[...] = mine.astype(BF16).reshape(2, 2, 64, 384)

    for d in range(1, 8):
        st1(d).wait_send()
        st2(d).wait_send()

    @pl.when(x != y)
    def _():
        st2(0).wait_send()

    for d in range(1, 4):
        xsend(d).wait_send()
        ss_send(d).wait_send()
        out_send(d).wait_send()

    @pl.when(t > 0)
    def _():
        for d in range(4):
            up(lax.rem(x + 4 - d, 4), d).wait_send()
        h2up().wait_send()

    @pl.when(t < 63)
    def _():
        for d in range(4):
            down(lax.rem(x + 4 - d, 4), d).wait_send()
        h2down().wait_send()

    @pl.when(c == 0)
    def _():
        for make in sent_a:
            make().wait_send()

    @pl.when(c == 1)
    def _():
        for make in sent_b:
            make().wait_send()


def per_device(latents, gain_first, conv_first, bias_first, gain_second, conv_second, bias_second):
    vm = pl.BlockSpec(memory_space=pltpu.VMEM)
    dma = pltpu.SemaphoreType.DMA
    return pl.pallas_call(
        kernel,
        out_shape=jax.ShapeDtypeStruct((2, 2, 64, 384), BF16),
        in_specs=[pl.BlockSpec(memory_space=pl.ANY)] * 7,
        out_specs=vm,
        scratch_shapes=[
            pltpu.VMEM((2, 2, 64, 384), BF16),
            pltpu.VMEM((4, 384), F32),
            pltpu.VMEM((27, 6, 384), BF16),
            pltpu.VMEM((27, 6, 384), BF16),
            pltpu.VMEM((8, 32, 128), BF16),
            pltpu.VMEM((8, 16, 384), BF16),
            pltpu.VMEM((48, 384), F32),
            pltpu.VMEM((8, 32, 128), BF16),
            pltpu.VMEM((8, 16, 384), BF16),
            pltpu.VMEM((2, 4, 3, 4, 2, 48, 128), BF16),
            pltpu.VMEM((4, 4, 2, 128, 384), BF16),
            pltpu.VMEM((4, 2, 4, 64, 384), BF16),
            pltpu.VMEM((4, 10, 2, 64, 256), F32),
            pltpu.VMEM((8, 2, 64, 128), F32),
            pltpu.VMEM((4, 8, 1024), F32),
            pltpu.VMEM((3, 10, 4, 64, 128), BF16),
            pltpu.VMEM((2, 8, 64, 128), BF16),
            pltpu.VMEM((3, 2, 2, 64, 384), BF16),
            pltpu.VMEM((3, 2, 2, 64, 384), BF16),
            dma((7,)), dma((8,)), dma((8,)), dma((8,)), dma((8,)), dma((3,)),
            dma((2, 27)), dma((2, 27)), dma((2, 9)), dma((2, 9)), dma((2, 9)), dma((2, 9)),
            dma((4,)), dma((4,)), dma((4,)), dma((4,)), dma((4,)), dma((4,)),
            dma((4,)), dma((4,)), dma((2,)), dma((2,)), dma((4,)), dma((4,)),
        ],
        compiler_params=pltpu.CompilerParams(
            collective_id=0, has_side_effects=True, vmem_limit_bytes=48 * 1024 * 1024
        ),
        cost_estimate=pl.CostEstimate(flops=4_000_000_000, bytes_accessed=8_000_000, transcendentals=400_000),
    )(
        latents, gain_first, bias_first, gain_second, bias_second,
        conv_first.reshape(27, 6, 384), conv_second.reshape(27, 6, 384),
    )


def solution(mesh):
    in_specs = (
        P("span", "tile", None, None),
        P(),
        P(None, None, None, "tile", None),
        P(),
        P(),
        P(None, None, None, "tile", None),
        P(),
    )
    out_specs = P("span", "tile", None, None)
    return jax.shard_map(
        per_device, mesh=mesh, in_specs=in_specs, out_specs=out_specs, check_vma=False
    )
```

```python
import jax
import jax.numpy as jnp
from jax import lax
from jax.experimental import pallas as pl
from jax.experimental.pallas import tpu as pltpu
from jax.sharding import PartitionSpec as P

MESH = pl.DeviceIdType.MESH
F32 = jnp.float32
BF16 = jnp.bfloat16

SLOTS = ((0, 1), (0, 0), (0, 2), (2, 0), (1, 1), (1, 0), (1, 2), (2, 2), (2, 1))


def silu(u):
    return u / (1.0 + jnp.exp(-u))


def kernel(
    lat_hbm, gain1_hbm, bias1_hbm, gain2_hbm, bias2_hbm, k1_hbm, k2_hbm, out,
    lat, vec, k1, k2, s1, s2, stack,
    r1, r2, w1, w2, abuf, pbuf, hbuf, ssbuf, a2s, a2h, sendb, recvb,
    ins, st1s, st1r, st2s, st2r, loc,
    ysend, yrecv, rsend, rrecv, bsend, brecv,
    xs, xr, ups, upr, dns, dnr, sss, ssr, h2s, h2r, fs, fr,
):
    x = lax.axis_index("span")
    t = lax.axis_index("tile")
    c = lax.rem(t, 2)
    z = lax.rem(lax.div(t, 2), 8)
    y = lax.div(t, 16)
    zi = lax.rem(z, 4)
    h = lax.div(z, 4)
    j = lax.rem(t, 8)
    g = lax.div(t, 8)

    def dev(yy, zz, cc):
        return (x, yy * 16 + zz * 2 + cc)

    def rc(src, dst, ssem, rsem, device):
        return pltpu.make_async_remote_copy(
            src_ref=src, dst_ref=dst, send_sem=ssem, recv_sem=rsem,
            device_id=device, device_id_type=MESH,
        )

    loads = [
        pltpu.make_async_copy(k1_hbm, k1, ins.at[0]),
        pltpu.make_async_copy(lat_hbm, lat, ins.at[1]),
        pltpu.make_async_copy(k2_hbm, k2, ins.at[2]),
        pltpu.make_async_copy(gain1_hbm, vec.at[0], ins.at[3]),
        pltpu.make_async_copy(bias1_hbm, vec.at[1], ins.at[4]),
        pltpu.make_async_copy(gain2_hbm, vec.at[2], ins.at[5]),
        pltpu.make_async_copy(bias2_hbm, vec.at[3], ins.at[6]),
    ]
    for load in loads:
        load.start()

    barrier = pltpu.get_barrier_semaphore()

    def hail(device):
        pl.semaphore_signal(barrier, inc=1, device_id=device, device_id_type=MESH)

    for d in range(1, 8):
        hail((x, g * 8 + lax.rem(j + d, 8)))

    @pl.when(x != y)
    def _():
        for d in range(8):
            hail((y, x * 16 + h * 8 + lax.rem(j + d, 8)))

    for d in range(1, 4):
        hail((lax.rem(x + d, 4), t))
    for d in range(1, 4):
        hail(dev(lax.rem(y + d, 4), z, c))
    for d in (1, 2, 6, 7):
        hail(dev(y, lax.rem(z + d, 8), c))

    @pl.when(t > 0)
    def _():
        hail((x, t - 1))

    @pl.when(t < 63)
    def _():
        hail((x, t + 1))

    lane8 = lax.broadcasted_iota(jnp.int32, (8, 128), 1)
    turn = lax.rem(384 - 96 * x, 384)

    def mine96(v):
        return pltpu.roll(v, turn, 1)[:, 0:128]

    loads[0].wait()
    pad2 = jnp.zeros((2, 384), F32)
    tiles = []
    for dy in range(3):
        got_slots = []
        for dt, dx in SLOTS:
            got_slots.append(mine96(jnp.concatenate([k1[dt * 9 + dy * 3 + dx].astype(F32), pad2], axis=0)))

        def at(n, by):
            return pltpu.roll(got_slots[n], by, 1) if by else got_slots[n]

        row = [
            jnp.where(lane8 < 96, at(0, 0), at(1, 96)),
            jnp.where(lane8 < 64, at(1, 96), at(2, 64)),
            jnp.where(lane8 < 32, at(2, 64), at(3, 32)),
            jnp.where(lane8 < 96, at(4, 0), at(5, 96)),
            jnp.where(lane8 < 64, at(5, 96), at(6, 64)),
            jnp.where(lane8 < 32, at(6, 64), at(7, 32)),
            jnp.where(lane8 < 96, at(8, 0), 0.0),
            jnp.zeros((8, 128), F32),
        ]
        tiles.append(row)
    for n in range(8):
        s1[n, 0:16] = jnp.concatenate([tiles[0][n], tiles[1][n]], axis=0).astype(BF16)
        s1[n, 16:32] = jnp.concatenate([tiles[2][n], jnp.zeros((8, 128), F32)], axis=0).astype(BF16)
    loads[2].wait()
    for n in range(8):
        tap = jnp.minimum(8 * x + n, 26)
        s2[n] = jnp.concatenate([k2[tap].astype(F32), jnp.zeros((10, 384), F32)], axis=0).astype(BF16)
    for load in loads[3:]:
        load.wait()
    loads[1].wait()
    gain1 = vec[0:1]
    bias2 = vec[3:4]
    bias1 = jnp.where(lane8[0:1] < 96, mine96(jnp.broadcast_to(vec[1:2], (8, 384)))[0:1], 0.0)
    gain2 = jnp.where(lane8[0:1] < 96, mine96(jnp.broadcast_to(vec[2:3], (8, 384)))[0:1], 0.0)

    w2[:, :, :, 96:128, :] = jnp.zeros((4, 4, 2, 32, 384), BF16)
    a2s[:, 0:2] = jnp.zeros((3, 2, 4, 64, 128), BF16)

    def zero_p(i, carry):
        pbuf[i, 0:2] = jnp.zeros((2, 2, 64, 256), F32)
        return carry

    lax.fori_loop(0, 4, zero_p, 0)

    def act1(i, carry):
        v = lat[i].reshape(128, 384).astype(F32)
        ms = jnp.mean(v * v, axis=-1, keepdims=True)
        u = v * lax.rsqrt(ms + 1e-6) * gain1
        abuf[x, i, 1:3] = silu(u).astype(BF16).reshape(2, 64, 384)
        return carry

    lax.fori_loop(0, 2, act1, 0)

    many = jnp.where(x != y, 8, 0) + jnp.where(t > 0, 1, 0) + jnp.where(t < 63, 1, 0) + 17
    pl.semaphore_wait(barrier, many)

    def st1(d):
        jj = lax.rem(j + d, 8)
        return rc(s1.at[jj], r1.at[j], st1s.at[d], st1r.at[d], (x, g * 8 + jj))

    def st2(d):
        jj = lax.rem(j + d, 8)
        return rc(s2.at[jj], r2.at[j], st2s.at[d], st2r.at[d], (y, x * 16 + h * 8 + jj))

    def own2():
        return pltpu.make_async_copy(s2.at[j], r2.at[j], loc.at[1])

    for d in range(1, 8):
        st1(d).start()
    own1 = pltpu.make_async_copy(s1.at[j], r1.at[j], loc.at[0])
    own1.start()

    def xsend(d):
        return rc(
            abuf.at[x, :, 1:3], abuf.at[x, :, 1:3], xs.at[d], xr.at[d], (lax.rem(x + d, 4), t)
        )

    def up(src, d):
        return rc(abuf.at[src, :, 1], abuf.at[src, :, 3], ups.at[d], upr.at[d], (x, t - 1))

    def down(src, d):
        return rc(abuf.at[src, :, 2], abuf.at[src, :, 0], dns.at[d], dnr.at[d], (x, t + 1))

    def halo_send(d):
        src = lax.rem(x + 4 - d, 4)

        @pl.when(t > 0)
        def _():
            up(src, d).start()

        @pl.when(t < 63)
        def _():
            down(src, d).start()

    def xstep(d):
        src = lax.rem(x + 4 - d, 4)
        land = abuf.at[src, :, 1:3]
        rc(land, land, xs.at[d], xr.at[d], (x, t)).wait_recv()
        halo_send(d)

    def halo_wait():
        for d in range(4):
            src = lax.rem(x + 4 - d, 4)

            @pl.when(t > 0)
            def _():
                land = abuf.at[src, :, 0]
                rc(land, land, dns.at[d], dnr.at[d], (x, t)).wait_recv()

            @pl.when(t < 63)
            def _():
                land = abuf.at[src, :, 3]
                rc(land, land, ups.at[d], upr.at[d], (x, t)).wait_recv()

        @pl.when(t == 0)
        def _():
            abuf[:, :, 0] = jnp.zeros((4, 2, 64, 384), BF16)

        @pl.when(t == 63)
        def _():
            abuf[:, :, 3] = jnp.zeros((4, 2, 64, 384), BF16)

    for d in range(1, 4):
        xsend(d).start()
    for d in range(8):
        if d == 0:

            @pl.when(x != y)
            def _():
                st2(0).start()

            @pl.when(x == y)
            def _():
                own2().start()
        else:
            st2(d).start()
    halo_send(0)

    def own_slice(k):
        if k == 0:
            return w1.at[c, zi, :, y, h]
        return w2.at[y, zi, c, pl.ds(pl.multiple_of(48 * h, 16), 48), :]

    def blk(k, yy, zz, cc):
        if k == 0:
            return w1.at[cc, lax.rem(zz, 4), :, yy, lax.div(zz, 4)]
        return w2.at[yy, lax.rem(zz, 4), cc, pl.ds(pl.multiple_of(48 * lax.div(zz, 4), 16), 48), :]

    def half(k, zz, hf):
        if k == 0:
            return w1.at[0, lax.rem(zz, 4), :, 2 * hf:2 * hf + 2, lax.div(zz, 4)]
        return w2.at[2 * hf:2 * hf + 2, lax.rem(zz, 4), 0, pl.ds(pl.multiple_of(48 * lax.div(zz, 4), 16), 48), :]

    def zset(k, zz):
        if k == 0:
            return w1.at[0, lax.rem(zz, 4), :, :, lax.div(zz, 4)]
        return w2.at[:, lax.rem(zz, 4), 0, pl.ds(pl.multiple_of(48 * lax.div(zz, 4), 16), 48), :]

    def yset(k, yy):
        if k == 0:
            return w1.at[1, :, :, yy]
        return w2.at[yy, :, 1, 0:96, :]

    def yhalf(k, yy, a):
        if k == 0:
            return w1.at[1, 2 * a:2 * a + 2, :, yy]
        return w2.at[yy, 2 * a:2 * a + 2, 1, 0:96, :]

    sent_a, sent_b = [], []

    def go(group, make):
        make().start()
        group.append(make)

    def got(ref, rsem):
        rc(ref, ref, loc.at[2], rsem, (x, t)).wait_recv()

    def zz(s):
        return lax.rem(z + 8 + s, 8)

    def a_y(k, d):
        def make():
            ref = blk(k, y, z, 0)
            return rc(ref, ref, ysend.at[k, d - 1], yrecv.at[k, d - 1], dev(lax.rem(y + d, 4), z, 0))

        go(sent_a, make)

    WAY = {1: 0, -1: 1, 2: 2, -2: 3, 3: 4, -3: 5, 4: 6, -4: 7, 0: 8}

    def a_z(k, origin, total, hf=None):
        def make():
            ref = zset(k, zz(origin)) if hf is None else half(k, zz(origin), hf)
            i = WAY[total]
            return rc(ref, ref, rsend.at[k, i], rrecv.at[k, i], dev(y, zz(origin + total), c))

        go(sent_a, make)

    def a_sib(k, s):
        def make():
            ref = zset(k, zz(s))
            return rc(ref, ref, bsend.at[k, WAY[s] % 9], brecv.at[k, WAY[s] % 9], dev(y, z, 1))

        go(sent_a, make)

    def b_z(k, origin, total):
        def make():
            ref = blk(k, y, zz(origin), 1)
            i = WAY[total]
            return rc(ref, ref, rsend.at[k, i], rrecv.at[k, i], dev(y, zz(origin + total), c))

        go(sent_b, make)

    def b_y(k, s):
        for d in range(1, 4):
            def make(d=d):
                ref = blk(k, y, zz(s), 1)
                i = (d - 1) * 9 + WAY[s]
                return rc(ref, ref, ysend.at[k, i], yrecv.at[k, i], dev(lax.rem(y + d, 4), z, 1))

            go(sent_b, make)

    def b_sib(k, d):
        def make():
            ref = yset(k, lax.rem(y + d, 4))
            return rc(ref, ref, bsend.at[k, d], brecv.at[k, d], dev(y, z, 0))

        go(sent_b, make)

    def wset(yy, cc):
        return w2.at[yy, :, cc, 0:96, :]

    def z2_send(origin, total):
        ref = blk(1, y, zz(origin), c)
        i = WAY[total]
        return rc(ref, ref, rsend.at[1, i], rrecv.at[1, i], dev(y, zz(origin + total), c))

    def z2_got(total):
        got(blk(1, y, zz(-total), c), rrecv.at[1, WAY[total]])

    def y2_send(d):
        ref = wset(y, c)
        return rc(ref, ref, ysend.at[1, d], yrecv.at[1, d], dev(lax.rem(y + d, 4), z, c))

    def sib2_send(d):
        ref = wset(lax.rem(y + d, 4), c)
        return rc(ref, ref, bsend.at[1, d], brecv.at[1, d], dev(y, z, 1 - c))

    Z2 = ((0, 2), (0, -2), (0, 1), (0, -1), (-2, 4), (-2, 3), (2, -3))

    def step2(n):
        if n == 0:
            for origin, total in Z2[:4]:
                z2_send(origin, total).start()
        if n == 1:
            z2_got(2)
            z2_send(-2, 4).start()
            z2_send(-2, 3).start()
            z2_got(-2)
            z2_send(2, -3).start()
        if n == 2:
            for total in (1, -1, 3, -3, 4):
                z2_got(total)
            for d in (2, 1, 3):
                y2_send(d).start()
            sib2_send(0).start()
        if n == 3:
            for d in (1, 3, 2):
                got(wset(lax.rem(y + 4 - d, 4), c), yrecv.at[1, d])
                sib2_send(4 - d).start()
        if n == 4:
            for d in range(4):
                got(wset(lax.rem(y + d, 4), 1 - c), brecv.at[1, d])

    def step2_sent():
        for origin, total in Z2:
            z2_send(origin, total).wait_send()
        for d in range(1, 4):
            y2_send(d).wait_send()
        for d in range(4):
            sib2_send(d).wait_send()

    def step(k, n):
        @pl.when(c == 0)
        def _():
            if n == 0:
                for d in range(1, 4):
                    a_y(k, d)
            if n == 1:
                for d in range(1, 4):
                    got(blk(k, lax.rem(y + 4 - d, 4), z, 0), yrecv.at[k, d - 1])
                for total in (2, -2, 1, -1):
                    a_z(k, 0, total)
                a_sib(k, 0)
            if n == 2:
                got(zset(k, zz(-2)), rrecv.at[k, WAY[2]])
                a_z(k, -2, 4, 0)
                a_z(k, -2, 3)
                got(zset(k, zz(2)), rrecv.at[k, WAY[-2]])
                a_z(k, 2, -4, 1)
                a_z(k, 2, -3)
                a_sib(k, -2)
                a_sib(k, 2)
            if n == 3:
                for s in (1, -1):
                    got(zset(k, zz(-s)), rrecv.at[k, WAY[s]])
                    a_sib(k, -s)
            if n == 4:
                for s in (3, -3):
                    got(zset(k, zz(-s)), rrecv.at[k, WAY[s]])
                    a_sib(k, -s)
                got(half(k, zz(4), 0), rrecv.at[k, WAY[4]])
                got(half(k, zz(4), 1), rrecv.at[k, WAY[-4]])
                a_sib(k, 4)
            if n == 5:
                for d in range(4):
                    got(yset(k, lax.rem(y + d, 4)), brecv.at[k, d])

        @pl.when(c == 1)
        def _():
            far = 4 if k == 0 else -4
            if n == 0:
                for total in (2, -2, 1, -1):
                    b_z(k, 0, total)
                b_y(k, 0)
            if n == 1:
                for s in (2, -2):
                    got(blk(k, y, zz(-s), 1), rrecv.at[k, WAY[s]])
                    if far * s > 0:
                        b_z(k, -s, far)
                    b_z(k, -s, 3 if s > 0 else -3)
                b_y(k, -2)
                b_y(k, 2)
            if n == 2:
                for s in (1, -1):
                    got(blk(k, y, zz(-s), 1), rrecv.at[k, WAY[s]])
                    b_y(k, -s)
            if n == 3:
                for s in (3, -3):
                    got(blk(k, y, zz(-s), 1), rrecv.at[k, WAY[s]])
                    b_y(k, -s)
                got(blk(k, y, zz(4), 1), rrecv.at[k, WAY[far]])
                b_y(k, 4)
                b_sib(k, 0)
            if n == 4:
                for d in range(1, 4):
                    for s in (0, 2, -2, 1, -1, 3, -3, 4):
                        got(blk(k, lax.rem(y + 4 - d, 4), zz(s), 1), yrecv.at[k, (d - 1) * 9 + WAY[s]])
                    b_sib(k, 4 - d)
            if n == 5:
                for s in (0, 2, -2, 1, -1, 3, -3, 4):
                    got(zset(k, zz(s)), brecv.at[k, WAY[s]])

    own1.wait()
    for d in range(1, 8):
        got(r1.at[lax.rem(j + 8 - d, 8)], st1r.at[d])
    for dy in range(3):
        for m in range(8):
            two = r1[m, 16 * (dy // 2):16 * (dy // 2) + 16].astype(F32)
            stack[m * 6:m * 6 + 6, 0:128] = two[(dy % 2) * 8:(dy % 2) * 8 + 6]
        w1[c, zi, dy, y, h] = stack[:, 0:128].astype(BF16)
    step(0, 0)
    step(0, 1)

    @pl.when(x != y)
    def _():
        got(r2.at[j], st2r.at[0])

    @pl.when(x == y)
    def _():
        own2().wait()

    for d in range(1, 8):
        got(r2.at[lax.rem(j + 8 - d, 8)], st2r.at[d])
    for m in range(8):
        stack[m * 6:m * 6 + 6] = r2[m].astype(F32)[0:6]
    w2[y, zi, c, pl.ds(pl.multiple_of(48 * h, 16), 48), :] = stack[...].astype(BF16)
    step2(0)
    step(0, 2)
    xstep(1)
    xstep(3)
    step(0, 3)
    xstep(2)
    step2(1)
    step2(2)
    step(0, 4)
    halo_wait()
    step(0, 5)

    def conv1(fp):
        rows = []
        for yy in range(2):
            rows.append(jnp.concatenate(
                [abuf[fp, :, yy + dy].reshape(128, 384) for dy in range(3)], axis=1))
        lhs = jnp.concatenate(rows, axis=0)

        def tile(n, carry):
            rhs = jnp.concatenate(
                [w1[0, n].reshape(1152, 128), w1[1, n].reshape(1152, 128)], axis=1)
            res = jnp.dot(lhs, rhs, preferred_element_type=F32)
            for yy in range(2):
                pbuf[n, 2 + 2 * fp:4 + 2 * fp, yy] = res[yy * 128:yy * 128 + 128].reshape(2, 64, 256)
            return carry

        lax.fori_loop(0, 4, tile, 0)

    for fp in range(4):
        conv1(fp)

    lane = lax.broadcasted_iota(jnp.int32, (64, 128), 1)
    row = lax.broadcasted_iota(jnp.int32, (64, 128), 0)

    def shift_down(v):
        return jnp.where(row > 0, pltpu.roll(v, 1, 0), 0.0)

    def shift_up(v):
        return jnp.where(row < 63, pltpu.roll(v, 63, 0), 0.0)

    def combine(f, carry):
        for yy in range(2):
            def p(dt, n):
                return pbuf[n // 2, f + dt, yy, :, (n % 2) * 128:(n % 2) * 128 + 128]

            m1 = p(0, 0) + p(1, 3) + p(2, 6)
            a_lo = p(0, 0) + p(1, 3)
            mid = p(0, 1) + p(1, 4)
            b_hi = p(0, 2) + p(1, 5)
            m0 = pltpu.roll(jnp.where(lane >= 96, a_lo, mid), 32, 1) + pltpu.roll(p(2, 2), 96, 1)
            m2 = pltpu.roll(jnp.where(lane >= 64, mid, b_hi), 64, 1) + pltpu.roll(p(2, 5), 96, 1)
            hid = m1 + shift_down(m0) + shift_up(m2) + bias1
            hbuf[f, yy] = jnp.where(lane < 96, hid, 0.0)
        return carry

    lax.fori_loop(0, 8, combine, 0)

    hv = hbuf[...].reshape(1024, 128)
    ssbuf[0] = lax.dot_general(
        jnp.ones((8, 128), F32), hv * hv, (((1,), (1,)), ((), ())),
        precision=lax.Precision.HIGHEST, preferred_element_type=F32,
    )

    def ss_send(d):
        return rc(ssbuf.at[0], ssbuf.at[d], sss.at[d], ssr.at[d], (lax.rem(x + d, 4), t))

    for d in range(1, 4):
        ss_send(d).start()
    for d in range(1, 4):
        got(ssbuf.at[d], ssr.at[d])
    total = ssbuf[0] + ssbuf[1] + ssbuf[2] + ssbuf[3]
    ms = lax.dot_general(
        total, jnp.full((8, 128), 0.125, F32), (((0,), (0,)), ((), ())),
        precision=lax.Precision.HIGHEST, preferred_element_type=F32,
    ) * (1.0 / 384.0)
    hv = hbuf[...].reshape(1024, 128)
    hbuf[...] = (hv * lax.rsqrt(ms + 1e-6) * gain2).reshape(8, 2, 64, 128)

    def spread(f, where, v):
        a2s[0, f + 2, where] = shift_down(v).astype(BF16)
        a2s[1, f + 2, where] = v.astype(BF16)
        a2s[2, f + 2, where] = shift_up(v).astype(BF16)

    def act2(f, carry):
        for yy in range(2):
            spread(f, 1 + yy, silu(hbuf[f, yy]))
        return carry

    lax.fori_loop(0, 8, act2, 0)

    def h2up():
        return rc(a2s.at[1, 2:10, 1], a2h.at[1], h2s.at[0], h2r.at[0], (x, t - 1))

    def h2down():
        return rc(a2s.at[1, 2:10, 2], a2h.at[0], h2s.at[1], h2r.at[1], (x, t + 1))

    @pl.when(t > 0)
    def _():
        h2up().start()

    @pl.when(t < 63)
    def _():
        h2down().start()

    step2(3)
    step2(4)

    @pl.when(t > 0)
    def _():
        got(a2h.at[0], h2r.at[1])

    @pl.when(t == 0)
    def _():
        a2h[0] = jnp.zeros((8, 64, 128), BF16)

    @pl.when(t < 63)
    def _():
        got(a2h.at[1], h2r.at[0])

    @pl.when(t == 63)
    def _():
        a2h[1] = jnp.zeros((8, 64, 128), BF16)

    def halo2(f, carry):
        spread(f, 0, a2h[0, f].astype(F32))
        spread(f, 3, a2h[1, f].astype(F32))
        return carry

    lax.fori_loop(0, 8, halo2, 0)

    def conv2(q):
        acc = None
        for dt in range(3):
            lhs, rhs = [], []
            for dy in range(3):
                for dx in range(3):
                    tap = dt * 9 + dy * 3 + dx
                    lhs.append(a2s[dx, pl.ds(2 * q + dt, 2), dy:dy + 2].reshape(256, 128))
                    rhs.append(w2[tap // 8, (tap % 8) // 2, tap % 2])
            part = jnp.dot(
                jnp.concatenate(lhs, axis=1), jnp.concatenate(rhs, axis=0),
                preferred_element_type=F32,
            )
            acc = part if acc is None else acc + part
        return acc

    def out_send(d):
        return rc(sendb.at[d - 1], recvb.at[d - 1], fs.at[d], fr.at[d], (lax.rem(x + d, 4), t))

    for d in (2, 1, 3):
        sendb[d - 1] = conv2(lax.rem(x + d, 4)).astype(BF16).reshape(2, 2, 64, 384)
        out_send(d).start()
    mine = conv2(x) + bias2 + lat[...].reshape(256, 384).astype(F32)
    for d in (2, 1, 3):
        got(recvb.at[d - 1], fr.at[d])
        mine = mine + recvb[d - 1].reshape(256, 384).astype(F32)
    out[...] = mine.astype(BF16).reshape(2, 2, 64, 384)

    for d in range(1, 8):
        st1(d).wait_send()
        st2(d).wait_send()

    @pl.when(x != y)
    def _():
        st2(0).wait_send()

    for d in range(1, 4):
        xsend(d).wait_send()
        ss_send(d).wait_send()
        out_send(d).wait_send()

    @pl.when(t > 0)
    def _():
        for d in range(4):
            up(lax.rem(x + 4 - d, 4), d).wait_send()
        h2up().wait_send()

    @pl.when(t < 63)
    def _():
        for d in range(4):
            down(lax.rem(x + 4 - d, 4), d).wait_send()
        h2down().wait_send()

    step2_sent()

    @pl.when(c == 0)
    def _():
        for make in sent_a:
            make().wait_send()

    @pl.when(c == 1)
    def _():
        for make in sent_b:
            make().wait_send()


def per_device(latents, gain_first, conv_first, bias_first, gain_second, conv_second, bias_second):
    vm = pl.BlockSpec(memory_space=pltpu.VMEM)
    dma = pltpu.SemaphoreType.DMA
    return pl.pallas_call(
        kernel,
        out_shape=jax.ShapeDtypeStruct((2, 2, 64, 384), BF16),
        in_specs=[pl.BlockSpec(memory_space=pltpu.HBM)] * 7,
        out_specs=vm,
        scratch_shapes=[
            pltpu.VMEM((2, 2, 64, 384), BF16),
            pltpu.VMEM((4, 384), F32),
            pltpu.VMEM((27, 6, 384), BF16),
            pltpu.VMEM((27, 6, 384), BF16),
            pltpu.VMEM((8, 32, 128), BF16),
            pltpu.VMEM((8, 16, 384), BF16),
            pltpu.VMEM((48, 384), F32),
            pltpu.VMEM((8, 32, 128), BF16),
            pltpu.VMEM((8, 16, 384), BF16),
            pltpu.VMEM((2, 4, 3, 4, 2, 48, 128), BF16),
            pltpu.VMEM((4, 4, 2, 128, 384), BF16),
            pltpu.VMEM((4, 2, 4, 64, 384), BF16),
            pltpu.VMEM((4, 10, 2, 64, 256), F32),
            pltpu.VMEM((8, 2, 64, 128), F32),
            pltpu.VMEM((4, 8, 1024), F32),
            pltpu.VMEM((3, 10, 4, 64, 128), BF16),
            pltpu.VMEM((2, 8, 64, 128), BF16),
            pltpu.VMEM((3, 2, 2, 64, 384), BF16),
            pltpu.VMEM((3, 2, 2, 64, 384), BF16),
            dma((7,)), dma((8,)), dma((8,)), dma((8,)), dma((8,)), dma((3,)),
            dma((2, 27)), dma((2, 27)), dma((2, 9)), dma((2, 9)), dma((2, 9)), dma((2, 9)),
            dma((4,)), dma((4,)), dma((4,)), dma((4,)), dma((4,)), dma((4,)),
            dma((4,)), dma((4,)), dma((2,)), dma((2,)), dma((4,)), dma((4,)),
        ],
        compiler_params=pltpu.CompilerParams(
            collective_id=0, has_side_effects=True, vmem_limit_bytes=63 * 1024 * 1024
        ),
        cost_estimate=pl.CostEstimate(flops=4_000_000_000, bytes_accessed=8_000_000, transcendentals=400_000),
    )(
        latents, gain_first, bias_first, gain_second, bias_second,
        conv_first.reshape(27, 6, 384), conv_second.reshape(27, 6, 384),
    )


def solution(mesh):
    in_specs = (
        P("span", "tile", None, None),
        P(),
        P(None, None, None, "tile", None),
        P(),
        P(),
        P(None, None, None, "tile", None),
        P(),
    )
    out_specs = P("span", "tile", None, None)
    return jax.shard_map(
        per_device, mesh=mesh, in_specs=in_specs, out_specs=out_specs, check_vma=False
    )
```

```python
import jax
import jax.numpy as jnp
from jax import lax
from jax.experimental import pallas as pl
from jax.experimental.pallas import tpu as pltpu
from jax.sharding import PartitionSpec as P

MESH = pl.DeviceIdType.MESH
F32 = jnp.float32
BF16 = jnp.bfloat16

SLOTS = ((0, 1), (0, 0), (0, 2), (2, 0), (1, 1), (1, 0), (1, 2), (2, 2), (2, 1))


def silu(u):
    return u / (1.0 + jnp.exp(-u))


def kernel(
    lat_hbm, gain1_hbm, bias1_hbm, gain2_hbm, bias2_hbm, k1_hbm, k2_hbm, out,
    lat, vec, k1, k2, s1, s2, stack,
    r1, r2, w1, w2, abuf, pbuf, hbuf, ssbuf, a2s, a2h, sendb, recvb,
    ins, st1s, st1r, st2s, st2r, loc,
    w1zs, w1zr, ysend, yrecv, rsend, rrecv, bsend, brecv,
    xs, xr, ups, upr, dns, dnr, sss, ssr, h2s, h2r, fs, fr,
):
    x = lax.axis_index("span")
    t = lax.axis_index("tile")
    c = lax.rem(t, 2)
    z = lax.rem(lax.div(t, 2), 8)
    y = lax.div(t, 16)
    zi = lax.rem(z, 4)
    h = lax.div(z, 4)
    j = lax.rem(t, 8)
    g = lax.div(t, 8)

    def dev(yy, zz, cc):
        return (x, yy * 16 + zz * 2 + cc)

    def rc(src, dst, ssem, rsem, device):
        return pltpu.make_async_remote_copy(
            src_ref=src, dst_ref=dst, send_sem=ssem, recv_sem=rsem,
            device_id=device, device_id_type=MESH,
        )

    loads = [
        pltpu.make_async_copy(k1_hbm, k1, ins.at[0]),
        pltpu.make_async_copy(lat_hbm, lat, ins.at[1]),
        pltpu.make_async_copy(k2_hbm, k2, ins.at[2]),
        pltpu.make_async_copy(gain1_hbm, vec.at[0], ins.at[3]),
        pltpu.make_async_copy(bias1_hbm, vec.at[1], ins.at[4]),
        pltpu.make_async_copy(gain2_hbm, vec.at[2], ins.at[5]),
        pltpu.make_async_copy(bias2_hbm, vec.at[3], ins.at[6]),
    ]
    for load in loads:
        load.start()

    barrier = pltpu.get_barrier_semaphore()

    def hail(device):
        pl.semaphore_signal(barrier, inc=1, device_id=device, device_id_type=MESH)

    for e in range(4):
        for d in range(8):
            if e or d:
                hail((x, lax.rem(y + e, 4) * 16 + h * 8 + lax.rem(j + d, 8)))

    @pl.when(x != y)
    def _():
        for d in range(8):
            hail((y, x * 16 + h * 8 + lax.rem(j + d, 8)))

    for d in range(1, 4):
        hail((lax.rem(x + d, 4), t))
    for d in (1, 2, 6, 7):
        hail(dev(y, lax.rem(z + d, 8), c))

    @pl.when(t > 0)
    def _():
        hail((x, t - 1))

    @pl.when(t < 63)
    def _():
        hail((x, t + 1))

    lane8 = lax.broadcasted_iota(jnp.int32, (8, 128), 1)
    turn = lax.rem(384 - 96 * x, 384)

    def mine96(v):
        return pltpu.roll(v, turn, 1)[:, 0:128]

    loads[0].wait()
    pad2 = jnp.zeros((2, 384), F32)
    tiles = []
    for dy in range(3):
        got_slots = []
        for dt, dx in SLOTS:
            got_slots.append(mine96(jnp.concatenate([k1[dt * 9 + dy * 3 + dx].astype(F32), pad2], axis=0)))

        def at(n, by):
            return pltpu.roll(got_slots[n], by, 1) if by else got_slots[n]

        row = [
            jnp.where(lane8 < 96, at(0, 0), at(1, 96)),
            jnp.where(lane8 < 64, at(1, 96), at(2, 64)),
            jnp.where(lane8 < 32, at(2, 64), at(3, 32)),
            jnp.where(lane8 < 96, at(4, 0), at(5, 96)),
            jnp.where(lane8 < 64, at(5, 96), at(6, 64)),
            jnp.where(lane8 < 32, at(6, 64), at(7, 32)),
            jnp.where(lane8 < 96, at(8, 0), 0.0),
            jnp.zeros((8, 128), F32),
        ]
        tiles.append(row)
    for n in range(8):
        s1[n, 0:16] = jnp.concatenate([tiles[0][n], tiles[1][n]], axis=0).astype(BF16)
        s1[n, 16:32] = jnp.concatenate([tiles[2][n], jnp.zeros((8, 128), F32)], axis=0).astype(BF16)
    loads[2].wait()
    for n in range(8):
        tap = jnp.minimum(8 * x + n, 26)
        s2[n] = jnp.concatenate([k2[tap].astype(F32), jnp.zeros((10, 384), F32)], axis=0).astype(BF16)
    for load in loads[3:]:
        load.wait()
    loads[1].wait()
    gain1 = vec[0:1]
    bias2 = vec[3:4]
    bias1 = jnp.where(lane8[0:1] < 96, mine96(jnp.broadcast_to(vec[1:2], (8, 384)))[0:1], 0.0)
    gain2 = jnp.where(lane8[0:1] < 96, mine96(jnp.broadcast_to(vec[2:3], (8, 384)))[0:1], 0.0)

    w1[1, 3] = jnp.zeros((3, 4, 2, 48, 128), BF16)
    w2[:, :, :, 96:128, :] = jnp.zeros((4, 4, 2, 32, 384), BF16)
    a2s[:, 0:2] = jnp.zeros((3, 2, 4, 64, 128), BF16)

    def zero_p(i, carry):
        pbuf[i, 0:2] = jnp.zeros((2, 2, 64, 256), F32)
        return carry

    lax.fori_loop(0, 4, zero_p, 0)

    def act1(i, carry):
        v = lat[i].reshape(128, 384).astype(F32)
        ms = jnp.mean(v * v, axis=-1, keepdims=True)
        u = v * lax.rsqrt(ms + 1e-6) * gain1
        abuf[x, i, 1:3] = silu(u).astype(BF16).reshape(2, 64, 384)
        return carry

    lax.fori_loop(0, 2, act1, 0)

    many = jnp.where(x != y, 8, 0) + jnp.where(t > 0, 1, 0) + jnp.where(t < 63, 1, 0) + 38
    pl.semaphore_wait(barrier, many)

    def st1(e, d):
        jj = lax.rem(j + d, 8)
        return rc(s1.at[jj], r1.at[y, j], st1s.at[e, d], st1r.at[e, d], (x, lax.rem(y + e, 4) * 16 + h * 8 + jj))

    def st2(d):
        jj = lax.rem(j + d, 8)
        return rc(s2.at[jj], r2.at[j], st2s.at[d], st2r.at[d], (y, x * 16 + h * 8 + jj))

    def own2():
        return pltpu.make_async_copy(s2.at[j], r2.at[j], loc.at[1])

    for e in (2, 1, 3, 0):
        for d in range(8):
            if e or d:

                @pl.when(lax.rem(j + d, 8) != 7)
                def _():
                    st1(e, d).start()

    own1 = pltpu.make_async_copy(s1.at[j], r1.at[y, j], loc.at[0])
    own1.start()

    def xsend(d):
        return rc(
            abuf.at[x, :, 1:3], abuf.at[x, :, 1:3], xs.at[d], xr.at[d], (lax.rem(x + d, 4), t)
        )

    def up(src, d):
        return rc(abuf.at[src, :, 1], abuf.at[src, :, 3], ups.at[d], upr.at[d], (x, t - 1))

    def down(src, d):
        return rc(abuf.at[src, :, 2], abuf.at[src, :, 0], dns.at[d], dnr.at[d], (x, t + 1))

    def halo_send(d):
        src = lax.rem(x + 4 - d, 4)

        @pl.when(t > 0)
        def _():
            up(src, d).start()

        @pl.when(t < 63)
        def _():
            down(src, d).start()

    def xstep(d):
        src = lax.rem(x + 4 - d, 4)
        land = abuf.at[src, :, 1:3]
        rc(land, land, xs.at[d], xr.at[d], (x, t)).wait_recv()
        halo_send(d)

    def halo_wait():
        for d in range(4):
            src = lax.rem(x + 4 - d, 4)

            @pl.when(t > 0)
            def _():
                land = abuf.at[src, :, 0]
                rc(land, land, dns.at[d], dnr.at[d], (x, t)).wait_recv()

            @pl.when(t < 63)
            def _():
                land = abuf.at[src, :, 3]
                rc(land, land, ups.at[d], upr.at[d], (x, t)).wait_recv()

        @pl.when(t == 0)
        def _():
            abuf[:, :, 0] = jnp.zeros((4, 2, 64, 384), BF16)

        @pl.when(t == 63)
        def _():
            abuf[:, :, 3] = jnp.zeros((4, 2, 64, 384), BF16)

    for d in range(1, 4):
        xsend(d).start()
    for d in range(8):
        if d == 0:

            @pl.when(x != y)
            def _():
                st2(0).start()

            @pl.when(x == y)
            def _():
                own2().start()
        else:
            st2(d).start()
    halo_send(0)

    def blk(k, yy, zz, cc):
        if k == 0:
            return w1.at[cc, lax.rem(zz, 4), :, yy, lax.div(zz, 4)]
        return w2.at[yy, lax.rem(zz, 4), cc, pl.ds(pl.multiple_of(48 * lax.div(zz, 4), 16), 48), :]

    def zset(zz):
        return w1.at[1, lax.rem(zz, 4), :, :, lax.div(zz, 4)]

    def yset(yy):
        return w1.at[0, :, :, yy]

    def got(ref, rsem):
        rc(ref, ref, loc.at[2], rsem, (x, t)).wait_recv()

    def zz(s):
        return lax.rem(z + 8 + s, 8)

    WAY = {1: 0, -1: 1, 2: 2, -2: 3, 3: 4, -3: 5, 4: 6, -4: 7, 0: 8}

    def yy_of(e):
        return lax.rem(y + e, 4)

    def live(origin):
        return lax.rem(z + 8 + origin, 4) != 3

    def a_z(e, origin, total):
        ref = blk(0, yy_of(e), zz(origin), 1)
        i = WAY[total]
        return rc(ref, ref, w1zs.at[i, e], w1zr.at[i, e], dev(y, zz(origin + total), 1))

    def a_got(e, total):
        got(blk(0, yy_of(e), zz(-total), 1), w1zr.at[WAY[total], e])

    def a_sib(s):
        ref = zset(zz(s))
        return rc(ref, ref, bsend.at[0, WAY[s]], brecv.at[0, WAY[s]], dev(y, z, 0))

    def b_z(origin, total):
        ref = blk(0, y, zz(origin), 0)
        i = WAY[total]
        return rc(ref, ref, w1zs.at[i, 0], w1zr.at[i, 0], dev(y, zz(origin + total), 0))

    def b_got(total):
        got(blk(0, y, zz(-total), 0), w1zr.at[WAY[total], 0])

    def b_y(d, s):
        ref = blk(0, y, zz(s), 0)
        i = (d - 1) * 9 + WAY[s]
        return rc(ref, ref, ysend.at[0, i], yrecv.at[0, i], dev(lax.rem(y + d, 4), z, 0))

    def b_sib(d):
        ref = yset(lax.rem(y + d, 4))
        return rc(ref, ref, bsend.at[0, d], brecv.at[0, d], dev(y, z, 1))

    AROUND = (2, -2, 1, -1)

    def a_relays(e, total):
        if total == 2:
            return ((-2, 3), (-2, 4)) if e < 2 else ((-2, 3),)
        return ((2, -3), (2, -4)) if e >= 2 else ((2, -3),)

    B_RELAYS = {2: ((-2, 4), (-2, 3)), -2: ((2, -3),)}
    OTHERS = (2, -2, 1, -1, 3, -3, 4)

    def on_core(core, f):
        @pl.when(c == core)
        def _():
            f()

    def when_live(origin, f):
        @pl.when(live(origin))
        def _():
            f()

    def first(e):
        def send_a():
            for total in AROUND:
                a_z(e, 0, total).start()

        on_core(1, lambda: when_live(0, send_a))
        if e == 0:

            def send_b():
                for total in AROUND:
                    b_z(0, total).start()

            on_core(0, send_b)

    def step(n):
        def core1():
            if n == 1:
                for total in (2, -2):

                    def relay(total=total):
                        for e in (0, 1, 3, 2):
                            a_got(e, total)
                            for origin, far in a_relays(e, total):
                                a_z(e, origin, far).start()
                        a_sib(-total).start()

                    when_live(-total, relay)
                when_live(0, lambda: a_sib(0).start())
            if n == 2:
                for total in (1, -1):

                    def take(total=total):
                        for e in range(4):
                            a_got(e, total)
                        a_sib(-total).start()

                    when_live(-total, take)
            if n == 3:
                for total in (3, -3):

                    def take(total=total):
                        for e in range(4):
                            a_got(e, total)
                        a_sib(-total).start()

                    when_live(-total, take)

                def last():
                    for e in range(4):
                        a_got(e, 4 if e < 2 else -4)
                    a_sib(4).start()

                when_live(4, last)
            if n == 5:
                for d in range(4):
                    got(yset(yy_of(d)), brecv.at[0, d])

        def core0():
            if n == 1:
                for total in (2, -2):
                    b_got(total)
                    for origin, far in B_RELAYS[total]:
                        b_z(origin, far).start()
                    for d in (2, 1, 3):
                        b_y(d, -total).start()
            if n == 2:
                for total in (1, -1):
                    b_got(total)
                    for d in (2, 1, 3):
                        b_y(d, -total).start()
            if n == 3:
                for total, origin in ((3, -3), (-3, 3), (4, 4)):
                    b_got(total)
                    for d in (2, 1, 3):
                        b_y(d, origin).start()
                b_sib(0).start()
            if n == 4:
                for d in (1, 3, 2):
                    for s in OTHERS:
                        got(blk(0, lax.rem(y + 4 - d, 4), zz(s), 0), yrecv.at[0, (d - 1) * 9 + WAY[s]])
                    b_sib(4 - d).start()
            if n == 5:
                for s in (0,) + OTHERS:
                    when_live(s, lambda s=s: got(zset(zz(s)), brecv.at[0, WAY[s]]))

        on_core(1, core1)
        on_core(0, core0)

    def step_sent():
        def core1():
            def own():
                for e in range(4):
                    for total in AROUND:
                        a_z(e, 0, total).wait_send()

            when_live(0, own)
            for total in (2, -2):

                def relayed(total=total):
                    for e in range(4):
                        for origin, far in a_relays(e, total):
                            a_z(e, origin, far).wait_send()

                when_live(-total, relayed)
            for s in (0,) + OTHERS:
                when_live(s, lambda s=s: a_sib(s).wait_send())

        def core0():
            for total in AROUND:
                b_z(0, total).wait_send()
            for total in (2, -2):
                for origin, far in B_RELAYS[total]:
                    b_z(origin, far).wait_send()
            for s in OTHERS:
                for d in range(1, 4):
                    b_y(d, s).wait_send()
            for d in range(4):
                b_sib(d).wait_send()

        on_core(1, core1)
        on_core(0, core0)

    def wset(yy, cc):
        return w2.at[yy, :, cc, 0:96, :]

    def z2_send(origin, total):
        ref = blk(1, y, zz(origin), c)
        i = WAY[total]
        return rc(ref, ref, rsend.at[1, i], rrecv.at[1, i], dev(y, zz(origin + total), c))

    def z2_got(total):
        got(blk(1, y, zz(-total), c), rrecv.at[1, WAY[total]])

    def y2_send(d):
        ref = wset(y, c)
        return rc(ref, ref, ysend.at[1, d], yrecv.at[1, d], dev(lax.rem(y + d, 4), z, c))

    def sib2_send(d):
        ref = wset(lax.rem(y + d, 4), c)
        return rc(ref, ref, bsend.at[1, d], brecv.at[1, d], dev(y, z, 1 - c))

    Z2 = ((0, 2), (0, -2), (0, 1), (0, -1), (-2, 4), (-2, 3), (2, -3))

    def step2(n):
        if n == 0:
            for origin, total in Z2[:4]:
                z2_send(origin, total).start()
        if n == 1:
            z2_got(2)
            z2_send(-2, 4).start()
            z2_send(-2, 3).start()
            z2_got(-2)
            z2_send(2, -3).start()
        if n == 2:
            for total in (1, -1, 3, -3, 4):
                z2_got(total)
            for d in (2, 1, 3):
                y2_send(d).start()
            sib2_send(0).start()
        if n == 3:
            for d in (1, 3, 2):
                got(wset(lax.rem(y + 4 - d, 4), c), yrecv.at[1, d])
                sib2_send(4 - d).start()
        if n == 4:
            for d in range(4):
                got(wset(lax.rem(y + d, 4), 1 - c), brecv.at[1, d])

    def step2_sent():
        for origin, total in Z2:
            z2_send(origin, total).wait_send()
        for d in range(1, 4):
            y2_send(d).wait_send()
        for d in range(4):
            sib2_send(d).wait_send()

    own1.wait()
    for e in (0, 1, 3, 2):
        src = lax.rem(y + e, 4)

        @pl.when(j != 7)
        def _():
            for d in range(8):
                if e or d:
                    got(r1.at[src, lax.rem(j + 8 - d, 8)], st1r.at[(4 - e) % 4, d])
            for dy in range(3):
                for m in range(8):
                    two = r1[src, m, 16 * (dy // 2):16 * (dy // 2) + 16].astype(F32)
                    stack[m * 6:m * 6 + 6, 0:128] = two[(dy % 2) * 8:(dy % 2) * 8 + 6]
                w1[c, zi, dy, src, h] = stack[:, 0:128].astype(BF16)

        first(e)
    step(1)

    @pl.when(x != y)
    def _():
        got(r2.at[j], st2r.at[0])

    @pl.when(x == y)
    def _():
        own2().wait()

    for d in range(1, 8):
        got(r2.at[lax.rem(j + 8 - d, 8)], st2r.at[d])
    for m in range(8):
        stack[m * 6:m * 6 + 6] = r2[m].astype(F32)[0:6]
    w2[y, zi, c, pl.ds(pl.multiple_of(48 * h, 16), 48), :] = stack[...].astype(BF16)
    step(2)
    xstep(1)
    xstep(3)
    step(3)
    step2(0)
    xstep(2)
    step2(1)
    step2(2)
    step(4)
    halo_wait()
    step(5)

    def conv1():
        rows = []
        for yy in range(2):
            rows.append(jnp.concatenate(
                [abuf[:, :, yy + dy].reshape(512, 384) for dy in range(3)], axis=1))
        lhs = jnp.concatenate(rows, axis=0)

        def tile(n, carry):
            rhs = jnp.concatenate(
                [w1[0, n].reshape(1152, 128), w1[1, n].reshape(1152, 128)], axis=1)
            res = jnp.dot(lhs, rhs, preferred_element_type=F32)
            for yy in range(2):
                pbuf[n, 2:10, yy] = res[yy * 512:yy * 512 + 512].reshape(8, 64, 256)
            return carry

        lax.fori_loop(0, 4, tile, 0)

    conv1()

    lane = lax.broadcasted_iota(jnp.int32, (64, 128), 1)
    row = lax.broadcasted_iota(jnp.int32, (64, 128), 0)

    def shift_down(v):
        return jnp.where(row > 0, pltpu.roll(v, 1, 0), 0.0)

    def shift_up(v):
        return jnp.where(row < 63, pltpu.roll(v, 63, 0), 0.0)

    def combine(f, carry):
        for yy in range(2):
            def p(dt, n):
                return pbuf[n // 2, f + dt, yy, :, (n % 2) * 128:(n % 2) * 128 + 128]

            m1 = p(0, 0) + p(1, 3) + p(2, 6)
            a_lo = p(0, 0) + p(1, 3)
            mid = p(0, 1) + p(1, 4)
            b_hi = p(0, 2) + p(1, 5)
            m0 = pltpu.roll(jnp.where(lane >= 96, a_lo, mid), 32, 1) + pltpu.roll(p(2, 2), 96, 1)
            m2 = pltpu.roll(jnp.where(lane >= 64, mid, b_hi), 64, 1) + pltpu.roll(p(2, 5), 96, 1)
            hid = m1 + shift_down(m0) + shift_up(m2) + bias1
            hbuf[f, yy] = jnp.where(lane < 96, hid, 0.0)
        return carry

    lax.fori_loop(0, 8, combine, 0)

    hv = hbuf[...].reshape(1024, 128)
    ssbuf[0] = lax.dot_general(
        jnp.ones((8, 128), F32), hv * hv, (((1,), (1,)), ((), ())),
        precision=lax.Precision.HIGHEST, preferred_element_type=F32,
    )

    def ss_send(d):
        return rc(ssbuf.at[0], ssbuf.at[d], sss.at[d], ssr.at[d], (lax.rem(x + d, 4), t))

    for d in range(1, 4):
        ss_send(d).start()
    for d in range(1, 4):
        got(ssbuf.at[d], ssr.at[d])
    total = ssbuf[0] + ssbuf[1] + ssbuf[2] + ssbuf[3]
    ms = lax.dot_general(
        total, jnp.full((8, 128), 0.125, F32), (((0,), (0,)), ((), ())),
        precision=lax.Precision.HIGHEST, preferred_element_type=F32,
    ) * (1.0 / 384.0)
    hv = hbuf[...].reshape(1024, 128)
    hbuf[...] = (hv * lax.rsqrt(ms + 1e-6) * gain2).reshape(8, 2, 64, 128)

    def spread(f, where, v):
        a2s[0, f + 2, where] = shift_down(v).astype(BF16)
        a2s[1, f + 2, where] = v.astype(BF16)
        a2s[2, f + 2, where] = shift_up(v).astype(BF16)

    def act2(f, carry):
        for yy in range(2):
            spread(f, 1 + yy, silu(hbuf[f, yy]))
        return carry

    lax.fori_loop(0, 8, act2, 0)

    def h2up():
        return rc(a2s.at[1, 2:10, 1], a2h.at[1], h2s.at[0], h2r.at[0], (x, t - 1))

    def h2down():
        return rc(a2s.at[1, 2:10, 2], a2h.at[0], h2s.at[1], h2r.at[1], (x, t + 1))

    @pl.when(t > 0)
    def _():
        h2up().start()

    @pl.when(t < 63)
    def _():
        h2down().start()

    step2(3)
    step2(4)

    @pl.when(t > 0)
    def _():
        got(a2h.at[0], h2r.at[1])

    @pl.when(t == 0)
    def _():
        a2h[0] = jnp.zeros((8, 64, 128), BF16)

    @pl.when(t < 63)
    def _():
        got(a2h.at[1], h2r.at[0])

    @pl.when(t == 63)
    def _():
        a2h[1] = jnp.zeros((8, 64, 128), BF16)

    def halo2(f, carry):
        spread(f, 0, a2h[0, f].astype(F32))
        spread(f, 3, a2h[1, f].astype(F32))
        return carry

    lax.fori_loop(0, 8, halo2, 0)

    def conv2(q):
        acc = None
        for dt in range(3):
            lhs, rhs = [], []
            for dy in range(3):
                for dx in range(3):
                    tap = dt * 9 + dy * 3 + dx
                    lhs.append(a2s[dx, pl.ds(2 * q + dt, 2), dy:dy + 2].reshape(256, 128))
                    rhs.append(w2[tap // 8, (tap % 8) // 2, tap % 2])
            part = jnp.dot(
                jnp.concatenate(lhs, axis=1), jnp.concatenate(rhs, axis=0),
                preferred_element_type=F32,
            )
            acc = part if acc is None else acc + part
        return acc

    def out_send(d):
        return rc(sendb.at[d - 1], recvb.at[d - 1], fs.at[d], fr.at[d], (lax.rem(x + d, 4), t))

    for d in (2, 1, 3):
        sendb[d - 1] = conv2(lax.rem(x + d, 4)).astype(BF16).reshape(2, 2, 64, 384)
        out_send(d).start()
    mine = conv2(x) + bias2 + lat[...].reshape(256, 384).astype(F32)
    for d in (2, 1, 3):
        got(recvb.at[d - 1], fr.at[d])
        mine = mine + recvb[d - 1].reshape(256, 384).astype(F32)
    out[...] = mine.astype(BF16).reshape(2, 2, 64, 384)

    for e in range(4):
        for d in range(8):
            if e or d:

                @pl.when(lax.rem(j + d, 8) != 7)
                def _():
                    st1(e, d).wait_send()

    for d in range(1, 8):
        st2(d).wait_send()

    @pl.when(x != y)
    def _():
        st2(0).wait_send()

    for d in range(1, 4):
        xsend(d).wait_send()
        ss_send(d).wait_send()
        out_send(d).wait_send()

    @pl.when(t > 0)
    def _():
        for d in range(4):
            up(lax.rem(x + 4 - d, 4), d).wait_send()
        h2up().wait_send()

    @pl.when(t < 63)
    def _():
        for d in range(4):
            down(lax.rem(x + 4 - d, 4), d).wait_send()
        h2down().wait_send()

    step2_sent()

    step_sent()


def per_device(latents, gain_first, conv_first, bias_first, gain_second, conv_second, bias_second):
    vm = pl.BlockSpec(memory_space=pltpu.VMEM)
    dma = pltpu.SemaphoreType.DMA
    return pl.pallas_call(
        kernel,
        out_shape=jax.ShapeDtypeStruct((2, 2, 64, 384), BF16),
        in_specs=[pl.BlockSpec(memory_space=pltpu.HBM)] * 7,
        out_specs=vm,
        scratch_shapes=[
            pltpu.VMEM((2, 2, 64, 384), BF16),
            pltpu.VMEM((4, 384), F32),
            pltpu.VMEM((27, 6, 384), BF16),
            pltpu.VMEM((27, 6, 384), BF16),
            pltpu.VMEM((8, 32, 128), BF16),
            pltpu.VMEM((8, 16, 384), BF16),
            pltpu.VMEM((48, 384), F32),
            pltpu.VMEM((4, 8, 32, 128), BF16),
            pltpu.VMEM((8, 16, 384), BF16),
            pltpu.VMEM((2, 4, 3, 4, 2, 48, 128), BF16),
            pltpu.VMEM((4, 4, 2, 128, 384), BF16),
            pltpu.VMEM((4, 2, 4, 64, 384), BF16),
            pltpu.VMEM((4, 10, 2, 64, 256), F32),
            pltpu.VMEM((8, 2, 64, 128), F32),
            pltpu.VMEM((4, 8, 1024), F32),
            pltpu.VMEM((3, 10, 4, 64, 128), BF16),
            pltpu.VMEM((2, 8, 64, 128), BF16),
            pltpu.VMEM((3, 2, 2, 64, 384), BF16),
            pltpu.VMEM((3, 2, 2, 64, 384), BF16),
            dma((7,)), dma((4, 8)), dma((4, 8)), dma((8,)), dma((8,)), dma((3,)),
            dma((9, 4)), dma((9, 4)),
            dma((2, 27)), dma((2, 27)), dma((2, 9)), dma((2, 9)), dma((2, 9)), dma((2, 9)),
            dma((4,)), dma((4,)), dma((4,)), dma((4,)), dma((4,)), dma((4,)),
            dma((4,)), dma((4,)), dma((2,)), dma((2,)), dma((4,)), dma((4,)),
        ],
        compiler_params=pltpu.CompilerParams(
            collective_id=0, has_side_effects=True, vmem_limit_bytes=63 * 1024 * 1024
        ),
        cost_estimate=pl.CostEstimate(flops=4_000_000_000, bytes_accessed=8_000_000, transcendentals=400_000),
    )(
        latents, gain_first, bias_first, gain_second, bias_second,
        conv_first.reshape(27, 6, 384), conv_second.reshape(27, 6, 384),
    )


def solution(mesh):
    in_specs = (
        P("span", "tile", None, None),
        P(),
        P(None, None, None, "tile", None),
        P(),
        P(),
        P(None, None, None, "tile", None),
        P(),
    )
    out_specs = P("span", "tile", None, None)
    return jax.shard_map(
        per_device, mesh=mesh, in_specs=in_specs, out_specs=out_specs, check_vma=False
    )
```

```python
import jax
import jax.numpy as jnp
from jax import lax
from jax.experimental import pallas as pl
from jax.experimental.pallas import tpu as pltpu
from jax.sharding import PartitionSpec as P

MESH = pl.DeviceIdType.MESH
F32 = jnp.float32
BF16 = jnp.bfloat16

SLOTS = ((0, 1), (0, 0), (0, 2), (2, 0), (1, 1), (1, 0), (1, 2), (2, 2), (2, 1))


def silu(u):
    return u / (1.0 + jnp.exp(-u))


def kernel(
    lat_hbm, gain1_hbm, bias1_hbm, gain2_hbm, bias2_hbm, k1_hbm, k2_hbm, out,
    lat, vec, k1, k2, s1, s2, stack,
    ruler, r1, r2, w1, w2, abuf, pbuf, hbuf, ssbuf, a2s, a2h, sendb, recvb,
    ins, st1s, st1r, st2s, st2r, loc,
    w1zs, w1zr, ysend, yrecv, rsend, rrecv, bsend, brecv,
    xs, xr, ups, upr, dns, dnr, sss, ssr, h2s, h2r, fs, fr,
):
    x = lax.axis_index("span")
    t = lax.axis_index("tile")
    c = lax.rem(t, 2)
    z = lax.rem(lax.div(t, 2), 8)
    y = lax.div(t, 16)
    zi = lax.rem(z, 4)
    h = lax.div(z, 4)
    j = lax.rem(t, 8)
    g = lax.div(t, 8)

    def dev(yy, zz, cc):
        return (x, yy * 16 + zz * 2 + cc)

    def rc(src, dst, ssem, rsem, device):
        return pltpu.make_async_remote_copy(
            src_ref=src, dst_ref=dst, send_sem=ssem, recv_sem=rsem,
            device_id=device, device_id_type=MESH,
        )

    def got(ref, rsem):
        rc(ref, ref, loc.at[2], rsem, (x, t)).wait_recv()

    def gone(rows, ssem):
        size = ruler.at[0:rows]
        rc(size, size, ssem, loc.at[2], (x, t)).wait_send()

    def came(rows, rsem):
        got(ruler.at[0:rows], rsem)

    loads = [
        pltpu.make_async_copy(k1_hbm, k1, ins.at[0]),
        pltpu.make_async_copy(lat_hbm, lat, ins.at[1]),
        pltpu.make_async_copy(k2_hbm, k2, ins.at[2]),
        pltpu.make_async_copy(gain1_hbm, vec.at[0], ins.at[3]),
        pltpu.make_async_copy(bias1_hbm, vec.at[1], ins.at[4]),
        pltpu.make_async_copy(gain2_hbm, vec.at[2], ins.at[5]),
        pltpu.make_async_copy(bias2_hbm, vec.at[3], ins.at[6]),
    ]
    for load in loads:
        load.start()

    barrier = pltpu.get_barrier_semaphore()

    def hail(device):
        pl.semaphore_signal(barrier, inc=1, device_id=device, device_id_type=MESH)

    for e in range(4):
        for d in range(8):
            if e or d:
                hail((x, lax.rem(y + e, 4) * 16 + h * 8 + lax.rem(j + d, 8)))

    @pl.when(x != y)
    def _():
        for d in range(8):
            hail((y, x * 16 + h * 8 + lax.rem(j + d, 8)))

    for d in range(1, 4):
        hail((lax.rem(x + d, 4), t))
    for d in (1, 2, 6, 7):
        hail(dev(y, lax.rem(z + d, 8), c))

    @pl.when(t > 0)
    def _():
        hail((x, t - 1))

    @pl.when(t < 63)
    def _():
        hail((x, t + 1))

    lane8 = lax.broadcasted_iota(jnp.int32, (8, 128), 1)
    turn = lax.rem(384 - 96 * x, 384)

    def mine96(v):
        return pltpu.roll(v, turn, 1)[:, 0:128]

    loads[0].wait()
    pad2 = jnp.zeros((2, 384), F32)
    tiles = []
    for dy in range(3):
        got_slots = []
        for dt, dx in SLOTS:
            got_slots.append(mine96(jnp.concatenate([k1[dt * 9 + dy * 3 + dx].astype(F32), pad2], axis=0)))

        def at(n, by):
            return pltpu.roll(got_slots[n], by, 1) if by else got_slots[n]

        row = [
            jnp.where(lane8 < 96, at(0, 0), at(1, 96)),
            jnp.where(lane8 < 64, at(1, 96), at(2, 64)),
            jnp.where(lane8 < 32, at(2, 64), at(3, 32)),
            jnp.where(lane8 < 96, at(4, 0), at(5, 96)),
            jnp.where(lane8 < 64, at(5, 96), at(6, 64)),
            jnp.where(lane8 < 32, at(6, 64), at(7, 32)),
            jnp.where(lane8 < 96, at(8, 0), 0.0),
            jnp.zeros((8, 128), F32),
        ]
        tiles.append(row)
    for n in range(8):
        s1[n, 0:16] = jnp.concatenate([tiles[0][n], tiles[1][n]], axis=0).astype(BF16)
        s1[n, 16:32] = jnp.concatenate([tiles[2][n], jnp.zeros((8, 128), F32)], axis=0).astype(BF16)
    loads[2].wait()
    for n in range(8):
        tap = jnp.minimum(8 * x + n, 26)
        s2[n] = jnp.concatenate([k2[tap].astype(F32), jnp.zeros((10, 384), F32)], axis=0).astype(BF16)
    for load in loads[3:]:
        load.wait()
    loads[1].wait()
    gain1 = vec[0:1]
    bias2 = vec[3:4]
    bias1 = jnp.where(lane8[0:1] < 96, mine96(jnp.broadcast_to(vec[1:2], (8, 384)))[0:1], 0.0)
    gain2 = jnp.where(lane8[0:1] < 96, mine96(jnp.broadcast_to(vec[2:3], (8, 384)))[0:1], 0.0)

    w1[1, 3] = jnp.zeros((3, 4, 2, 48, 128), BF16)
    w2[:, :, :, 96:128, :] = jnp.zeros((4, 4, 2, 32, 384), BF16)
    a2s[:, 0:2] = jnp.zeros((3, 2, 4, 64, 128), BF16)

    def zero_p(i, carry):
        pbuf[i, 0:2] = jnp.zeros((2, 2, 64, 256), F32)
        return carry

    lax.fori_loop(0, 4, zero_p, 0)

    def act1(i, carry):
        v = lat[i].reshape(128, 384).astype(F32)
        ms = jnp.mean(v * v, axis=-1, keepdims=True)
        u = v * lax.rsqrt(ms + 1e-6) * gain1
        abuf[x, i, 1:3] = silu(u).astype(BF16).reshape(2, 64, 384)
        return carry

    lax.fori_loop(0, 2, act1, 0)

    many = jnp.where(x != y, 8, 0) + jnp.where(t > 0, 1, 0) + jnp.where(t < 63, 1, 0) + 38
    pl.semaphore_wait(barrier, many)

    def st1(e, d):
        jj = lax.rem(j + d, 8)
        return rc(s1.at[jj], r1.at[y, j], st1s.at[0], st1r.at[e], (x, lax.rem(y + e, 4) * 16 + h * 8 + jj))

    def st2(d):
        jj = lax.rem(j + d, 8)
        return rc(s2.at[jj], r2.at[j], st2s.at[0], st2r.at[0], (y, x * 16 + h * 8 + jj))

    def own2():
        return pltpu.make_async_copy(s2.at[j], r2.at[j], loc.at[1])

    for e in (2, 1, 3, 0):
        for d in range(8):
            if e or d:

                @pl.when(lax.rem(j + d, 8) != 7)
                def _():
                    st1(e, d).start()

    own1 = pltpu.make_async_copy(s1.at[j], r1.at[y, j], loc.at[0])
    own1.start()

    def xsend(d):
        return rc(
            abuf.at[x, :, 1:3], abuf.at[x, :, 1:3], xs.at[0], xr.at[d], (lax.rem(x + d, 4), t)
        )

    def up(src, d):
        return rc(abuf.at[src, :, 1], abuf.at[src, :, 3], ups.at[0], upr.at[0], (x, t - 1))

    def down(src, d):
        return rc(abuf.at[src, :, 2], abuf.at[src, :, 0], dns.at[0], dnr.at[0], (x, t + 1))

    def halo_send(d):
        src = lax.rem(x + 4 - d, 4)

        @pl.when(t > 0)
        def _():
            up(src, d).start()

        @pl.when(t < 63)
        def _():
            down(src, d).start()

    def xstep(d):
        src = lax.rem(x + 4 - d, 4)
        land = abuf.at[src, :, 1:3]
        got(land, xr.at[d])
        halo_send(d)

    def halo_wait():
        @pl.when(t > 0)
        def _():
            came(4 * 384, dnr.at[0])

        @pl.when(t < 63)
        def _():
            came(4 * 384, upr.at[0])

        @pl.when(t == 0)
        def _():
            abuf[:, :, 0] = jnp.zeros((4, 2, 64, 384), BF16)

        @pl.when(t == 63)
        def _():
            abuf[:, :, 3] = jnp.zeros((4, 2, 64, 384), BF16)

    for d in range(8):
        if d == 0:

            @pl.when(x != y)
            def _():
                st2(0).start()

            @pl.when(x == y)
            def _():
                own2().start()
        else:
            st2(d).start()
    for d in (2, 1, 3):
        xsend(d).start()
    halo_send(0)

    def blk(k, yy, zz, cc):
        if k == 0:
            return w1.at[cc, lax.rem(zz, 4), :, yy, lax.div(zz, 4)]
        return w2.at[yy, lax.rem(zz, 4), cc, pl.ds(pl.multiple_of(48 * lax.div(zz, 4), 16), 48), :]

    def zset(zz):
        return w1.at[1, lax.rem(zz, 4), :, :, lax.div(zz, 4)]

    def zz(s):
        return lax.rem(z + 8 + s, 8)

    WAY = {1: 0, -1: 1, 2: 2, -2: 3, 3: 4, -3: 5, 4: 6, -4: 7, 0: 8}
    AROUND = (2, -2, 1, -1)
    B_RELAYS = {2: ((-2, 4), (-2, 3)), -2: ((2, -3),)}

    def yy_of(e):
        return lax.rem(y + e, 4)

    def zi_of(origin):
        return lax.rem(z + 8 + origin, 4)

    def when_a(origin, f):
        @pl.when(jnp.logical_and(c == 1, zi_of(origin) == 0))
        def _():
            f()

    def when_b(origin, f):
        k = zi_of(origin)

        @pl.when(jnp.logical_or(c == 0, jnp.logical_or(k == 1, k == 2)))
        def _():
            f()

    def on_core(core, f):
        @pl.when(c == core)
        def _():
            f()

    def a_z(e, origin, total):
        ref = blk(0, yy_of(e), zz(origin), 1)
        i = WAY[total]
        k = 9 + 4 * (i - 2) + e if total in (2, -2) else i
        return rc(ref, ref, w1zs.at[0], w1zr.at[k], dev(y, zz(origin + total), 1))

    def a_got(e, total):
        got(blk(0, yy_of(e), zz(-total), 1), w1zr.at[9 + 4 * (WAY[total] - 2) + e])

    def a_relays(e, total):
        if total == 2:
            return ((-2, 3), (-2, 4)) if e < 2 else ((-2, 3),)
        return ((2, -3), (2, -4)) if e >= 2 else ((2, -3),)

    def a_sib(s):
        ref = zset(zz(s))
        return rc(ref, ref, bsend.at[0], brecv.at[0], dev(y, z, 0))

    def b_z(origin, total):
        ref = blk(0, y, zz(origin), c)
        i = WAY[total]
        return rc(ref, ref, w1zs.at[0], w1zr.at[i], dev(y, zz(origin + total), c))

    def b_got(total):
        got(blk(0, y, zz(-total), c), w1zr.at[WAY[total]])

    def b_y(d, s):
        ref = blk(0, y, zz(s), c)
        return rc(ref, ref, ysend.at[0], yrecv.at[d - 1], dev(lax.rem(y + d, 4), z, c))

    def b_sib(core, d):
        yy = lax.rem(y + d, 4)
        ref = w1.at[0, :, :, yy] if core == 0 else w1.at[1, 1:3, :, yy]
        return rc(ref, ref, bsend.at[0], brecv.at[0], dev(y, z, 1 - core))

    def first(e):
        def send_a():
            for total in AROUND:
                a_z(e, 0, total).start()

        when_a(0, send_a)
        if e == 0:

            def send_b():
                for total in AROUND:
                    b_z(0, total).start()

            when_b(0, send_b)

    def y_all(origin):
        for d in (2, 1, 3):
            b_y(d, origin).start()

    def step(n):
        if n == 1:
            for total in (2, -2):

                def relay(total=total):
                    for e in (0, 1, 3, 2):
                        a_got(e, total)
                        for origin, far in a_relays(e, total):
                            a_z(e, origin, far).start()
                    a_sib(-total).start()

                def take(total=total):
                    b_got(total)
                    for origin, far in B_RELAYS[total]:
                        b_z(origin, far).start()
                    y_all(-total)

                when_a(-total, relay)
                when_b(-total, take)
            when_a(0, lambda: a_sib(0).start())
        if n == 2 or n == 3:
            for total in ((1, -1) if n == 2 else (3, -3)):

                def whole(total=total):
                    came(4 * 144, w1zr.at[WAY[total]])
                    a_sib(-total).start()

                def take(total=total):
                    b_got(total)
                    y_all(-total)

                when_a(-total, whole)
                when_b(-total, take)
        if n == 3:

            def last():
                came(2 * 144, w1zr.at[WAY[4]])
                came(2 * 144, w1zr.at[WAY[-4]])
                a_sib(4).start()

            def take4():
                b_got(4)
                y_all(4)

            when_a(4, last)
            when_b(4, take4)
            for core in range(2):
                on_core(core, lambda core=core: b_sib(core, 0).start())
        if n == 4:

            def arrived(core, count):
                for d in (1, 3, 2):
                    came(count * 144, yrecv.at[d - 1])
                    b_sib(core, 4 - d).start()

            on_core(0, lambda: arrived(0, 7))
            own_b = jnp.logical_or(zi == 1, zi == 2)

            @pl.when(jnp.logical_and(c == 1, own_b))
            def _():
                arrived(1, 3)

            @pl.when(jnp.logical_and(c == 1, jnp.logical_not(own_b)))
            def _():
                arrived(1, 4)
        if n == 5:
            on_core(0, lambda: came(24 * 144, brecv.at[0]))
            on_core(1, lambda: came(32 * 144, brecv.at[0]))

    def step_sent():
        def core0():
            gone(7 * 144, w1zs.at[0])
            gone(21 * 144, ysend.at[0])
            gone(32 * 144, bsend.at[0])

        on_core(0, core0)
        for k, (along_z, along_y) in enumerate(((19, 12), (4, 9), (16, 9), (3, 12))):

            @pl.when(jnp.logical_and(c == 1, zi == k))
            def _():
                gone(along_z * 144, w1zs.at[0])
                gone(along_y * 144, ysend.at[0])

        on_core(1, lambda: gone(24 * 144, bsend.at[0]))

    def wset(yy, cc):
        return w2.at[yy, :, cc, 0:96, :]

    def z2_send(origin, total):
        ref = blk(1, y, zz(origin), c)
        i = WAY[total]
        return rc(ref, ref, rsend.at[0], rrecv.at[i], dev(y, zz(origin + total), c))

    def z2_got(total):
        got(blk(1, y, zz(-total), c), rrecv.at[WAY[total]])

    def y2_send(d):
        ref = wset(y, c)
        return rc(ref, ref, ysend.at[1], yrecv.at[2 + d], dev(lax.rem(y + d, 4), z, c))

    def sib2_send(d):
        ref = wset(lax.rem(y + d, 4), c)
        return rc(ref, ref, bsend.at[1], brecv.at[1], dev(y, z, 1 - c))

    Z2 = ((0, 2), (0, -2), (0, 1), (0, -1), (-2, 4), (-2, 3), (2, -3))

    def step2(n):
        if n == 0:
            for origin, total in Z2[:4]:
                z2_send(origin, total).start()
        if n == 1:
            z2_got(2)
            z2_send(-2, 4).start()
            z2_send(-2, 3).start()
            z2_got(-2)
            z2_send(2, -3).start()
        if n == 2:
            for total in (1, -1, 3, -3, 4):
                z2_got(total)
            for d in (2, 1, 3):
                y2_send(d).start()
            sib2_send(0).start()
        if n == 3:
            for d in (1, 3, 2):
                got(wset(lax.rem(y + 4 - d, 4), c), yrecv.at[2 + d])
                sib2_send(4 - d).start()
        if n == 4:
            came(32 * 144, brecv.at[1])

    def step2_sent():
        gone(7 * 144, rsend.at[0])
        gone(24 * 144, ysend.at[1])
        gone(32 * 144, bsend.at[1])

    own1.wait()
    for e in (0, 1, 3, 2):
        src = lax.rem(y + e, 4)

        @pl.when(j != 7)
        def _():
            came(8 * 32 if e else 7 * 32, st1r.at[(4 - e) % 4])
            for dy in range(3):
                for m in range(8):
                    two = r1[src, m, 16 * (dy // 2):16 * (dy // 2) + 16].astype(F32)
                    stack[m * 6:m * 6 + 6, 0:128] = two[(dy % 2) * 8:(dy % 2) * 8 + 6]
                w1[c, zi, dy, src, h] = stack[:, 0:128].astype(BF16)

        first(e)
    @pl.when(x != y)
    def _():
        came(8 * 48, st2r.at[0])

    @pl.when(x == y)
    def _():
        own2().wait()
        came(7 * 48, st2r.at[0])

    for m in range(8):
        stack[m * 6:m * 6 + 6] = r2[m].astype(F32)[0:6]
    w2[y, zi, c, pl.ds(pl.multiple_of(48 * h, 16), 48), :] = stack[...].astype(BF16)
    step2(0)
    step(1)
    step(2)
    xstep(1)
    xstep(3)
    step2(1)
    step(3)
    xstep(2)
    step2(2)
    step(4)
    halo_wait()
    step(5)

    def conv1():
        rows = []
        for yy in range(2):
            rows.append(jnp.concatenate(
                [abuf[:, :, yy + dy].reshape(512, 384) for dy in range(3)], axis=1))
        lhs = jnp.concatenate(rows, axis=0)

        def tile(n, carry):
            rhs = jnp.concatenate(
                [w1[0, n].reshape(1152, 128), w1[1, n].reshape(1152, 128)], axis=1)
            res = jnp.dot(lhs, rhs, preferred_element_type=F32)
            for yy in range(2):
                pbuf[n, 2:10, yy] = res[yy * 512:yy * 512 + 512].reshape(8, 64, 256)
            return carry

        lax.fori_loop(0, 4, tile, 0)

    conv1()

    lane = lax.broadcasted_iota(jnp.int32, (64, 128), 1)
    row = lax.broadcasted_iota(jnp.int32, (64, 128), 0)

    def shift_down(v):
        return jnp.where(row > 0, pltpu.roll(v, 1, 0), 0.0)

    def shift_up(v):
        return jnp.where(row < 63, pltpu.roll(v, 63, 0), 0.0)

    def combine(f, carry):
        both = []
        for yy in range(2):
            def p(dt, n):
                return pbuf[n // 2, f + dt, yy, :, (n % 2) * 128:(n % 2) * 128 + 128]

            m1 = p(0, 0) + p(1, 3) + p(2, 6)
            a_lo = p(0, 0) + p(1, 3)
            mid = p(0, 1) + p(1, 4)
            b_hi = p(0, 2) + p(1, 5)
            m0 = pltpu.roll(jnp.where(lane >= 96, a_lo, mid), 32, 1) + pltpu.roll(p(2, 2), 96, 1)
            m2 = pltpu.roll(jnp.where(lane >= 64, mid, b_hi), 64, 1) + pltpu.roll(p(2, 5), 96, 1)
            hid = m1 + shift_down(m0) + shift_up(m2) + bias1
            hid = jnp.where(lane < 96, hid, 0.0)
            hbuf[f, yy] = hid
            both.append(hid * hid)
        sums = jnp.sum(jnp.transpose(jnp.concatenate(both, axis=0)), axis=0, keepdims=True)
        ssbuf[0, pl.ds(f, 1)] = sums
        return carry

    lax.fori_loop(0, 8, combine, 0, unroll=2)

    def ss_send(d):
        return rc(ssbuf.at[0], ssbuf.at[d], sss.at[0], ssr.at[0], (lax.rem(x + d, 4), t))

    for d in range(1, 4):
        ss_send(d).start()
    sizes = ssbuf.at[1:4]
    got(sizes, ssr.at[0])
    ssbuf[4] = (ssbuf[0] + ssbuf[1]) + (ssbuf[2] + ssbuf[3])

    def spread(f, where, v):
        a2s[0, f + 2, where] = shift_down(v).astype(BF16)
        a2s[1, f + 2, where] = v.astype(BF16)
        a2s[2, f + 2, where] = shift_up(v).astype(BF16)

    def act2(f, carry):
        ms = jnp.transpose(jnp.broadcast_to(ssbuf[4, pl.ds(f, 1)], (128, 128))) * (1.0 / 384.0)
        u = hbuf[f].reshape(128, 128) * lax.rsqrt(ms + 1e-6) * gain2
        v = silu(u)
        for yy in range(2):
            spread(f, 1 + yy, v[64 * yy:64 * yy + 64])
        return carry

    lax.fori_loop(0, 8, act2, 0, unroll=2)

    def h2up():
        return rc(a2s.at[1, 2:10, 1], a2h.at[1], h2s.at[0], h2r.at[0], (x, t - 1))

    def h2down():
        return rc(a2s.at[1, 2:10, 2], a2h.at[0], h2s.at[1], h2r.at[1], (x, t + 1))

    @pl.when(t > 0)
    def _():
        h2up().start()

    @pl.when(t < 63)
    def _():
        h2down().start()

    step2(3)
    step2(4)

    @pl.when(t > 0)
    def _():
        got(a2h.at[0], h2r.at[1])

    @pl.when(t == 0)
    def _():
        a2h[0] = jnp.zeros((8, 64, 128), BF16)

    @pl.when(t < 63)
    def _():
        got(a2h.at[1], h2r.at[0])

    @pl.when(t == 63)
    def _():
        a2h[1] = jnp.zeros((8, 64, 128), BF16)

    def halo2(f, carry):
        spread(f, 0, a2h[0, f].astype(F32))
        spread(f, 3, a2h[1, f].astype(F32))
        return carry

    lax.fori_loop(0, 8, halo2, 0)

    def conv2(q):
        acc = None
        for dt in range(3):
            lhs, rhs = [], []
            for dy in range(3):
                for dx in range(3):
                    tap = dt * 9 + dy * 3 + dx
                    lhs.append(a2s[dx, pl.ds(2 * q + dt, 2), dy:dy + 2].reshape(256, 128))
                    rhs.append(w2[tap // 8, (tap % 8) // 2, tap % 2])
            part = jnp.dot(
                jnp.concatenate(lhs, axis=1), jnp.concatenate(rhs, axis=0),
                preferred_element_type=F32,
            )
            acc = part if acc is None else acc + part
        return acc

    def out_send(d):
        return rc(sendb.at[d - 1], recvb.at[d - 1], fs.at[0], fr.at[d], (lax.rem(x + d, 4), t))

    for d in (2, 1, 3):
        sendb[d - 1] = conv2(lax.rem(x + d, 4)).astype(BF16).reshape(2, 2, 64, 384)
        out_send(d).start()
    mine = conv2(x) + bias2 + lat[...].reshape(256, 384).astype(F32)
    for d in (2, 1, 3):
        got(recvb.at[d - 1], fr.at[d])
        mine = mine + recvb[d - 1].reshape(256, 384).astype(F32)
    out[...] = mine.astype(BF16).reshape(2, 2, 64, 384)

    @pl.when(j == 7)
    def _():
        gone(28 * 32, st1s.at[0])

    @pl.when(j != 7)
    def _():
        gone(27 * 32, st1s.at[0])

    @pl.when(x != y)
    def _():
        gone(8 * 48, st2s.at[0])

    @pl.when(x == y)
    def _():
        gone(7 * 48, st2s.at[0])

    gone(3 * 768, xs.at[0])
    rc(ssbuf.at[1:4], ssbuf.at[1:4], sss.at[0], loc.at[2], (x, t)).wait_send()
    gone(3 * 768, fs.at[0])

    @pl.when(t > 0)
    def _():
        gone(4 * 384, ups.at[0])
        h2up().wait_send()

    @pl.when(t < 63)
    def _():
        gone(4 * 384, dns.at[0])
        h2down().wait_send()

    step2_sent()

    step_sent()


def per_device(latents, gain_first, conv_first, bias_first, gain_second, conv_second, bias_second):
    vm = pl.BlockSpec(memory_space=pltpu.VMEM)
    dma = pltpu.SemaphoreType.DMA
    return pl.pallas_call(
        kernel,
        out_shape=jax.ShapeDtypeStruct((2, 2, 64, 384), BF16),
        in_specs=[pl.BlockSpec(memory_space=pltpu.HBM)] * 7,
        out_specs=vm,
        scratch_shapes=[
            pltpu.VMEM((2, 2, 64, 384), BF16),
            pltpu.VMEM((4, 384), F32),
            pltpu.VMEM((27, 6, 384), BF16),
            pltpu.VMEM((27, 6, 384), BF16),
            pltpu.VMEM((8, 32, 128), BF16),
            pltpu.VMEM((8, 16, 384), BF16),
            pltpu.VMEM((48, 384), F32),
            pltpu.VMEM((4608, 128), BF16),
            pltpu.VMEM((4, 8, 32, 128), BF16),
            pltpu.VMEM((8, 16, 384), BF16),
            pltpu.VMEM((2, 4, 3, 4, 2, 48, 128), BF16),
            pltpu.VMEM((4, 4, 2, 128, 384), BF16),
            pltpu.VMEM((4, 2, 4, 64, 384), BF16),
            pltpu.VMEM((4, 10, 2, 64, 256), F32),
            pltpu.VMEM((8, 2, 64, 128), F32),
            pltpu.VMEM((5, 8, 128), F32),
            pltpu.VMEM((3, 10, 4, 64, 128), BF16),
            pltpu.VMEM((2, 8, 64, 128), BF16),
            pltpu.VMEM((3, 2, 2, 64, 384), BF16),
            pltpu.VMEM((3, 2, 2, 64, 384), BF16),
            dma((7,)), dma((1,)), dma((4,)), dma((1,)), dma((1,)), dma((3,)),
            dma((1,)), dma((17,)), dma((2,)), dma((6,)), dma((1,)), dma((9,)), dma((2,)), dma((2,)),
            dma((1,)), dma((4,)), dma((1,)), dma((1,)), dma((1,)), dma((1,)),
            dma((1,)), dma((1,)), dma((2,)), dma((2,)), dma((1,)), dma((4,)),
        ],
        compiler_params=pltpu.CompilerParams(
            collective_id=0, has_side_effects=True, vmem_limit_bytes=63 * 1024 * 1024
        ),
        cost_estimate=pl.CostEstimate(flops=4_000_000_000, bytes_accessed=8_000_000, transcendentals=400_000),
    )(
        latents, gain_first, bias_first, gain_second, bias_second,
        conv_first.reshape(27, 6, 384), conv_second.reshape(27, 6, 384),
    )


def solution(mesh):
    in_specs = (
        P("span", "tile", None, None),
        P(),
        P(None, None, None, "tile", None),
        P(),
        P(),
        P(None, None, None, "tile", None),
        P(),
    )
    out_specs = P("span", "tile", None, None)
    return jax.shard_map(
        per_device, mesh=mesh, in_specs=in_specs, out_specs=out_specs, check_vma=False
    )
```

```python
import jax
import jax.numpy as jnp
from jax import lax
from jax.experimental import pallas as pl
from jax.experimental.pallas import tpu as pltpu
from jax.sharding import PartitionSpec as P

MESH = pl.DeviceIdType.MESH
F32 = jnp.float32
BF16 = jnp.bfloat16

WHOLE = 1

SLOTS = ((0, 1), (0, 0), (0, 2), (2, 0), (1, 1), (1, 0), (1, 2), (2, 2), (2, 1))


def silu(u):
    return u / (1.0 + jnp.exp(-u))


def kernel(
    lat_hbm, gain1_hbm, bias1_hbm, gain2_hbm, bias2_hbm, k1_hbm, k2_hbm, out,
    lat, vec, k1, k2, s1, s2, stack,
    ruler, r1, r2, w1, w2, abuf, pbuf, hbuf, hedge, ssbuf, a2s, a2h, sendb, recvb,
    ins, st1s, st1r, st2s, st2r, loc,
    w1zs, w1zr, ysend, yrecv, rsend, rrecv, bsend, brecv,
    xs, xr, ups, upr, dns, dnr, sss, ssr, h2s, h2r, fs, fr,
):
    x = lax.axis_index("span")
    t = lax.axis_index("tile")
    c = lax.rem(t, 2)
    z = lax.rem(lax.div(t, 2), 8)
    y = lax.div(t, 16)
    zi = lax.rem(z, 4)
    h = lax.div(z, 4)
    j = lax.rem(t, 8)
    g = lax.div(t, 8)

    def dev(yy, zz, cc):
        return (x, yy * 16 + zz * 2 + cc)

    def rc(src, dst, ssem, rsem, device):
        return pltpu.make_async_remote_copy(
            src_ref=src, dst_ref=dst, send_sem=ssem, recv_sem=rsem,
            device_id=device, device_id_type=MESH,
        )

    def got(ref, rsem):
        rc(ref, ref, loc.at[2], rsem, (x, t)).wait_recv()

    def gone(rows, ssem):
        size = ruler.at[0:rows]
        rc(size, size, ssem, loc.at[2], (x, t)).wait_send()

    def came(rows, rsem):
        got(ruler.at[0:rows], rsem)

    loads = [
        pltpu.make_async_copy(k1_hbm, k1, ins.at[0]),
        pltpu.make_async_copy(lat_hbm, lat, ins.at[1]),
        pltpu.make_async_copy(k2_hbm, k2, ins.at[2]),
        pltpu.make_async_copy(gain1_hbm, vec.at[0], ins.at[3]),
        pltpu.make_async_copy(bias1_hbm, vec.at[1], ins.at[4]),
        pltpu.make_async_copy(gain2_hbm, vec.at[2], ins.at[5]),
        pltpu.make_async_copy(bias2_hbm, vec.at[3], ins.at[6]),
    ]
    for load in loads:
        load.start()

    barrier = pltpu.get_barrier_semaphore()

    def hail(device):
        pl.semaphore_signal(barrier, inc=1, device_id=device, device_id_type=MESH)

    for e in range(4):
        for d in range(8):
            if e or d:
                hail((x, lax.rem(y + e, 4) * 16 + h * 8 + lax.rem(j + d, 8)))

    @pl.when(x != y)
    def _():
        for d in range(8):
            hail((y, x * 16 + h * 8 + lax.rem(j + d, 8)))

    for d in range(1, 4):
        hail((lax.rem(x + d, 4), t))
    for d in (1, 2, 6, 7):
        hail(dev(y, lax.rem(z + d, 8), c))

    @pl.when(t > 0)
    def _():
        for d in range(4):
            hail((lax.rem(x + d, 4), t - 1))

    @pl.when(t < 63)
    def _():
        for d in range(4):
            hail((lax.rem(x + d, 4), t + 1))

    lane8 = lax.broadcasted_iota(jnp.int32, (8, 128), 1)
    turn = lax.rem(384 - 96 * x, 384)

    def mine96(v):
        return pltpu.roll(v, turn, 1)[:, 0:128]

    loads[0].wait()
    pad2 = jnp.zeros((2, 384), F32)
    tiles = []
    for dy in range(3):
        got_slots = []
        for dt, dx in SLOTS:
            got_slots.append(mine96(jnp.concatenate([k1[dt * 9 + dy * 3 + dx].astype(F32), pad2], axis=0)))

        def at(n, by):
            return pltpu.roll(got_slots[n], by, 1) if by else got_slots[n]

        row = [
            jnp.where(lane8 < 96, at(0, 0), at(1, 96)),
            jnp.where(lane8 < 64, at(1, 96), at(2, 64)),
            jnp.where(lane8 < 32, at(2, 64), at(3, 32)),
            jnp.where(lane8 < 96, at(4, 0), at(5, 96)),
            jnp.where(lane8 < 64, at(5, 96), at(6, 64)),
            jnp.where(lane8 < 32, at(6, 64), at(7, 32)),
            jnp.where(lane8 < 96, at(8, 0), 0.0),
            jnp.zeros((8, 128), F32),
        ]
        tiles.append(row)
    for n in range(8):
        s1[n, 0:16] = jnp.concatenate([tiles[0][n], tiles[1][n]], axis=0).astype(BF16)
        s1[n, 16:32] = jnp.concatenate([tiles[2][n], jnp.zeros((8, 128), F32)], axis=0).astype(BF16)
    loads[2].wait()
    for n in range(8):
        tap = jnp.minimum(8 * x + n, 26)
        s2[n] = jnp.concatenate([k2[tap].astype(F32), jnp.zeros((10, 384), F32)], axis=0).astype(BF16)
    for load in loads[3:]:
        load.wait()
    loads[1].wait()
    gain1 = vec[0:1]
    bias2 = vec[3:4]
    bias1 = jnp.where(lane8[0:1] < 96, mine96(jnp.broadcast_to(vec[1:2], (8, 384)))[0:1], 0.0)
    gain2 = jnp.where(lane8[0:1] < 96, mine96(jnp.broadcast_to(vec[2:3], (8, 384)))[0:1], 0.0)

    w1[1, 3] = jnp.zeros((3, 4, 2, 48, 128), BF16)
    w2[:, :, :, 96:128, :] = jnp.zeros((4, 4, 2, 32, 384), BF16)
    a2s[:, 0:2] = jnp.zeros((3, 2, 4, 64, 128), BF16)

    def zero_p(i, carry):
        pbuf[i, 0:2] = jnp.zeros((2, 2, 64, 256), F32)
        return carry

    lax.fori_loop(0, 4, zero_p, 0)

    def act1(i, carry):
        v = lat[i].reshape(128, 384).astype(F32)
        ms = jnp.mean(v * v, axis=-1, keepdims=True)
        u = v * lax.rsqrt(ms + 1e-6) * gain1
        abuf[x, i, 1:3] = silu(u).astype(BF16).reshape(2, 64, 384)
        return carry

    lax.fori_loop(0, 2, act1, 0)

    many = jnp.where(x != y, 8, 0) + jnp.where(t > 0, 4, 0) + jnp.where(t < 63, 4, 0) + 38
    pl.semaphore_wait(barrier, many)

    def st1(e, d):
        jj = lax.rem(j + d, 8)
        return rc(s1.at[jj], r1.at[y, j], st1s.at[0], st1r.at[e], (x, lax.rem(y + e, 4) * 16 + h * 8 + jj))

    def st2(d):
        jj = lax.rem(j + d, 8)
        return rc(s2.at[jj], r2.at[j], st2s.at[0], st2r.at[0], (y, x * 16 + h * 8 + jj))

    def own2():
        return pltpu.make_async_copy(s2.at[j], r2.at[j], loc.at[1])

    for e in (2, 1, 3):
        for k in range(WHOLE):
            st1(e, lax.rem(9 + 2 * k - j, 8)).start()
    for d in range(1, 8):

        @pl.when(lax.rem(j + d, 8) != 7)
        def _():
            st1(0, d).start()

    own1 = pltpu.make_async_copy(s1.at[j], r1.at[y, j], loc.at[0])
    own1.start()

    def xsend(d):
        return rc(
            abuf.at[x, :, 1:3], abuf.at[x, :, 1:3], xs.at[0], xr.at[d], (lax.rem(x + d, 4), t)
        )

    def up(src, d):
        return rc(abuf.at[src, :, 1], abuf.at[src, :, 3], ups.at[0], upr.at[0], (x, t - 1))

    def down(src, d):
        return rc(abuf.at[src, :, 2], abuf.at[src, :, 0], dns.at[0], dnr.at[0], (x, t + 1))

    def halo_send(d):
        src = lax.rem(x + 4 - d, 4)

        @pl.when(t > 0)
        def _():
            up(src, d).start()

        @pl.when(t < 63)
        def _():
            down(src, d).start()

    def xstep(d):
        src = lax.rem(x + 4 - d, 4)
        land = abuf.at[src, :, 1:3]
        got(land, xr.at[d])
        halo_send(d)

    def halo_wait():
        @pl.when(t > 0)
        def _():
            came(4 * 384, dnr.at[0])

        @pl.when(t < 63)
        def _():
            came(4 * 384, upr.at[0])

        @pl.when(t == 0)
        def _():
            abuf[:, :, 0] = jnp.zeros((4, 2, 64, 384), BF16)

        @pl.when(t == 63)
        def _():
            abuf[:, :, 3] = jnp.zeros((4, 2, 64, 384), BF16)

    for d in range(8):
        if d == 0:

            @pl.when(x != y)
            def _():
                st2(0).start()

            @pl.when(x == y)
            def _():
                own2().start()
        else:
            st2(d).start()
    for d in (2, 1, 3):
        xsend(d).start()
    halo_send(0)

    def blk(k, yy, zz, cc):
        if k == 0:
            return w1.at[cc, lax.rem(zz, 4), :, yy, lax.div(zz, 4)]
        return w2.at[yy, lax.rem(zz, 4), cc, pl.ds(pl.multiple_of(48 * lax.div(zz, 4), 16), 48), :]

    def zset(zz):
        return w1.at[1, lax.rem(zz, 4), :, :, lax.div(zz, 4)]

    def zz(s):
        return lax.rem(z + 8 + s, 8)

    WAY = {1: 0, -1: 1, 2: 2, -2: 3, 3: 4, -3: 5, 4: 6, -4: 7, 0: 8}
    AROUND = (2, -2, 1, -1)
    B_RELAYS = {2: ((-2, 4), (-2, 3)), -2: ((2, -3),)}

    def yy_of(e):
        return lax.rem(y + e, 4)

    def zi_of(origin):
        return lax.rem(z + 8 + origin, 4)

    def when_a(origin, f):
        @pl.when(jnp.logical_and(c == 1, zi_of(origin) < WHOLE))
        def _():
            f()

    def when_b(origin, f):
        k = zi_of(origin)

        @pl.when(jnp.logical_or(c == 0, jnp.logical_and(k >= WHOLE, k <= 2)))
        def _():
            f()

    def on_core(core, f):
        @pl.when(c == core)
        def _():
            f()

    def a_z(e, origin, total):
        ref = blk(0, yy_of(e), zz(origin), 1)
        i = WAY[total]
        k = 9 + 4 * (i - 2) + e if total in (2, -2) else i
        return rc(ref, ref, w1zs.at[0], w1zr.at[k], dev(y, zz(origin + total), 1))

    def a_got(e, total):
        got(blk(0, yy_of(e), zz(-total), 1), w1zr.at[9 + 4 * (WAY[total] - 2) + e])

    def a_relays(e, total):
        if total == 2:
            return ((-2, 3), (-2, 4)) if e < 2 else ((-2, 3),)
        return ((2, -3), (2, -4)) if e >= 2 else ((2, -3),)

    def a_sib(s):
        ref = zset(zz(s))
        return rc(ref, ref, bsend.at[0], brecv.at[0], dev(y, z, 0))

    def b_z(origin, total):
        ref = blk(0, y, zz(origin), c)
        i = WAY[total]
        return rc(ref, ref, w1zs.at[0], w1zr.at[i], dev(y, zz(origin + total), c))

    def b_got(total):
        got(blk(0, y, zz(-total), c), w1zr.at[WAY[total]])

    UP = (0, -2, 1, 3)

    def b_y(d, s):
        ref = blk(0, y, zz(s), c)
        return rc(ref, ref, ysend.at[0], yrecv.at[0, d - 1], dev(yy_of(d), z, c))

    def b_sib(core, d):
        yy = lax.rem(y + d, 4)
        ref = w1.at[0, :, :, yy] if core == 0 else w1.at[1, WHOLE:3, :, yy]
        return rc(ref, ref, bsend.at[0], brecv.at[0], dev(y, z, 1 - core))

    def y_all(origin):
        for d in (2, 1, 3):
            b_y(d, origin).start()

    def first(e):
        def send_a():
            for total in AROUND:
                a_z(e, 0, total).start()

        when_a(0, send_a)
        if e == 0:

            def send_b():
                for total in AROUND:
                    b_z(0, total).start()
                y_all(0)

            when_b(0, send_b)

    def step(n):
        if n == 1:
            for total in (2, -2):

                def relay(total=total):
                    for e in (0, 1, 3, 2):
                        a_got(e, total)
                        for origin, far in a_relays(e, total):
                            a_z(e, origin, far).start()
                    a_sib(-total).start()

                def take(total=total):
                    b_got(total)
                    for origin, far in B_RELAYS[total]:
                        b_z(origin, far).start()
                    y_all(-total)

                when_a(-total, relay)
                when_b(-total, take)
            when_a(0, lambda: a_sib(0).start())
        if n == 2 or n == 3:
            for total in ((1, -1) if n == 2 else (3, -3)):

                def whole(total=total):
                    came(4 * 144, w1zr.at[WAY[total]])
                    a_sib(-total).start()

                def take(total=total):
                    b_got(total)
                    y_all(-total)

                when_a(-total, whole)
                when_b(-total, take)
        if n == 3:

            def last():
                came(2 * 144, w1zr.at[WAY[4]])
                came(2 * 144, w1zr.at[WAY[-4]])
                a_sib(4).start()

            def take4():
                b_got(4)
                y_all(4)

            when_a(4, last)
            when_b(4, take4)
            on_core(0, lambda: b_sib(0, 0).start())
            if WHOLE < 3:
                on_core(1, lambda: b_sib(1, 0).start())
        if n == 4:

            def arrived(core, count):
                if count:
                    for d in (1, 3, 2):
                        came(count * 144, yrecv.at[0, d - 1])
                        b_sib(core, 4 - d).start()

            on_core(0, lambda: arrived(0, 8))
            on_core(1, lambda: arrived(1, 2 * (3 - WHOLE)))
        if n == 5:
            on_core(0, lambda: came(24 * 144, brecv.at[0]))
            on_core(1, lambda: came(32 * 144, brecv.at[0]))

    def step_sent():
        def core0():
            gone(7 * 144, w1zs.at[0])
            gone(24 * 144, ysend.at[0])
            gone(32 * 144, bsend.at[0])

        on_core(0, core0)
        def sends(k, whole, block):
            return 0 if k == 3 else whole if k < WHOLE else block

        for k in range(4):
            along_z = sends(k, 16, 4) + sends((k + 2) % 4, 12, 3)
            along_y = 6 * (3 - WHOLE)

            @pl.when(jnp.logical_and(c == 1, zi == k))
            def _():
                gone(along_z * 144, w1zs.at[0])
                if along_y:
                    gone(along_y * 144, ysend.at[0])

        on_core(1, lambda: gone(24 * 144, bsend.at[0]))

    def wset(yy, cc):
        return w2.at[yy, :, cc, 0:96, :]

    def z2_send(origin, total):
        ref = blk(1, y, zz(origin), c)
        i = WAY[total]
        return rc(ref, ref, rsend.at[0], rrecv.at[i], dev(y, zz(origin + total), c))

    def z2_got(total):
        got(blk(1, y, zz(-total), c), rrecv.at[WAY[total]])

    def y2_one(d, origin, step):
        ref = blk(1, yy_of(4 + origin), zz(step), c)
        k = 18 if origin else WAY[step] + 9 * (d // 2)
        return rc(ref, ref, ysend.at[1], yrecv.at[1, k], dev(yy_of(d), z, c))

    def y2_send(origin):
        for d in (1, 3):
            y2_one(d, 0, origin).start()

    def y2_relay(*steps):
        for k in steps:
            got(blk(1, yy_of(3), zz(k), c), yrecv.at[1, WAY[k]])
            if k in UP:
                y2_one(1, -1, k).start()
            got(blk(1, yy_of(1), zz(k), c), yrecv.at[1, WAY[k] + 9])
            if k not in UP:
                y2_one(3, 1, k).start()

    def sib2_send(d):
        ref = wset(lax.rem(y + d, 4), c)
        return rc(ref, ref, bsend.at[1], brecv.at[1], dev(y, z, 1 - c))

    Z2 = ((0, 2), (0, -2), (0, 1), (0, -1), (-2, 4), (-2, 3), (2, -3))

    def step2(n):
        if n == 0:
            for origin, total in Z2[:4]:
                z2_send(origin, total).start()
        if n == 1:
            z2_got(2)
            z2_send(-2, 4).start()
            z2_send(-2, 3).start()
            z2_got(-2)
            z2_send(2, -3).start()
        if n == 2:
            for origin in (0, 2, -2):
                y2_send(origin)
            for total, origin in ((1, -1), (-1, 1), (3, -3), (-3, 3), (4, 4)):
                z2_got(total)
                y2_send(origin)
            sib2_send(0).start()
        if n == 3:
            came(8 * 144, yrecv.at[1, 18])
            sib2_send(2).start()
        if n == 4:
            came(32 * 144, brecv.at[1])

    def step2_sent():
        gone(7 * 144, rsend.at[0])
        gone(24 * 144, ysend.at[1])
        gone(32 * 144, bsend.at[1])

    own1.wait()
    for e in (0, 1, 3, 2):
        src = lax.rem(y + e, 4)

        @pl.when(jnp.logical_and(c == 1, zi < WHOLE) if e else j != 7)
        def _():
            came(8 * 32 if e else 7 * 32, st1r.at[(4 - e) % 4])
            for dy in range(3):
                for m in range(8):
                    two = r1[src, m, 16 * (dy // 2):16 * (dy // 2) + 16].astype(F32)
                    stack[m * 6:m * 6 + 6, 0:128] = two[(dy % 2) * 8:(dy % 2) * 8 + 6]
                w1[c, zi, dy, src, h] = stack[:, 0:128].astype(BF16)

        first(e)
    step(1)
    @pl.when(x != y)
    def _():
        came(8 * 48, st2r.at[0])

    @pl.when(x == y)
    def _():
        own2().wait()
        came(7 * 48, st2r.at[0])

    for m in range(8):
        stack[m * 6:m * 6 + 6] = r2[m].astype(F32)[0:6]
    w2[y, zi, c, pl.ds(pl.multiple_of(48 * h, 16), 48), :] = stack[...].astype(BF16)
    step2(0)
    step(2)
    step2(1)
    xstep(1)
    xstep(3)
    step(3)
    xstep(2)
    step2(2)
    step(4)
    halo_wait()
    step(5)

    def conv1():
        rows = []
        for yy in range(2):
            rows.append(jnp.concatenate(
                [abuf[:, :, yy + dy].reshape(512, 384) for dy in range(3)], axis=1))
        lhs = jnp.concatenate(rows, axis=0)

        def tile(n, carry):
            rhs = jnp.concatenate(
                [w1[0, n].reshape(1152, 128), w1[1, n].reshape(1152, 128)], axis=1)
            res = jnp.dot(lhs, rhs, preferred_element_type=F32)
            for yy in range(2):
                pbuf[n, 2:10, yy] = res[yy * 512:yy * 512 + 512].reshape(8, 64, 256)
            return carry

        tile(0, 0)
        tile(1, 0)
        y2_relay(0, 2, -2)
        tile(2, 0)
        tile(3, 0)

    conv1()
    y2_relay(1, -1, 3, -3, 4)
    sib2_send(1).start()
    sib2_send(3).start()

    lane = lax.broadcasted_iota(jnp.int32, (64, 128), 1)
    row = lax.broadcasted_iota(jnp.int32, (64, 128), 0)

    def shift_down(v):
        return jnp.where(row > 0, pltpu.roll(v, 1, 0), 0.0)

    def shift_up(v):
        return jnp.where(row < 63, pltpu.roll(v, 63, 0), 0.0)

    def combine(f, carry):
        both = []
        for yy in range(2):
            def p(dt, n):
                return pbuf[n // 2, f + dt, yy, :, (n % 2) * 128:(n % 2) * 128 + 128]

            m1 = p(0, 0) + p(1, 3) + p(2, 6)
            a_lo = p(0, 0) + p(1, 3)
            mid = p(0, 1) + p(1, 4)
            b_hi = p(0, 2) + p(1, 5)
            m0 = pltpu.roll(jnp.where(lane >= 96, a_lo, mid), 32, 1) + pltpu.roll(p(2, 2), 96, 1)
            m2 = pltpu.roll(jnp.where(lane >= 64, mid, b_hi), 64, 1) + pltpu.roll(p(2, 5), 96, 1)
            hid = m1 + shift_down(m0) + shift_up(m2) + bias1
            hid = jnp.where(lane < 96, hid, 0.0)
            hbuf[f, yy] = hid
            hedge[f, yy] = hid.astype(BF16)
            both.append(hid * hid)
        sums = jnp.sum(jnp.transpose(jnp.concatenate(both, axis=0)), axis=0, keepdims=True)
        ssbuf[0, pl.ds(f, 1)] = sums
        return carry

    lax.fori_loop(0, 8, combine, 0, unroll=2)

    def ss_send(d):
        return rc(ssbuf.at[0], ssbuf.at[d], sss.at[0], ssr.at[0], (lax.rem(x + d, 4), t))

    def ss_up(d):
        return rc(ssbuf.at[0], ssbuf.at[8 + d], sss.at[1], ssr.at[2], (lax.rem(x + d, 4), t - 1))

    def ss_down(d):
        return rc(ssbuf.at[0], ssbuf.at[4 + d], sss.at[2], ssr.at[1], (lax.rem(x + d, 4), t + 1))

    def h2up():
        return rc(hedge.at[:, 0], a2h.at[1], h2s.at[0], h2r.at[0], (x, t - 1))

    def h2down():
        return rc(hedge.at[:, 1], a2h.at[0], h2s.at[1], h2r.at[1], (x, t + 1))

    for d in (2, 1, 3):
        ss_send(d).start()

    @pl.when(t > 0)
    def _():
        for d in (2, 1, 3, 0):
            ss_up(d).start()
        h2up().start()

    @pl.when(t < 63)
    def _():
        for d in (2, 1, 3, 0):
            ss_down(d).start()
        h2down().start()

    @pl.when(t == 0)
    def _():
        a2h[0] = jnp.zeros((8, 64, 128), BF16)
        ssbuf[4:8] = jnp.zeros((4, 8, 128), F32)

    @pl.when(t == 63)
    def _():
        a2h[1] = jnp.zeros((8, 64, 128), BF16)
        ssbuf[8:12] = jnp.zeros((4, 8, 128), F32)

    step2(3)
    sizes = ssbuf.at[1:4]
    got(sizes, ssr.at[0])
    ssbuf[12] = (ssbuf[0] + ssbuf[1]) + (ssbuf[2] + ssbuf[3])

    def spread(f, where, v):
        a2s[0, f + 2, where] = shift_down(v).astype(BF16)
        a2s[1, f + 2, where] = v.astype(BF16)
        a2s[2, f + 2, where] = shift_up(v).astype(BF16)

    def act2(f, carry):
        ms = jnp.transpose(jnp.broadcast_to(ssbuf[12, pl.ds(f, 1)], (128, 128))) * (1.0 / 384.0)
        u = hbuf[f].reshape(128, 128) * lax.rsqrt(ms + 1e-6) * gain2
        v = silu(u)
        for yy in range(2):
            spread(f, 1 + yy, v[64 * yy:64 * yy + 64])
        return carry

    lax.fori_loop(0, 8, act2, 0, unroll=2)

    @pl.when(t > 0)
    def _():
        got(ssbuf.at[4:8], ssr.at[1])
        got(a2h.at[0], h2r.at[1])

    @pl.when(t < 63)
    def _():
        got(ssbuf.at[8:12], ssr.at[2])
        got(a2h.at[1], h2r.at[0])

    above = (ssbuf[4] + ssbuf[5]) + (ssbuf[6] + ssbuf[7])
    below = (ssbuf[8] + ssbuf[9]) + (ssbuf[10] + ssbuf[11])
    ssbuf[13] = jnp.where(lane8 >= 64, above, below)

    def halo2(f, carry):
        ms = jnp.transpose(jnp.broadcast_to(ssbuf[13, pl.ds(f, 1)], (128, 128))) * (1.0 / 384.0)
        hv = jnp.concatenate([a2h[1, f], a2h[0, f]], axis=0).astype(F32)
        v = silu(hv * lax.rsqrt(ms + 1e-6) * gain2)
        spread(f, 0, v[64:128])
        spread(f, 3, v[0:64])
        return carry

    lax.fori_loop(0, 8, halo2, 0, unroll=2)
    step2(4)

    def conv2(q):
        acc = None
        for dt in range(3):
            lhs, rhs = [], []
            for dy in range(3):
                for dx in range(3):
                    tap = dt * 9 + dy * 3 + dx
                    lhs.append(a2s[dx, pl.ds(2 * q + dt, 2), dy:dy + 2].reshape(256, 128))
                    rhs.append(w2[tap // 8, (tap % 8) // 2, tap % 2])
            part = jnp.dot(
                jnp.concatenate(lhs, axis=1), jnp.concatenate(rhs, axis=0),
                preferred_element_type=F32,
            )
            acc = part if acc is None else acc + part
        return acc

    def out_send(d):
        return rc(sendb.at[d - 1], recvb.at[d - 1], fs.at[0], fr.at[d], (lax.rem(x + d, 4), t))

    for d in (2, 1, 3):
        sendb[d - 1] = conv2(lax.rem(x + d, 4)).astype(BF16).reshape(2, 2, 64, 384)
        out_send(d).start()
    mine = conv2(x) + bias2 + lat[...].reshape(256, 384).astype(F32)
    for d in (2, 1, 3):
        got(recvb.at[d - 1], fr.at[d])
        mine = mine + recvb[d - 1].reshape(256, 384).astype(F32)
    out[...] = mine.astype(BF16).reshape(2, 2, 64, 384)

    @pl.when(j == 7)
    def _():
        gone((7 + 3 * WHOLE) * 32, st1s.at[0])

    @pl.when(j != 7)
    def _():
        gone((6 + 3 * WHOLE) * 32, st1s.at[0])

    @pl.when(x != y)
    def _():
        gone(8 * 48, st2s.at[0])

    @pl.when(x == y)
    def _():
        gone(7 * 48, st2s.at[0])

    gone(3 * 768, xs.at[0])
    def ss_gone(count, i):
        size = ssbuf.at[0:count]
        rc(size, size, sss.at[i], loc.at[2], (x, t)).wait_send()

    ss_gone(3, 0)
    gone(3 * 768, fs.at[0])

    @pl.when(t > 0)
    def _():
        gone(4 * 384, ups.at[0])
        ss_gone(4, 1)
        h2up().wait_send()

    @pl.when(t < 63)
    def _():
        gone(4 * 384, dns.at[0])
        ss_gone(4, 2)
        h2down().wait_send()

    step2_sent()

    step_sent()


def per_device(latents, gain_first, conv_first, bias_first, gain_second, conv_second, bias_second):
    vm = pl.BlockSpec(memory_space=pltpu.VMEM)
    dma = pltpu.SemaphoreType.DMA
    return pl.pallas_call(
        kernel,
        out_shape=jax.ShapeDtypeStruct((2, 2, 64, 384), BF16),
        in_specs=[pl.BlockSpec(memory_space=pltpu.HBM)] * 7,
        out_specs=vm,
        scratch_shapes=[
            pltpu.VMEM((2, 2, 64, 384), BF16),
            pltpu.VMEM((4, 384), F32),
            pltpu.VMEM((27, 6, 384), BF16),
            pltpu.VMEM((27, 6, 384), BF16),
            pltpu.VMEM((8, 32, 128), BF16),
            pltpu.VMEM((8, 16, 384), BF16),
            pltpu.VMEM((48, 384), F32),
            pltpu.VMEM((4608, 128), BF16),
            pltpu.VMEM((4, 8, 32, 128), BF16),
            pltpu.VMEM((8, 16, 384), BF16),
            pltpu.VMEM((2, 4, 3, 4, 2, 48, 128), BF16),
            pltpu.VMEM((4, 4, 2, 128, 384), BF16),
            pltpu.VMEM((4, 2, 4, 64, 384), BF16),
            pltpu.VMEM((4, 10, 2, 64, 256), F32),
            pltpu.VMEM((8, 2, 64, 128), F32),
            pltpu.VMEM((8, 2, 64, 128), BF16),
            pltpu.VMEM((14, 8, 128), F32),
            pltpu.VMEM((3, 10, 4, 64, 128), BF16),
            pltpu.VMEM((2, 8, 64, 128), BF16),
            pltpu.VMEM((3, 2, 2, 64, 384), BF16),
            pltpu.VMEM((3, 2, 2, 64, 384), BF16),
            dma((7,)), dma((1,)), dma((4,)), dma((1,)), dma((1,)), dma((3,)),
            dma((1,)), dma((17,)), dma((2,)), dma((2, 19)), dma((1,)), dma((9,)), dma((2,)), dma((2,)),
            dma((1,)), dma((4,)), dma((1,)), dma((1,)), dma((1,)), dma((1,)),
            dma((3,)), dma((3,)), dma((2,)), dma((2,)), dma((1,)), dma((4,)),
        ],
        compiler_params=pltpu.CompilerParams(
            collective_id=0, has_side_effects=True, vmem_limit_bytes=63 * 1024 * 1024
        ),
        cost_estimate=pl.CostEstimate(flops=4_000_000_000, bytes_accessed=8_000_000, transcendentals=400_000),
    )(
        latents, gain_first, bias_first, gain_second, bias_second,
        conv_first.reshape(27, 6, 384), conv_second.reshape(27, 6, 384),
    )


def solution(mesh):
    in_specs = (
        P("span", "tile", None, None),
        P(),
        P(None, None, None, "tile", None),
        P(),
        P(),
        P(None, None, None, "tile", None),
        P(),
    )
    out_specs = P("span", "tile", None, None)
    return jax.shard_map(
        per_device, mesh=mesh, in_specs=in_specs, out_specs=out_specs, check_vma=False
    )
```

```python
import jax
import jax.numpy as jnp
from jax import lax
from jax.experimental import pallas as pl
from jax.experimental.pallas import tpu as pltpu
from jax.sharding import PartitionSpec as P

MESH = pl.DeviceIdType.MESH
F32 = jnp.float32
BF16 = jnp.bfloat16

WHOLE = 1

SLOTS = ((0, 1), (0, 0), (0, 2), (2, 0), (1, 1), (1, 0), (1, 2), (2, 2), (2, 1))


def silu(u):
    return u / (1.0 + jnp.exp(-u))


def kernel(
    lat_hbm, gain1_hbm, bias1_hbm, gain2_hbm, bias2_hbm, k1_hbm, k2_hbm, out,
    lat, vec, k1, k2, s1, s2, stack,
    ruler, r1, r2, w1, w2, abuf, pbuf, hbuf, hedge, ssbuf, a2s, a2h, sendb, recvb,
    ins, st1s, st1r, st2s, st2r, loc,
    w1zs, w1zr, ysend, yrecv, rsend, rrecv, bsend, brecv,
    xs, xr, ups, upr, dns, dnr, sss, ssr, h2s, h2r, fs, fr,
):
    x = lax.axis_index("span")
    t = lax.axis_index("tile")
    c = lax.rem(t, 2)
    z = lax.rem(lax.div(t, 2), 8)
    y = lax.div(t, 16)
    zi = lax.rem(z, 4)
    h = lax.div(z, 4)
    j = lax.rem(t, 8)
    g = lax.div(t, 8)

    def dev(yy, zz, cc):
        return (x, yy * 16 + zz * 2 + cc)

    def rc(src, dst, ssem, rsem, device):
        return pltpu.make_async_remote_copy(
            src_ref=src, dst_ref=dst, send_sem=ssem, recv_sem=rsem,
            device_id=device, device_id_type=MESH,
        )

    def got(ref, rsem):
        rc(ref, ref, loc.at[2], rsem, (x, t)).wait_recv()

    def gone(rows, ssem):
        size = ruler.at[0:rows]
        rc(size, size, ssem, loc.at[2], (x, t)).wait_send()

    def came(rows, rsem):
        got(ruler.at[0:rows], rsem)

    loads = [
        pltpu.make_async_copy(k1_hbm, k1, ins.at[0]),
        pltpu.make_async_copy(lat_hbm, lat, ins.at[1]),
        pltpu.make_async_copy(k2_hbm, k2, ins.at[2]),
        pltpu.make_async_copy(gain1_hbm, vec.at[0], ins.at[3]),
        pltpu.make_async_copy(bias1_hbm, vec.at[1], ins.at[4]),
        pltpu.make_async_copy(gain2_hbm, vec.at[2], ins.at[5]),
        pltpu.make_async_copy(bias2_hbm, vec.at[3], ins.at[6]),
    ]
    for load in loads:
        load.start()

    barrier = pltpu.get_barrier_semaphore()

    def hail(device):
        pl.semaphore_signal(barrier, inc=1, device_id=device, device_id_type=MESH)

    for e in range(4):
        for d in range(8):
            if e or d:
                hail((x, lax.rem(y + e, 4) * 16 + h * 8 + lax.rem(j + d, 8)))

    @pl.when(x != y)
    def _():
        for d in range(8):
            hail((y, x * 16 + h * 8 + lax.rem(j + d, 8)))

    for d in range(1, 4):
        hail((lax.rem(x + d, 4), t))
    for d in (1, 2, 6, 7):
        hail(dev(y, lax.rem(z + d, 8), c))

    @pl.when(t > 0)
    def _():
        for d in range(4):
            hail((lax.rem(x + d, 4), t - 1))

    @pl.when(t < 63)
    def _():
        for d in range(4):
            hail((lax.rem(x + d, 4), t + 1))

    lane8 = lax.broadcasted_iota(jnp.int32, (8, 128), 1)
    turn = lax.rem(384 - 96 * x, 384)

    def mine96(v):
        return pltpu.roll(v, turn, 1)[:, 0:128]

    loads[0].wait()
    pad2 = jnp.zeros((2, 384), F32)
    tiles = []
    for dy in range(3):
        got_slots = []
        for dt, dx in SLOTS:
            got_slots.append(mine96(jnp.concatenate([k1[dt * 9 + dy * 3 + dx].astype(F32), pad2], axis=0)))

        def at(n, by):
            return pltpu.roll(got_slots[n], by, 1) if by else got_slots[n]

        row = [
            jnp.where(lane8 < 96, at(0, 0), at(1, 96)),
            jnp.where(lane8 < 64, at(1, 96), at(2, 64)),
            jnp.where(lane8 < 32, at(2, 64), at(3, 32)),
            jnp.where(lane8 < 96, at(4, 0), at(5, 96)),
            jnp.where(lane8 < 64, at(5, 96), at(6, 64)),
            jnp.where(lane8 < 32, at(6, 64), at(7, 32)),
            jnp.where(lane8 < 96, at(8, 0), 0.0),
            jnp.zeros((8, 128), F32),
        ]
        tiles.append(row)
    for n in range(8):
        s1[n, 0:16] = jnp.concatenate([tiles[0][n], tiles[1][n]], axis=0).astype(BF16)
        s1[n, 16:32] = jnp.concatenate([tiles[2][n], jnp.zeros((8, 128), F32)], axis=0).astype(BF16)
    loads[2].wait()
    for n in range(8):
        tap = jnp.minimum(8 * x + n, 26)
        s2[n] = jnp.concatenate([k2[tap].astype(F32), jnp.zeros((10, 384), F32)], axis=0).astype(BF16)
    for load in loads[3:]:
        load.wait()
    loads[1].wait()
    gain1 = vec[0:1]
    bias2 = vec[3:4]
    bias1 = jnp.where(lane8[0:1] < 96, mine96(jnp.broadcast_to(vec[1:2], (8, 384)))[0:1], 0.0)
    gain2 = jnp.where(lane8[0:1] < 96, mine96(jnp.broadcast_to(vec[2:3], (8, 384)))[0:1], 0.0)

    w1[1, 3] = jnp.zeros((3, 4, 2, 48, 128), BF16)
    w2[:, :, :, 96:128, :] = jnp.zeros((4, 4, 2, 32, 384), BF16)
    a2s[:, 0:2] = jnp.zeros((3, 2, 4, 64, 128), BF16)

    def zero_p(i, carry):
        pbuf[i, 0:2] = jnp.zeros((2, 2, 64, 256), F32)
        return carry

    lax.fori_loop(0, 4, zero_p, 0)

    def act1(i, carry):
        v = lat[i].reshape(128, 384).astype(F32)
        ms = jnp.mean(v * v, axis=-1, keepdims=True)
        u = v * lax.rsqrt(ms + 1e-6) * gain1
        abuf[x, i, 1:3] = silu(u).astype(BF16).reshape(2, 64, 384)
        return carry

    lax.fori_loop(0, 2, act1, 0)

    many = jnp.where(x != y, 8, 0) + jnp.where(t > 0, 4, 0) + jnp.where(t < 63, 4, 0) + 38
    pl.semaphore_wait(barrier, many)

    def st1(e, d):
        jj = lax.rem(j + d, 8)
        return rc(s1.at[jj], r1.at[y, j], st1s.at[0], st1r.at[e], (x, lax.rem(y + e, 4) * 16 + h * 8 + jj))

    def st2(d):
        jj = lax.rem(j + d, 8)
        return rc(s2.at[jj], r2.at[j], st2s.at[0], st2r.at[0], (y, x * 16 + h * 8 + jj))

    def own2():
        return pltpu.make_async_copy(s2.at[j], r2.at[j], loc.at[1])

    for e in (2, 1, 3):
        for k in range(WHOLE):
            st1(e, lax.rem(9 + 2 * k - j, 8)).start()
    for d in range(1, 8):

        @pl.when(lax.rem(j + d, 8) != 7)
        def _():
            st1(0, d).start()

    own1 = pltpu.make_async_copy(s1.at[j], r1.at[y, j], loc.at[0])
    own1.start()

    def xsend(d):
        return rc(
            abuf.at[x, :, 1:3], abuf.at[x, :, 1:3], xs.at[0], xr.at[d], (lax.rem(x + d, 4), t)
        )

    def up(src, d):
        return rc(abuf.at[src, :, 1], abuf.at[src, :, 3], ups.at[0], upr.at[0], (x, t - 1))

    def down(src, d):
        return rc(abuf.at[src, :, 2], abuf.at[src, :, 0], dns.at[0], dnr.at[0], (x, t + 1))

    def halo_send(d):
        src = lax.rem(x + 4 - d, 4)

        @pl.when(t > 0)
        def _():
            up(src, d).start()

        @pl.when(t < 63)
        def _():
            down(src, d).start()

    def xstep(d):
        src = lax.rem(x + 4 - d, 4)
        land = abuf.at[src, :, 1:3]
        got(land, xr.at[d])
        halo_send(d)

    def halo_wait():
        @pl.when(t > 0)
        def _():
            came(4 * 384, dnr.at[0])

        @pl.when(t < 63)
        def _():
            came(4 * 384, upr.at[0])

        @pl.when(t == 0)
        def _():
            abuf[:, :, 0] = jnp.zeros((4, 2, 64, 384), BF16)

        @pl.when(t == 63)
        def _():
            abuf[:, :, 3] = jnp.zeros((4, 2, 64, 384), BF16)

    for d in range(8):
        if d == 0:

            @pl.when(x != y)
            def _():
                st2(0).start()

            @pl.when(x == y)
            def _():
                own2().start()
        else:
            st2(d).start()
    for d in (2, 1, 3):
        xsend(d).start()
    halo_send(0)

    def blk(k, yy, zz, cc):
        if k == 0:
            return w1.at[cc, lax.rem(zz, 4), :, yy, lax.div(zz, 4)]
        return w2.at[yy, lax.rem(zz, 4), cc, pl.ds(pl.multiple_of(48 * lax.div(zz, 4), 16), 48), :]

    def zset(zz):
        return w1.at[1, lax.rem(zz, 4), :, :, lax.div(zz, 4)]

    def zz(s):
        return lax.rem(z + 8 + s, 8)

    WAY = {1: 0, -1: 1, 2: 2, -2: 3, 3: 4, -3: 5, 4: 6, -4: 7, 0: 8}
    AROUND = (2, -2, 1, -1)
    B_RELAYS = {2: ((-2, 4), (-2, 3)), -2: ((2, -3),)}

    def yy_of(e):
        return lax.rem(y + e, 4)

    def zi_of(origin):
        return lax.rem(z + 8 + origin, 4)

    def when_a(origin, f):
        @pl.when(jnp.logical_and(c == 1, zi_of(origin) < WHOLE))
        def _():
            f()

    def when_b(origin, f):
        k = zi_of(origin)

        @pl.when(jnp.logical_or(c == 0, jnp.logical_and(k >= WHOLE, k <= 2)))
        def _():
            f()

    def on_core(core, f):
        @pl.when(c == core)
        def _():
            f()

    def a_z(e, origin, total):
        ref = blk(0, yy_of(e), zz(origin), 1)
        i = WAY[total]
        k = 9 + 4 * (i - 2) + e if total in (2, -2) else i
        return rc(ref, ref, w1zs.at[0], w1zr.at[k], dev(y, zz(origin + total), 1))

    def a_got(e, total):
        got(blk(0, yy_of(e), zz(-total), 1), w1zr.at[9 + 4 * (WAY[total] - 2) + e])

    def a_relays(e, total):
        if total == 2:
            return ((-2, 3), (-2, 4)) if e < 2 else ((-2, 3),)
        return ((2, -3), (2, -4)) if e >= 2 else ((2, -3),)

    def a_sib(s):
        ref = zset(zz(s))
        return rc(ref, ref, bsend.at[0], brecv.at[0], dev(y, z, 0))

    def b_z(origin, total):
        ref = blk(0, y, zz(origin), c)
        i = WAY[total]
        return rc(ref, ref, w1zs.at[0], w1zr.at[i], dev(y, zz(origin + total), c))

    def b_got(total):
        got(blk(0, y, zz(-total), c), w1zr.at[WAY[total]])

    UP = (0, -2, 1, 3)

    def b_y(d, s):
        ref = blk(0, y, zz(s), c)
        return rc(ref, ref, ysend.at[0], yrecv.at[5 + d - 1], dev(yy_of(d), z, c))

    def b_sib(core, d):
        yy = lax.rem(y + d, 4)
        ref = w1.at[0, :, :, yy] if core == 0 else w1.at[1, WHOLE:3, :, yy]
        return rc(ref, ref, bsend.at[0], brecv.at[0], dev(y, z, 1 - core))

    def y_all(origin):
        for d in (2, 1, 3):
            b_y(d, origin).start()

    def first(e):
        def send_a():
            for total in AROUND:
                a_z(e, 0, total).start()

        when_a(0, send_a)
        if e == 0:

            def send_b():
                for total in AROUND:
                    b_z(0, total).start()
                y_all(0)

            when_b(0, send_b)

    def step(n):
        if n == 1:
            for total in (2, -2):

                def relay(total=total):
                    for e in (0, 1, 3, 2):
                        a_got(e, total)
                        for origin, far in a_relays(e, total):
                            a_z(e, origin, far).start()
                    a_sib(-total).start()

                def take(total=total):
                    b_got(total)
                    for origin, far in B_RELAYS[total]:
                        b_z(origin, far).start()
                    y_all(-total)

                when_a(-total, relay)
                when_b(-total, take)
            when_a(0, lambda: a_sib(0).start())
        if n == 2 or n == 3:
            for total in ((1, -1) if n == 2 else (3, -3)):

                def whole(total=total):
                    came(4 * 144, w1zr.at[WAY[total]])
                    a_sib(-total).start()

                def take(total=total):
                    b_got(total)
                    y_all(-total)

                when_a(-total, whole)
                when_b(-total, take)
        if n == 3:

            def last():
                came(2 * 144, w1zr.at[WAY[4]])
                came(2 * 144, w1zr.at[WAY[-4]])
                a_sib(4).start()

            def take4():
                b_got(4)
                y_all(4)

            when_a(4, last)
            when_b(4, take4)
            on_core(0, lambda: b_sib(0, 0).start())
            if WHOLE < 3:
                on_core(1, lambda: b_sib(1, 0).start())
        if n == 4:

            def arrived(core, count):
                if count:
                    for d in (1, 3, 2):
                        came(count * 144, yrecv.at[5 + d - 1])
                        b_sib(core, 4 - d).start()

            on_core(0, lambda: arrived(0, 8))
            on_core(1, lambda: arrived(1, 2 * (3 - WHOLE)))
        if n == 5:
            on_core(0, lambda: came(24 * 144, brecv.at[0]))
            on_core(1, lambda: came(32 * 144, brecv.at[0]))

    def step_sent():
        def core0():
            gone(7 * 144, w1zs.at[0])
            gone(24 * 144, ysend.at[0])
            gone(32 * 144, bsend.at[0])

        on_core(0, core0)
        def sends(k, whole, block):
            return 0 if k == 3 else whole if k < WHOLE else block

        for k in range(4):
            along_z = sends(k, 16, 4) + sends((k + 2) % 4, 12, 3)
            along_y = 6 * (3 - WHOLE)

            @pl.when(jnp.logical_and(c == 1, zi == k))
            def _():
                gone(along_z * 144, w1zs.at[0])
                if along_y:
                    gone(along_y * 144, ysend.at[0])

        on_core(1, lambda: gone(24 * 144, bsend.at[0]))

    def wset(yy, cc):
        return w2.at[yy, :, cc, 0:96, :]

    def z2_send(origin, total):
        ref = blk(1, y, zz(origin), c)
        i = WAY[total]
        return rc(ref, ref, rsend.at[0], rrecv.at[i], dev(y, zz(origin + total), c))

    def z2_got(total):
        got(blk(1, y, zz(-total), c), rrecv.at[WAY[total]])

    EARLY = (0, 2, -2)
    LATE = (1, -1, 3, -3, 4)

    def y2_one(d, origin, step):
        ref = blk(1, yy_of(4 + origin), zz(step), 0)
        k = 4 if origin else 2 * (d // 2) + (step in LATE)
        return rc(ref, ref, ysend.at[1], yrecv.at[k], dev(yy_of(d), z, 0))

    def y2_send(origin):
        for d in (1, 3):
            y2_one(d, 0, origin).start()

    def y2_relay(group):
        steps = LATE if group else EARLY
        for k, (d, back) in enumerate(((1, -1), (3, 1))):
            came(len(steps) * 144, yrecv.at[2 * k + group])
            for step in steps:
                if (step in UP) == (d == 1):
                    y2_one(d, back, step).start()

    def sib2_send(d):
        ref = wset(lax.rem(y + d, 4), c)
        return rc(ref, ref, bsend.at[1], brecv.at[1], dev(y, z, 1 - c))

    Z2 = ((0, 2), (0, -2), (0, 1), (0, -1), (-2, 4), (-2, 3), (2, -3))

    def col(origin):
        zo = zz(origin)
        return w2.at[:, lax.rem(zo, 4), 1, pl.ds(pl.multiple_of(48 * lax.div(zo, 4), 16), 48), :]

    def y2_own(d):
        ref = blk(1, y, z, 1)
        return rc(ref, ref, ysend.at[1], yrecv.at[4], dev(yy_of(d), z, 1))

    def z2_col(e, origin, total):
        ref = blk(1, yy_of(e), zz(origin), 1)
        i = WAY[total]
        k = 9 + 4 * (i - 2) + e if total in (2, -2) else i
        return rc(ref, ref, rsend.at[0], rrecv.at[k], dev(y, zz(origin + total), 1))

    def col_sib(origin):
        ref = col(origin)
        return rc(ref, ref, bsend.at[1], brecv.at[1], dev(y, z, 0))

    def step2(n):
        def core0():
            if n == 0:
                for origin, total in Z2[:4]:
                    z2_send(origin, total).start()
            if n == 1:
                z2_got(2)
                z2_send(-2, 4).start()
                z2_send(-2, 3).start()
                z2_got(-2)
                z2_send(2, -3).start()
            if n == 2:
                for origin in EARLY:
                    y2_send(origin)
                for total, origin in ((1, -1), (-1, 1), (3, -3), (-3, 3), (4, 4)):
                    z2_got(total)
                    y2_send(origin)
                sib2_send(0).start()
            if n == 4:
                y2_relay(0)
            if n == 5:
                y2_relay(1)
                sib2_send(1).start()
                sib2_send(3).start()
            if n == 6:
                came(8 * 144, yrecv.at[4])
                sib2_send(2).start()

        def core1():
            if n == 0:
                for d in (2, 1, 3):
                    y2_own(d).start()
            if n == 1:
                came(3 * 144, yrecv.at[4])
                for e in (0, 1, 3, 2):
                    for total in AROUND:
                        z2_col(e, 0, total).start()
                col_sib(0).start()
            if n == 3:
                for total in (2, -2):
                    for e in (0, 1, 3, 2):
                        got(blk(1, yy_of(e), zz(-total), 1), rrecv.at[9 + 4 * (WAY[total] - 2) + e])
                        for origin, far in a_relays(e, total):
                            z2_col(e, origin, far).start()
                    col_sib(-total).start()
                for total in (1, -1):
                    came(4 * 144, rrecv.at[WAY[total]])
                    col_sib(-total).start()
            if n == 5:
                for total in (3, -3):
                    came(4 * 144, rrecv.at[WAY[total]])
                    col_sib(-total).start()
                came(2 * 144, rrecv.at[WAY[4]])
                came(2 * 144, rrecv.at[WAY[-4]])
                col_sib(4).start()

        on_core(0, core0)
        on_core(1, core1)
        if n == 7:
            came(32 * 144, brecv.at[1])

    def step2_sent():
        def core0():
            gone(7 * 144, rsend.at[0])
            gone(24 * 144, ysend.at[1])

        def core1():
            gone(28 * 144, rsend.at[0])
            gone(3 * 144, ysend.at[1])

        on_core(0, core0)
        on_core(1, core1)
        gone(32 * 144, bsend.at[1])

    own1.wait()
    for e in (0, 1, 3, 2):
        src = lax.rem(y + e, 4)

        @pl.when(jnp.logical_and(c == 1, zi < WHOLE) if e else j != 7)
        def _():
            came(8 * 32 if e else 7 * 32, st1r.at[(4 - e) % 4])
            for dy in range(3):
                for m in range(8):
                    two = r1[src, m, 16 * (dy // 2):16 * (dy // 2) + 16].astype(F32)
                    stack[m * 6:m * 6 + 6, 0:128] = two[(dy % 2) * 8:(dy % 2) * 8 + 6]
                w1[c, zi, dy, src, h] = stack[:, 0:128].astype(BF16)

        first(e)
    step(1)
    @pl.when(x != y)
    def _():
        came(8 * 48, st2r.at[0])

    @pl.when(x == y)
    def _():
        own2().wait()
        came(7 * 48, st2r.at[0])

    for m in range(8):
        stack[m * 6:m * 6 + 6] = r2[m].astype(F32)[0:6]
    w2[y, zi, c, pl.ds(pl.multiple_of(48 * h, 16), 48), :] = stack[...].astype(BF16)
    step2(0)
    step(2)
    xstep(1)
    xstep(3)
    step2(1)
    xstep(2)
    step(3)
    step2(2)
    step(4)
    step2(3)
    halo_wait()
    step(5)

    def conv1():
        rows = []
        for yy in range(2):
            rows.append(jnp.concatenate(
                [abuf[:, :, yy + dy].reshape(512, 384) for dy in range(3)], axis=1))
        lhs = jnp.concatenate(rows, axis=0)

        def tile(n, carry):
            rhs = jnp.concatenate(
                [w1[0, n].reshape(1152, 128), w1[1, n].reshape(1152, 128)], axis=1)
            res = jnp.dot(lhs, rhs, preferred_element_type=F32)
            for yy in range(2):
                pbuf[n, 2:10, yy] = res[yy * 512:yy * 512 + 512].reshape(8, 64, 256)
            return carry

        tile(0, 0)
        tile(1, 0)
        step2(4)
        tile(2, 0)
        tile(3, 0)

    conv1()
    step2(5)

    lane = lax.broadcasted_iota(jnp.int32, (64, 128), 1)
    row = lax.broadcasted_iota(jnp.int32, (64, 128), 0)

    def shift_down(v):
        return jnp.where(row > 0, pltpu.roll(v, 1, 0), 0.0)

    def shift_up(v):
        return jnp.where(row < 63, pltpu.roll(v, 63, 0), 0.0)

    def combine(f, carry):
        both = []
        for yy in range(2):
            def p(dt, n):
                return pbuf[n // 2, f + dt, yy, :, (n % 2) * 128:(n % 2) * 128 + 128]

            m1 = p(0, 0) + p(1, 3) + p(2, 6)
            a_lo = p(0, 0) + p(1, 3)
            mid = p(0, 1) + p(1, 4)
            b_hi = p(0, 2) + p(1, 5)
            m0 = pltpu.roll(jnp.where(lane >= 96, a_lo, mid), 32, 1) + pltpu.roll(p(2, 2), 96, 1)
            m2 = pltpu.roll(jnp.where(lane >= 64, mid, b_hi), 64, 1) + pltpu.roll(p(2, 5), 96, 1)
            hid = m1 + shift_down(m0) + shift_up(m2) + bias1
            hid = jnp.where(lane < 96, hid, 0.0)
            hbuf[f, yy] = hid
            hedge[f, yy] = hid.astype(BF16)
            both.append(hid * hid)
        sums = jnp.sum(jnp.transpose(jnp.concatenate(both, axis=0)), axis=0, keepdims=True)
        ssbuf[0, pl.ds(f, 1)] = sums
        return carry

    lax.fori_loop(0, 8, combine, 0, unroll=2)

    def ss_send(d):
        return rc(ssbuf.at[0], ssbuf.at[d], sss.at[0], ssr.at[0], (lax.rem(x + d, 4), t))

    def ss_up(d):
        return rc(ssbuf.at[0], ssbuf.at[8 + d], sss.at[1], ssr.at[2], (lax.rem(x + d, 4), t - 1))

    def ss_down(d):
        return rc(ssbuf.at[0], ssbuf.at[4 + d], sss.at[2], ssr.at[1], (lax.rem(x + d, 4), t + 1))

    def h2up():
        return rc(hedge.at[:, 0], a2h.at[1], h2s.at[0], h2r.at[0], (x, t - 1))

    def h2down():
        return rc(hedge.at[:, 1], a2h.at[0], h2s.at[1], h2r.at[1], (x, t + 1))

    for d in (2, 1, 3):
        ss_send(d).start()

    @pl.when(t > 0)
    def _():
        for d in (2, 1, 3, 0):
            ss_up(d).start()
        h2up().start()

    @pl.when(t < 63)
    def _():
        for d in (2, 1, 3, 0):
            ss_down(d).start()
        h2down().start()

    @pl.when(t == 0)
    def _():
        a2h[0] = jnp.zeros((8, 64, 128), BF16)
        ssbuf[4:8] = jnp.zeros((4, 8, 128), F32)

    @pl.when(t == 63)
    def _():
        a2h[1] = jnp.zeros((8, 64, 128), BF16)
        ssbuf[8:12] = jnp.zeros((4, 8, 128), F32)

    step2(6)
    sizes = ssbuf.at[1:4]
    got(sizes, ssr.at[0])
    ssbuf[12] = (ssbuf[0] + ssbuf[1]) + (ssbuf[2] + ssbuf[3])

    def spread(f, where, v):
        a2s[0, f + 2, where] = shift_down(v).astype(BF16)
        a2s[1, f + 2, where] = v.astype(BF16)
        a2s[2, f + 2, where] = shift_up(v).astype(BF16)

    def act2(f, carry):
        ms = jnp.transpose(jnp.broadcast_to(ssbuf[12, pl.ds(f, 1)], (128, 128))) * (1.0 / 384.0)
        u = hbuf[f].reshape(128, 128) * lax.rsqrt(ms + 1e-6) * gain2
        v = silu(u)
        for yy in range(2):
            spread(f, 1 + yy, v[64 * yy:64 * yy + 64])
        return carry

    lax.fori_loop(0, 8, act2, 0, unroll=2)

    @pl.when(t > 0)
    def _():
        got(ssbuf.at[4:8], ssr.at[1])
        got(a2h.at[0], h2r.at[1])

    @pl.when(t < 63)
    def _():
        got(ssbuf.at[8:12], ssr.at[2])
        got(a2h.at[1], h2r.at[0])

    above = (ssbuf[4] + ssbuf[5]) + (ssbuf[6] + ssbuf[7])
    below = (ssbuf[8] + ssbuf[9]) + (ssbuf[10] + ssbuf[11])
    ssbuf[13] = jnp.where(lane8 >= 64, above, below)

    def halo2(f, carry):
        ms = jnp.transpose(jnp.broadcast_to(ssbuf[13, pl.ds(f, 1)], (128, 128))) * (1.0 / 384.0)
        hv = jnp.concatenate([a2h[1, f], a2h[0, f]], axis=0).astype(F32)
        v = silu(hv * lax.rsqrt(ms + 1e-6) * gain2)
        spread(f, 0, v[64:128])
        spread(f, 3, v[0:64])
        return carry

    lax.fori_loop(0, 8, halo2, 0, unroll=2)
    step2(7)

    def conv2(q):
        acc = None
        for dt in range(3):
            lhs, rhs = [], []
            for dy in range(3):
                for dx in range(3):
                    tap = dt * 9 + dy * 3 + dx
                    lhs.append(a2s[dx, pl.ds(2 * q + dt, 2), dy:dy + 2].reshape(256, 128))
                    rhs.append(w2[tap // 8, (tap % 8) // 2, tap % 2])
            part = jnp.dot(
                jnp.concatenate(lhs, axis=1), jnp.concatenate(rhs, axis=0),
                preferred_element_type=F32,
            )
            acc = part if acc is None else acc + part
        return acc

    def out_send(d):
        return rc(sendb.at[d - 1], recvb.at[d - 1], fs.at[0], fr.at[d], (lax.rem(x + d, 4), t))

    for d in (2, 1, 3):
        sendb[d - 1] = conv2(lax.rem(x + d, 4)).astype(BF16).reshape(2, 2, 64, 384)
        out_send(d).start()
    mine = conv2(x) + bias2 + lat[...].reshape(256, 384).astype(F32)
    for d in (2, 1, 3):
        got(recvb.at[d - 1], fr.at[d])
        mine = mine + recvb[d - 1].reshape(256, 384).astype(F32)
    out[...] = mine.astype(BF16).reshape(2, 2, 64, 384)

    @pl.when(j == 7)
    def _():
        gone((7 + 3 * WHOLE) * 32, st1s.at[0])

    @pl.when(j != 7)
    def _():
        gone((6 + 3 * WHOLE) * 32, st1s.at[0])

    @pl.when(x != y)
    def _():
        gone(8 * 48, st2s.at[0])

    @pl.when(x == y)
    def _():
        gone(7 * 48, st2s.at[0])

    gone(3 * 768, xs.at[0])
    def ss_gone(count, i):
        size = ssbuf.at[0:count]
        rc(size, size, sss.at[i], loc.at[2], (x, t)).wait_send()

    ss_gone(3, 0)
    gone(3 * 768, fs.at[0])

    @pl.when(t > 0)
    def _():
        gone(4 * 384, ups.at[0])
        ss_gone(4, 1)
        h2up().wait_send()

    @pl.when(t < 63)
    def _():
        gone(4 * 384, dns.at[0])
        ss_gone(4, 2)
        h2down().wait_send()

    step2_sent()

    step_sent()


def per_device(latents, gain_first, conv_first, bias_first, gain_second, conv_second, bias_second):
    vm = pl.BlockSpec(memory_space=pltpu.VMEM)
    dma = pltpu.SemaphoreType.DMA
    return pl.pallas_call(
        kernel,
        out_shape=jax.ShapeDtypeStruct((2, 2, 64, 384), BF16),
        in_specs=[pl.BlockSpec(memory_space=pltpu.HBM)] * 7,
        out_specs=vm,
        scratch_shapes=[
            pltpu.VMEM((2, 2, 64, 384), BF16),
            pltpu.VMEM((4, 384), F32),
            pltpu.VMEM((27, 6, 384), BF16),
            pltpu.VMEM((27, 6, 384), BF16),
            pltpu.VMEM((8, 32, 128), BF16),
            pltpu.VMEM((8, 16, 384), BF16),
            pltpu.VMEM((48, 384), F32),
            pltpu.VMEM((4608, 128), BF16),
            pltpu.VMEM((4, 8, 32, 128), BF16),
            pltpu.VMEM((8, 16, 384), BF16),
            pltpu.VMEM((2, 4, 3, 4, 2, 48, 128), BF16),
            pltpu.VMEM((4, 4, 2, 128, 384), BF16),
            pltpu.VMEM((4, 2, 4, 64, 384), BF16),
            pltpu.VMEM((4, 10, 2, 64, 256), F32),
            pltpu.VMEM((8, 2, 64, 128), F32),
            pltpu.VMEM((8, 2, 64, 128), BF16),
            pltpu.VMEM((14, 8, 128), F32),
            pltpu.VMEM((3, 10, 4, 64, 128), BF16),
            pltpu.VMEM((2, 8, 64, 128), BF16),
            pltpu.VMEM((3, 2, 2, 64, 384), BF16),
            pltpu.VMEM((3, 2, 2, 64, 384), BF16),
            dma((7,)), dma((1,)), dma((4,)), dma((1,)), dma((1,)), dma((3,)),
            dma((1,)), dma((17,)), dma((2,)), dma((8,)), dma((1,)), dma((17,)), dma((2,)), dma((2,)),
            dma((1,)), dma((4,)), dma((1,)), dma((1,)), dma((1,)), dma((1,)),
            dma((3,)), dma((3,)), dma((2,)), dma((2,)), dma((1,)), dma((4,)),
        ],
        compiler_params=pltpu.CompilerParams(
            collective_id=0, has_side_effects=True, vmem_limit_bytes=63 * 1024 * 1024
        ),
        cost_estimate=pl.CostEstimate(flops=4_000_000_000, bytes_accessed=8_000_000, transcendentals=400_000),
    )(
        latents, gain_first, bias_first, gain_second, bias_second,
        conv_first.reshape(27, 6, 384), conv_second.reshape(27, 6, 384),
    )


def solution(mesh):
    in_specs = (
        P("span", "tile", None, None),
        P(),
        P(None, None, None, "tile", None),
        P(),
        P(),
        P(None, None, None, "tile", None),
        P(),
    )
    out_specs = P("span", "tile", None, None)
    return jax.shard_map(
        per_device, mesh=mesh, in_specs=in_specs, out_specs=out_specs, check_vma=False
    )
```

```python
import jax
import jax.numpy as jnp
from jax import lax
from jax.experimental import pallas as pl
from jax.experimental.pallas import tpu as pltpu
from jax.sharding import PartitionSpec as P

MESH = pl.DeviceIdType.MESH
F32 = jnp.float32
BF16 = jnp.bfloat16

SLOTS = ((0, 1), (0, 0), (0, 2), (2, 0), (1, 1), (1, 0), (1, 2), (2, 2), (2, 1))


def silu(u):
    return u / (1.0 + jnp.exp(-u))


def kernel(
    lat_hbm, gain1_hbm, bias1_hbm, gain2_hbm, bias2_hbm, k1_hbm, k2_hbm, out,
    lat, vec, k1, k2, s1, s2, stack,
    ruler, r1, r2, w1, w2, abuf, pbuf, hbuf, hedge, ssbuf, a2s, a2h, sendb, recvb,
    ins, st1s, st1r, st2s, st2r, loc,
    w1zs, w1zr, ysend, yrecv, rsend, rrecv, bsend, brecv,
    xs, xr, ups, upr, dns, dnr, sss, ssr, h2s, h2r, fs, fr,
):
    x = lax.axis_index("span")
    t = lax.axis_index("tile")
    c = lax.rem(t, 2)
    z = lax.rem(lax.div(t, 2), 8)
    y = lax.div(t, 16)
    zi = lax.rem(z, 4)
    h = lax.div(z, 4)
    j = lax.rem(t, 8)
    g = lax.div(t, 8)

    def dev(yy, zz, cc):
        return (x, yy * 16 + zz * 2 + cc)

    def rc(src, dst, ssem, rsem, device):
        return pltpu.make_async_remote_copy(
            src_ref=src, dst_ref=dst, send_sem=ssem, recv_sem=rsem,
            device_id=device, device_id_type=MESH,
        )

    def got(ref, rsem):
        rc(ref, ref, loc.at[2], rsem, (x, t)).wait_recv()

    def gone(rows, ssem):
        size = ruler.at[0:rows]
        rc(size, size, ssem, loc.at[2], (x, t)).wait_send()

    def came(rows, rsem):
        got(ruler.at[0:rows], rsem)

    loads = [
        pltpu.make_async_copy(k1_hbm, k1, ins.at[0]),
        pltpu.make_async_copy(lat_hbm, lat, ins.at[1]),
        pltpu.make_async_copy(k2_hbm, k2, ins.at[2]),
        pltpu.make_async_copy(gain1_hbm, vec.at[0], ins.at[3]),
        pltpu.make_async_copy(bias1_hbm, vec.at[1], ins.at[4]),
        pltpu.make_async_copy(gain2_hbm, vec.at[2], ins.at[5]),
        pltpu.make_async_copy(bias2_hbm, vec.at[3], ins.at[6]),
    ]
    for load in loads:
        load.start()

    barrier = pltpu.get_barrier_semaphore()

    def hail(device):
        pl.semaphore_signal(barrier, inc=1, device_id=device, device_id_type=MESH)

    for d in range(1, 8):
        hail((x, g * 8 + lax.rem(j + d, 8)))
    for d in range(1, 4):
        hail(dev(lax.rem(y + d, 4), z, c))

    @pl.when(x != y)
    def _():
        for d in range(8):
            hail((y, x * 16 + h * 8 + lax.rem(j + d, 8)))

    for d in range(1, 4):
        hail((lax.rem(x + d, 4), t))
    for d in (1, 2, 6, 7):
        hail(dev(y, lax.rem(z + d, 8), c))

    @pl.when(t > 0)
    def _():
        for d in range(4):
            hail((lax.rem(x + d, 4), t - 1))

    @pl.when(t < 63)
    def _():
        for d in range(4):
            hail((lax.rem(x + d, 4), t + 1))

    lane8 = lax.broadcasted_iota(jnp.int32, (8, 128), 1)
    turn = lax.rem(384 - 96 * x, 384)

    def mine96(v):
        return pltpu.roll(v, turn, 1)[:, 0:128]

    loads[0].wait()
    pad2 = jnp.zeros((2, 384), F32)
    tiles = []
    for dy in range(3):
        got_slots = []
        for dt, dx in SLOTS:
            got_slots.append(mine96(jnp.concatenate([k1[dt * 9 + dy * 3 + dx].astype(F32), pad2], axis=0)))

        def at(n, by):
            return pltpu.roll(got_slots[n], by, 1) if by else got_slots[n]

        row = [
            jnp.where(lane8 < 96, at(0, 0), at(1, 96)),
            jnp.where(lane8 < 64, at(1, 96), at(2, 64)),
            jnp.where(lane8 < 32, at(2, 64), at(3, 32)),
            jnp.where(lane8 < 96, at(4, 0), at(5, 96)),
            jnp.where(lane8 < 64, at(5, 96), at(6, 64)),
            jnp.where(lane8 < 32, at(6, 64), at(7, 32)),
            jnp.where(lane8 < 96, at(8, 0), 0.0),
            jnp.zeros((8, 128), F32),
        ]
        tiles.append(row)
    for n in range(8):
        s1[n, 0:16] = jnp.concatenate([tiles[0][n], tiles[1][n]], axis=0).astype(BF16)
        s1[n, 16:32] = jnp.concatenate([tiles[2][n], jnp.zeros((8, 128), F32)], axis=0).astype(BF16)
    loads[2].wait()
    for n in range(8):
        tap = jnp.minimum(8 * x + n, 26)
        s2[n] = jnp.concatenate([k2[tap].astype(F32), jnp.zeros((10, 384), F32)], axis=0).astype(BF16)
    for load in loads[3:]:
        load.wait()
    loads[1].wait()
    gain1 = vec[0:1]
    bias2 = vec[3:4]
    bias1 = jnp.where(lane8[0:1] < 96, mine96(jnp.broadcast_to(vec[1:2], (8, 384)))[0:1], 0.0)
    gain2 = jnp.where(lane8[0:1] < 96, mine96(jnp.broadcast_to(vec[2:3], (8, 384)))[0:1], 0.0)

    w1[1, 3] = jnp.zeros((3, 4, 2, 48, 128), BF16)
    w2[:, :, :, 96:128, :] = jnp.zeros((4, 4, 2, 32, 384), BF16)
    a2s[:, 0:2] = jnp.zeros((3, 2, 4, 64, 128), BF16)

    def zero_p(i, carry):
        pbuf[i, 0:2] = jnp.zeros((2, 2, 64, 256), F32)
        return carry

    lax.fori_loop(0, 4, zero_p, 0)

    def act1(i, carry):
        v = lat[i].reshape(128, 384).astype(F32)
        ms = jnp.mean(v * v, axis=-1, keepdims=True)
        u = v * lax.rsqrt(ms + 1e-6) * gain1
        abuf[x, i, 1:3] = silu(u).astype(BF16).reshape(2, 64, 384)
        return carry

    lax.fori_loop(0, 2, act1, 0)

    many = jnp.where(x != y, 8, 0) + jnp.where(t > 0, 4, 0) + jnp.where(t < 63, 4, 0) + 17
    pl.semaphore_wait(barrier, many)

    def st1(d):
        jj = lax.rem(j + d, 8)
        return rc(s1.at[jj], r1.at[j], st1s.at[0], st1r.at[0], (x, g * 8 + jj))

    def st2(d):
        jj = lax.rem(j + d, 8)
        return rc(s2.at[jj], r2.at[j], st2s.at[0], st2r.at[0], (y, x * 16 + h * 8 + jj))

    def own2():
        return pltpu.make_async_copy(s2.at[j], r2.at[j], loc.at[1])

    for d in range(1, 8):

        @pl.when(lax.rem(j + d, 8) != 7)
        def _():
            st1(d).start()

    own1 = pltpu.make_async_copy(s1.at[j], r1.at[j], loc.at[0])
    own1.start()

    def xsend(d):
        return rc(
            abuf.at[x, :, 1:3], abuf.at[x, :, 1:3], xs.at[0], xr.at[d], (lax.rem(x + d, 4), t)
        )

    def up(src, d):
        return rc(abuf.at[src, :, 1], abuf.at[src, :, 3], ups.at[0], upr.at[0], (x, t - 1))

    def down(src, d):
        return rc(abuf.at[src, :, 2], abuf.at[src, :, 0], dns.at[0], dnr.at[0], (x, t + 1))

    def halo_send(d):
        src = lax.rem(x + 4 - d, 4)

        @pl.when(t > 0)
        def _():
            up(src, d).start()

        @pl.when(t < 63)
        def _():
            down(src, d).start()

    def xstep(d):
        src = lax.rem(x + 4 - d, 4)
        land = abuf.at[src, :, 1:3]
        got(land, xr.at[d])
        halo_send(d)

    def halo_wait():
        @pl.when(t > 0)
        def _():
            came(4 * 384, dnr.at[0])

        @pl.when(t < 63)
        def _():
            came(4 * 384, upr.at[0])

        @pl.when(t == 0)
        def _():
            abuf[:, :, 0] = jnp.zeros((4, 2, 64, 384), BF16)

        @pl.when(t == 63)
        def _():
            abuf[:, :, 3] = jnp.zeros((4, 2, 64, 384), BF16)

    for d in range(8):
        if d == 0:

            @pl.when(x != y)
            def _():
                st2(0).start()

            @pl.when(x == y)
            def _():
                own2().start()
        else:
            st2(d).start()
    for d in (2, 1, 3):
        xsend(d).start()
    halo_send(0)

    def blk(k, yy, zz, cc):
        if k == 0:
            return w1.at[cc, lax.rem(zz, 4), :, yy, lax.div(zz, 4)]
        return w2.at[yy, lax.rem(zz, 4), cc, pl.ds(pl.multiple_of(48 * lax.div(zz, 4), 16), 48), :]

    def zset(zz):
        return w1.at[1, lax.rem(zz, 4), :, :, lax.div(zz, 4)]

    def zz(s):
        return lax.rem(z + 8 + s, 8)

    WAY = {1: 0, -1: 1, 2: 2, -2: 3, 3: 4, -3: 5, 4: 6, -4: 7, 0: 8}
    AROUND = (2, -2, 1, -1)
    B_RELAYS = {2: ((-2, 4), (-2, 3)), -2: ((2, -3),)}

    def yy_of(e):
        return lax.rem(y + e, 4)

    def zi_of(origin):
        return lax.rem(z + 8 + origin, 4)

    def when_b(origin, f):
        k = zi_of(origin)

        @pl.when(jnp.logical_or(c == 0, k <= 2))
        def _():
            f()

    def on_core(core, f):
        @pl.when(c == core)
        def _():
            f()

    def a_relays(e, total):
        if total == 2:
            return ((-2, 3), (-2, 4)) if e < 2 else ((-2, 3),)
        return ((2, -3), (2, -4)) if e >= 2 else ((2, -3),)

    def b_z(origin, total):
        ref = blk(0, y, zz(origin), c)
        i = WAY[total]
        return rc(ref, ref, w1zs.at[0], w1zr.at[i], dev(y, zz(origin + total), c))

    def b_got(total):
        got(blk(0, y, zz(-total), c), w1zr.at[WAY[total]])

    UP = (0, -2, 1, 3)

    def b_y(d, s):
        ref = blk(0, y, zz(s), c)
        return rc(ref, ref, ysend.at[0], yrecv.at[5 + d - 1], dev(yy_of(d), z, c))

    def b_sib(core, d):
        yy = lax.rem(y + d, 4)
        ref = w1.at[0, :, :, yy] if core == 0 else w1.at[1, 0:3, :, yy]
        return rc(ref, ref, bsend.at[0], brecv.at[0], dev(y, z, 1 - core))

    def y_all(origin):
        for d in (2, 1, 3):
            b_y(d, origin).start()

    def first():
        def send():
            for total in AROUND:
                b_z(0, total).start()
            y_all(0)

        when_b(0, send)

    def step(n):
        if n == 1:
            for total in (2, -2):

                def take(total=total):
                    b_got(total)
                    for origin, far in B_RELAYS[total]:
                        b_z(origin, far).start()
                    y_all(-total)

                when_b(-total, take)
        if n == 2 or n == 3:
            for total in ((1, -1) if n == 2 else (3, -3)):

                def take(total=total):
                    b_got(total)
                    y_all(-total)

                when_b(-total, take)
        if n == 3:

            def take4():
                b_got(4)
                y_all(4)

            when_b(4, take4)
            on_core(0, lambda: b_sib(0, 0).start())
            on_core(1, lambda: b_sib(1, 0).start())
        if n == 4:

            def arrived(core, count):
                for d in (1, 3, 2):
                    came(count * 144, yrecv.at[5 + d - 1])
                    b_sib(core, 4 - d).start()

            on_core(0, lambda: arrived(0, 8))
            on_core(1, lambda: arrived(1, 6))
        if n == 5:
            on_core(0, lambda: came(24 * 144, brecv.at[0]))
            on_core(1, lambda: came(32 * 144, brecv.at[0]))

    def step_sent():
        def core0():
            gone(7 * 144, w1zs.at[0])
            gone(24 * 144, ysend.at[0])
            gone(32 * 144, bsend.at[0])

        on_core(0, core0)
        for k, along_z in enumerate((7, 4, 7, 3)):

            @pl.when(jnp.logical_and(c == 1, zi == k))
            def _():
                gone(along_z * 144, w1zs.at[0])

        on_core(1, lambda: gone(18 * 144, ysend.at[0]))
        on_core(1, lambda: gone(24 * 144, bsend.at[0]))

    def wset(yy, cc):
        return w2.at[yy, :, cc, 0:96, :]

    def z2_send(origin, total):
        ref = blk(1, y, zz(origin), c)
        i = WAY[total]
        return rc(ref, ref, rsend.at[0], rrecv.at[i], dev(y, zz(origin + total), c))

    def z2_got(total):
        got(blk(1, y, zz(-total), c), rrecv.at[WAY[total]])

    EARLY = (0, 2, -2)
    LATE = (1, -1, 3, -3, 4)

    def y2_one(d, origin, step):
        ref = blk(1, yy_of(4 + origin), zz(step), 0)
        k = 4 if origin else 2 * (d // 2) + (step in LATE)
        return rc(ref, ref, ysend.at[1], yrecv.at[k], dev(yy_of(d), z, 0))

    def y2_send(origin):
        for d in (1, 3):
            y2_one(d, 0, origin).start()

    def y2_relay(group):
        steps = LATE if group else EARLY
        for k, (d, back) in enumerate(((1, -1), (3, 1))):
            came(len(steps) * 144, yrecv.at[2 * k + group])
            for step in steps:
                if (step in UP) == (d == 1):
                    y2_one(d, back, step).start()

    def sib2_send(d):
        ref = wset(lax.rem(y + d, 4), c)
        return rc(ref, ref, bsend.at[1], brecv.at[1], dev(y, z, 1 - c))

    Z2 = ((0, 2), (0, -2), (0, 1), (0, -1), (-2, 4), (-2, 3), (2, -3))

    def col(origin):
        zo = zz(origin)
        return w2.at[:, lax.rem(zo, 4), 1, pl.ds(pl.multiple_of(48 * lax.div(zo, 4), 16), 48), :]

    def y2_own(d):
        ref = blk(1, y, z, 1)
        return rc(ref, ref, ysend.at[1], yrecv.at[4], dev(yy_of(d), z, 1))

    def z2_col(e, origin, total):
        ref = blk(1, yy_of(e), zz(origin), 1)
        i = WAY[total]
        k = 9 + 4 * (i - 2) + e if total in (2, -2) else i
        return rc(ref, ref, rsend.at[0], rrecv.at[k], dev(y, zz(origin + total), 1))

    def when_used(e, origin, f):
        @pl.when(jnp.logical_not(jnp.logical_and(yy_of(e) == 3, zi_of(origin) > 0)))
        def _():
            f()

    def col_came(total):
        k = WAY[total]

        @pl.when(zi_of(-total) > 0)
        def _():
            came(3 * 144, rrecv.at[k])

        @pl.when(zi_of(-total) == 0)
        def _():
            came(4 * 144, rrecv.at[k])

    def col_sib(origin):
        ref = col(origin)
        return rc(ref, ref, bsend.at[1], brecv.at[1], dev(y, z, 0))

    def step2(n):
        def core0():
            if n == 0:
                for origin, total in Z2[:4]:
                    z2_send(origin, total).start()
            if n == 1:
                z2_got(2)
                z2_send(-2, 4).start()
                z2_send(-2, 3).start()
                z2_got(-2)
                z2_send(2, -3).start()
            if n == 2:
                for origin in EARLY:
                    y2_send(origin)
                for total, origin in ((1, -1), (-1, 1), (3, -3), (-3, 3), (4, 4)):
                    z2_got(total)
                    y2_send(origin)
                sib2_send(0).start()
            if n == 4:
                y2_relay(0)
            if n == 5:
                y2_relay(1)
                sib2_send(1).start()
                sib2_send(3).start()
            if n == 6:
                came(8 * 144, yrecv.at[4])
                sib2_send(2).start()

        def core1():
            if n == 0:
                for d in (2, 1, 3):
                    y2_own(d).start()
            if n == 1:
                came(3 * 144, yrecv.at[4])
                for e in (0, 1, 3, 2):

                    def send(e=e):
                        for total in AROUND:
                            z2_col(e, 0, total).start()

                    when_used(e, 0, send)
                col_sib(0).start()
            if n == 3:
                for total in (2, -2):
                    for e in (0, 1, 3, 2):

                        def relay(e=e, total=total):
                            got(blk(1, yy_of(e), zz(-total), 1), rrecv.at[9 + 4 * (WAY[total] - 2) + e])
                            for origin, far in a_relays(e, total):
                                z2_col(e, origin, far).start()

                        when_used(e, -total, relay)
                    col_sib(-total).start()
                for total in (1, -1):
                    col_came(total)
                    col_sib(-total).start()
            if n == 5:
                for total in (3, -3):
                    col_came(total)
                    col_sib(-total).start()
                for way, rows in ((4, (0, 1)), (-4, (2, 3))):
                    short = jnp.logical_and(zi_of(4) > 0, jnp.logical_or(yy_of(rows[0]) == 3, yy_of(rows[1]) == 3))

                    @pl.when(short)
                    def _():
                        came(144, rrecv.at[WAY[way]])

                    @pl.when(jnp.logical_not(short))
                    def _():
                        came(2 * 144, rrecv.at[WAY[way]])

                col_sib(4).start()

        on_core(0, core0)
        on_core(1, core1)
        if n == 7:
            came(32 * 144, brecv.at[1])

    def step2_sent():
        def core0():
            gone(7 * 144, rsend.at[0])
            gone(24 * 144, ysend.at[1])

        def core1():
            for k in range(4):

                @pl.when(zi == k)
                def _():
                    gone(((16 if k == 0 else 12) + (12 if k == 2 else 9)) * 144, rsend.at[0])

            gone(3 * 144, ysend.at[1])

        on_core(0, core0)
        on_core(1, core1)
        gone(32 * 144, bsend.at[1])

    own1.wait()

    @pl.when(j != 7)
    def _():
        came(7 * 32, st1r.at[0])
        for dy in range(3):
            for m in range(8):
                two = r1[m, 16 * (dy // 2):16 * (dy // 2) + 16].astype(F32)
                stack[m * 6:m * 6 + 6, 0:128] = two[(dy % 2) * 8:(dy % 2) * 8 + 6]
            w1[c, zi, dy, y, h] = stack[:, 0:128].astype(BF16)

    first()
    step(1)
    @pl.when(x != y)
    def _():
        came(8 * 48, st2r.at[0])

    @pl.when(x == y)
    def _():
        own2().wait()
        came(7 * 48, st2r.at[0])

    for m in range(8):
        stack[m * 6:m * 6 + 6] = r2[m].astype(F32)[0:6]
    w2[y, zi, c, pl.ds(pl.multiple_of(48 * h, 16), 48), :] = stack[...].astype(BF16)
    step2(0)
    step(2)
    xstep(1)
    xstep(3)
    step2(1)
    xstep(2)
    step(3)
    step2(2)
    step(4)
    step2(3)
    halo_wait()
    step(5)

    def conv1():
        rows = []
        for yy in range(2):
            rows.append(jnp.concatenate(
                [abuf[:, :, yy + dy].reshape(512, 384) for dy in range(3)], axis=1))
        lhs = jnp.concatenate(rows, axis=0)

        def tile(n, carry):
            rhs = jnp.concatenate(
                [w1[0, n].reshape(1152, 128), w1[1, n].reshape(1152, 128)], axis=1)
            res = jnp.dot(lhs, rhs, preferred_element_type=F32)
            for yy in range(2):
                pbuf[n, 2:10, yy] = res[yy * 512:yy * 512 + 512].reshape(8, 64, 256)
            return carry

        tile(0, 0)
        tile(1, 0)
        step2(4)
        tile(2, 0)
        tile(3, 0)

    conv1()
    step2(5)

    lane = lax.broadcasted_iota(jnp.int32, (64, 128), 1)
    row = lax.broadcasted_iota(jnp.int32, (64, 128), 0)

    def shift_down(v):
        return jnp.where(row > 0, pltpu.roll(v, 1, 0), 0.0)

    def shift_up(v):
        return jnp.where(row < 63, pltpu.roll(v, 63, 0), 0.0)

    def combine(f, carry):
        both = []
        for yy in range(2):
            def p(dt, n):
                return pbuf[n // 2, f + dt, yy, :, (n % 2) * 128:(n % 2) * 128 + 128]

            m1 = p(0, 0) + p(1, 3) + p(2, 6)
            a_lo = p(0, 0) + p(1, 3)
            mid = p(0, 1) + p(1, 4)
            b_hi = p(0, 2) + p(1, 5)
            m0 = pltpu.roll(jnp.where(lane >= 96, a_lo, mid), 32, 1) + pltpu.roll(p(2, 2), 96, 1)
            m2 = pltpu.roll(jnp.where(lane >= 64, mid, b_hi), 64, 1) + pltpu.roll(p(2, 5), 96, 1)
            hid = m1 + shift_down(m0) + shift_up(m2) + bias1
            hid = jnp.where(lane < 96, hid, 0.0)
            hbuf[f, yy] = hid
            hedge[f, yy] = hid.astype(BF16)
            both.append(hid * hid)
        sums = jnp.sum(jnp.transpose(jnp.concatenate(both, axis=0)), axis=0, keepdims=True)
        ssbuf[0, pl.ds(f, 1)] = sums
        return carry

    lax.fori_loop(0, 8, combine, 0, unroll=2)

    def ss_send(d):
        return rc(ssbuf.at[0], ssbuf.at[d], sss.at[0], ssr.at[0], (lax.rem(x + d, 4), t))

    def ss_up(d):
        return rc(ssbuf.at[0], ssbuf.at[8 + d], sss.at[1], ssr.at[2], (lax.rem(x + d, 4), t - 1))

    def ss_down(d):
        return rc(ssbuf.at[0], ssbuf.at[4 + d], sss.at[2], ssr.at[1], (lax.rem(x + d, 4), t + 1))

    def h2up():
        return rc(hedge.at[:, 0], a2h.at[1], h2s.at[0], h2r.at[0], (x, t - 1))

    def h2down():
        return rc(hedge.at[:, 1], a2h.at[0], h2s.at[1], h2r.at[1], (x, t + 1))

    for d in (2, 1, 3):
        ss_send(d).start()

    @pl.when(t > 0)
    def _():
        for d in (2, 1, 3, 0):
            ss_up(d).start()
        h2up().start()

    @pl.when(t < 63)
    def _():
        for d in (2, 1, 3, 0):
            ss_down(d).start()
        h2down().start()

    @pl.when(t == 0)
    def _():
        a2h[0] = jnp.zeros((8, 64, 128), BF16)
        ssbuf[4:8] = jnp.zeros((4, 8, 128), F32)

    @pl.when(t == 63)
    def _():
        a2h[1] = jnp.zeros((8, 64, 128), BF16)
        ssbuf[8:12] = jnp.zeros((4, 8, 128), F32)

    step2(6)
    sizes = ssbuf.at[1:4]
    got(sizes, ssr.at[0])
    ssbuf[12] = (ssbuf[0] + ssbuf[1]) + (ssbuf[2] + ssbuf[3])

    def spread(f, where, v):
        a2s[0, f + 2, where] = shift_down(v).astype(BF16)
        a2s[1, f + 2, where] = v.astype(BF16)
        a2s[2, f + 2, where] = shift_up(v).astype(BF16)

    def act2(f, carry):
        ms = jnp.transpose(jnp.broadcast_to(ssbuf[12, pl.ds(f, 1)], (128, 128))) * (1.0 / 384.0)
        u = hbuf[f].reshape(128, 128) * lax.rsqrt(ms + 1e-6) * gain2
        v = silu(u)
        for yy in range(2):
            spread(f, 1 + yy, v[64 * yy:64 * yy + 64])
        return carry

    lax.fori_loop(0, 8, act2, 0, unroll=2)

    @pl.when(t > 0)
    def _():
        got(ssbuf.at[4:8], ssr.at[1])
        got(a2h.at[0], h2r.at[1])

    @pl.when(t < 63)
    def _():
        got(ssbuf.at[8:12], ssr.at[2])
        got(a2h.at[1], h2r.at[0])

    above = (ssbuf[4] + ssbuf[5]) + (ssbuf[6] + ssbuf[7])
    below = (ssbuf[8] + ssbuf[9]) + (ssbuf[10] + ssbuf[11])
    ssbuf[13] = jnp.where(lane8 >= 64, above, below)

    def halo2(f, carry):
        ms = jnp.transpose(jnp.broadcast_to(ssbuf[13, pl.ds(f, 1)], (128, 128))) * (1.0 / 384.0)
        hv = jnp.concatenate([a2h[1, f], a2h[0, f]], axis=0).astype(F32)
        v = silu(hv * lax.rsqrt(ms + 1e-6) * gain2)
        spread(f, 0, v[64:128])
        spread(f, 3, v[0:64])
        return carry

    def halo_pair(d):
        first_frame = 2 * lax.rem(x + d, 4)
        for f in range(2):
            halo2(first_frame + f, 0)

    halo_pair(1)
    halo_pair(2)
    step2(7)

    def conv2(q):
        acc = None
        for dt in range(3):
            lhs, rhs = [], []
            for dy in range(3):
                for dx in range(3):
                    tap = dt * 9 + dy * 3 + dx
                    lhs.append(a2s[dx, pl.ds(2 * q + dt, 2), dy:dy + 2].reshape(256, 128))
                    rhs.append(w2[tap // 8, (tap % 8) // 2, tap % 2])
            part = jnp.dot(
                jnp.concatenate(lhs, axis=1), jnp.concatenate(rhs, axis=0),
                preferred_element_type=F32,
            )
            acc = part if acc is None else acc + part
        return acc

    def out_send(d):
        return rc(sendb.at[d - 1], recvb.at[d - 1], fs.at[0], fr.at[d], (lax.rem(x + d, 4), t))

    for d, ready in ((2, 3), (3, 0), (1, None)):
        sendb[d - 1] = conv2(lax.rem(x + d, 4)).astype(BF16).reshape(2, 2, 64, 384)
        out_send(d).start()
        if ready is not None:
            halo_pair(ready)
    mine = conv2(x) + bias2 + lat[...].reshape(256, 384).astype(F32)
    for d in (2, 1, 3):
        got(recvb.at[d - 1], fr.at[d])
        mine = mine + recvb[d - 1].reshape(256, 384).astype(F32)
    out[...] = mine.astype(BF16).reshape(2, 2, 64, 384)

    @pl.when(j == 7)
    def _():
        gone(7 * 32, st1s.at[0])

    @pl.when(j != 7)
    def _():
        gone(6 * 32, st1s.at[0])

    @pl.when(x != y)
    def _():
        gone(8 * 48, st2s.at[0])

    @pl.when(x == y)
    def _():
        gone(7 * 48, st2s.at[0])

    gone(3 * 768, xs.at[0])
    def ss_gone(count, i):
        size = ssbuf.at[0:count]
        rc(size, size, sss.at[i], loc.at[2], (x, t)).wait_send()

    ss_gone(3, 0)
    gone(3 * 768, fs.at[0])

    @pl.when(t > 0)
    def _():
        gone(4 * 384, ups.at[0])
        ss_gone(4, 1)
        h2up().wait_send()

    @pl.when(t < 63)
    def _():
        gone(4 * 384, dns.at[0])
        ss_gone(4, 2)
        h2down().wait_send()

    step2_sent()

    step_sent()


def per_device(latents, gain_first, conv_first, bias_first, gain_second, conv_second, bias_second):
    vm = pl.BlockSpec(memory_space=pltpu.VMEM)
    dma = pltpu.SemaphoreType.DMA
    return pl.pallas_call(
        kernel,
        out_shape=jax.ShapeDtypeStruct((2, 2, 64, 384), BF16),
        in_specs=[pl.BlockSpec(memory_space=pltpu.HBM)] * 7,
        out_specs=vm,
        scratch_shapes=[
            pltpu.VMEM((2, 2, 64, 384), BF16),
            pltpu.VMEM((4, 384), F32),
            pltpu.VMEM((27, 6, 384), BF16),
            pltpu.VMEM((27, 6, 384), BF16),
            pltpu.VMEM((8, 32, 128), BF16),
            pltpu.VMEM((8, 16, 384), BF16),
            pltpu.VMEM((48, 384), F32),
            pltpu.VMEM((4608, 128), BF16),
            pltpu.VMEM((8, 32, 128), BF16),
            pltpu.VMEM((8, 16, 384), BF16),
            pltpu.VMEM((2, 4, 3, 4, 2, 48, 128), BF16),
            pltpu.VMEM((4, 4, 2, 128, 384), BF16),
            pltpu.VMEM((4, 2, 4, 64, 384), BF16),
            pltpu.VMEM((4, 10, 2, 64, 256), F32),
            pltpu.VMEM((8, 2, 64, 128), F32),
            pltpu.VMEM((8, 2, 64, 128), BF16),
            pltpu.VMEM((14, 8, 128), F32),
            pltpu.VMEM((3, 10, 4, 64, 128), BF16),
            pltpu.VMEM((2, 8, 64, 128), BF16),
            pltpu.VMEM((3, 2, 2, 64, 384), BF16),
            pltpu.VMEM((3, 2, 2, 64, 384), BF16),
            dma((7,)), dma((1,)), dma((1,)), dma((1,)), dma((1,)), dma((3,)),
            dma((1,)), dma((9,)), dma((2,)), dma((8,)), dma((1,)), dma((17,)), dma((2,)), dma((2,)),
            dma((1,)), dma((4,)), dma((1,)), dma((1,)), dma((1,)), dma((1,)),
            dma((3,)), dma((3,)), dma((2,)), dma((2,)), dma((1,)), dma((4,)),
        ],
        compiler_params=pltpu.CompilerParams(
            collective_id=0, has_side_effects=True, vmem_limit_bytes=63 * 1024 * 1024
        ),
        cost_estimate=pl.CostEstimate(flops=4_000_000_000, bytes_accessed=8_000_000, transcendentals=400_000),
    )(
        latents, gain_first, bias_first, gain_second, bias_second,
        conv_first.reshape(27, 6, 384), conv_second.reshape(27, 6, 384),
    )


def solution(mesh):
    in_specs = (
        P("span", "tile", None, None),
        P(),
        P(None, None, None, "tile", None),
        P(),
        P(),
        P(None, None, None, "tile", None),
        P(),
    )
    out_specs = P("span", "tile", None, None)
    return jax.shard_map(
        per_device, mesh=mesh, in_specs=in_specs, out_specs=out_specs, check_vma=False
    )
```

```python
import jax
import jax.numpy as jnp
from jax import lax
from jax.experimental import pallas as pl
from jax.experimental.pallas import tpu as pltpu
from jax.sharding import PartitionSpec as P

MESH = pl.DeviceIdType.MESH
F32 = jnp.float32
BF16 = jnp.bfloat16

SLOTS = ((0, 1), (0, 0), (0, 2), (2, 0), (1, 1), (1, 0), (1, 2), (2, 2), (2, 1))


def silu(u):
    return u / (1.0 + jnp.exp(-u))


def kernel(
    lat_hbm, gain1_hbm, bias1_hbm, gain2_hbm, bias2_hbm, k1_hbm, k2_hbm, out,
    lat, vec, k1, k2, s1, s2, stack,
    ruler, r1, r2, w1, w2, abuf, pbuf, hbuf, hedge, ssbuf, a2s, a2h, sendb, recvb, hop, keep,
    ins, st1s, st1r, st2s, st2r, loc,
    w1zs, w1zr, ysend, yrecv, rsend, rrecv, bsend, brecv,
    xs, xr, ups, upr, dns, dnr, sss, ssr, h2s, h2r, fs, fr,
):
    x = lax.axis_index("span")
    t = lax.axis_index("tile")
    c = lax.rem(t, 2)
    z = lax.rem(lax.div(t, 2), 8)
    y = lax.div(t, 16)
    zi = lax.rem(z, 4)
    h = lax.div(z, 4)
    j = lax.rem(t, 8)
    g = lax.div(t, 8)

    def dev(yy, zz, cc):
        return (x, yy * 16 + zz * 2 + cc)

    def rc(src, dst, ssem, rsem, device):
        return pltpu.make_async_remote_copy(
            src_ref=src, dst_ref=dst, send_sem=ssem, recv_sem=rsem,
            device_id=device, device_id_type=MESH,
        )

    def got(ref, rsem):
        rc(ref, ref, loc.at[2], rsem, (x, t)).wait_recv()

    def gone(rows, ssem):
        size = ruler.at[0:rows]
        rc(size, size, ssem, loc.at[2], (x, t)).wait_send()

    def came(rows, rsem):
        got(ruler.at[0:rows], rsem)

    loads = [
        pltpu.make_async_copy(k1_hbm, k1, ins.at[0]),
        pltpu.make_async_copy(lat_hbm, lat, ins.at[1]),
        pltpu.make_async_copy(k2_hbm, k2, ins.at[2]),
        pltpu.make_async_copy(gain1_hbm, vec.at[0], ins.at[3]),
        pltpu.make_async_copy(bias1_hbm, vec.at[1], ins.at[4]),
        pltpu.make_async_copy(gain2_hbm, vec.at[2], ins.at[5]),
        pltpu.make_async_copy(bias2_hbm, vec.at[3], ins.at[6]),
    ]
    for load in loads:
        load.start()

    barrier = pltpu.get_barrier_semaphore()

    def hail(device):
        pl.semaphore_signal(barrier, inc=1, device_id=device, device_id_type=MESH)

    for d in range(1, 8):
        hail((x, g * 8 + lax.rem(j + d, 8)))
    for d in range(1, 4):
        hail(dev(lax.rem(y + d, 4), z, c))

    @pl.when(x != y)
    def _():
        for d in range(8):
            hail((y, x * 16 + h * 8 + lax.rem(j + d, 8)))

    for d in range(1, 4):
        hail((lax.rem(x + d, 4), t))
    for d in (1, 2, 6, 7):
        hail(dev(y, lax.rem(z + d, 8), c))

    @pl.when(t > 0)
    def _():
        for d in range(4):
            hail((lax.rem(x + d, 4), t - 1))

    @pl.when(t < 63)
    def _():
        for d in range(4):
            hail((lax.rem(x + d, 4), t + 1))

    lane8 = lax.broadcasted_iota(jnp.int32, (8, 128), 1)
    turn = lax.rem(384 - 96 * x, 384)

    def mine96(v):
        return pltpu.roll(v, turn, 1)[:, 0:128]

    loads[0].wait()
    pad2 = jnp.zeros((2, 384), F32)
    tiles = []
    for dy in range(3):
        got_slots = []
        for dt, dx in SLOTS:
            got_slots.append(mine96(jnp.concatenate([k1[dt * 9 + dy * 3 + dx].astype(F32), pad2], axis=0)))

        def at(n, by):
            return pltpu.roll(got_slots[n], by, 1) if by else got_slots[n]

        row = [
            jnp.where(lane8 < 96, at(0, 0), at(1, 96)),
            jnp.where(lane8 < 64, at(1, 96), at(2, 64)),
            jnp.where(lane8 < 32, at(2, 64), at(3, 32)),
            jnp.where(lane8 < 96, at(4, 0), at(5, 96)),
            jnp.where(lane8 < 64, at(5, 96), at(6, 64)),
            jnp.where(lane8 < 32, at(6, 64), at(7, 32)),
            jnp.where(lane8 < 96, at(8, 0), 0.0),
            jnp.zeros((8, 128), F32),
        ]
        tiles.append(row)
    for n in range(8):
        s1[n, 0:16] = jnp.concatenate([tiles[0][n], tiles[1][n]], axis=0).astype(BF16)
        s1[n, 16:32] = jnp.concatenate([tiles[2][n], jnp.zeros((8, 128), F32)], axis=0).astype(BF16)
    loads[2].wait()
    for n in range(8):
        tap = jnp.minimum(8 * x + n, 26)
        s2[n] = jnp.concatenate([k2[tap].astype(F32), jnp.zeros((10, 384), F32)], axis=0).astype(BF16)
    for load in loads[3:]:
        load.wait()
    loads[1].wait()
    gain1 = vec[0:1]
    bias2 = vec[3:4]
    bias1 = jnp.where(lane8[0:1] < 96, mine96(jnp.broadcast_to(vec[1:2], (8, 384)))[0:1], 0.0)
    gain2 = jnp.where(lane8[0:1] < 96, mine96(jnp.broadcast_to(vec[2:3], (8, 384)))[0:1], 0.0)

    w1[1, 3] = jnp.zeros((3, 4, 2, 48, 128), BF16)
    w2[:, :, :, 96:128, :] = jnp.zeros((4, 4, 2, 32, 384), BF16)
    a2s[:, 0:2] = jnp.zeros((3, 2, 4, 64, 128), BF16)

    def zero_p(i, carry):
        pbuf[i, 0:2] = jnp.zeros((2, 2, 64, 256), F32)
        return carry

    lax.fori_loop(0, 4, zero_p, 0)

    def act1(i, carry):
        v = lat[i].reshape(128, 384).astype(F32)
        ms = jnp.mean(v * v, axis=-1, keepdims=True)
        u = v * lax.rsqrt(ms + 1e-6) * gain1
        abuf[x, i, 1:3] = silu(u).astype(BF16).reshape(2, 64, 384)
        return carry

    lax.fori_loop(0, 2, act1, 0)

    many = jnp.where(x != y, 8, 0) + jnp.where(t > 0, 4, 0) + jnp.where(t < 63, 4, 0) + 17
    pl.semaphore_wait(barrier, many)

    def st1(d):
        jj = lax.rem(j + d, 8)
        return rc(s1.at[jj], r1.at[j], st1s.at[0], st1r.at[0], (x, g * 8 + jj))

    def st2(d):
        jj = lax.rem(j + d, 8)
        return rc(s2.at[jj], r2.at[j], st2s.at[0], st2r.at[0], (y, x * 16 + h * 8 + jj))

    def own2():
        return pltpu.make_async_copy(s2.at[j], r2.at[j], loc.at[1])

    for d in range(1, 8):

        @pl.when(lax.rem(j + d, 8) != 7)
        def _():
            st1(d).start()

    own1 = pltpu.make_async_copy(s1.at[j], r1.at[j], loc.at[0])
    own1.start()

    def xsend(d):
        return rc(
            abuf.at[x, :, 1:3], abuf.at[x, :, 1:3], xs.at[0], xr.at[d], (lax.rem(x + d, 4), t)
        )

    def up(src, d):
        return rc(abuf.at[src, :, 1], abuf.at[src, :, 3], ups.at[0], upr.at[0], (x, t - 1))

    def down(src, d):
        return rc(abuf.at[src, :, 2], abuf.at[src, :, 0], dns.at[0], dnr.at[0], (x, t + 1))

    def halo_send(d):
        src = lax.rem(x + 4 - d, 4)

        @pl.when(t > 0)
        def _():
            up(src, d).start()

        @pl.when(t < 63)
        def _():
            down(src, d).start()

    def xstep(d):
        src = lax.rem(x + 4 - d, 4)
        land = abuf.at[src, :, 1:3]
        got(land, xr.at[d])
        halo_send(d)

    def halo_wait():
        @pl.when(t > 0)
        def _():
            came(4 * 384, dnr.at[0])

        @pl.when(t < 63)
        def _():
            came(4 * 384, upr.at[0])

        @pl.when(t == 0)
        def _():
            abuf[:, :, 0] = jnp.zeros((4, 2, 64, 384), BF16)

        @pl.when(t == 63)
        def _():
            abuf[:, :, 3] = jnp.zeros((4, 2, 64, 384), BF16)

    for d in range(8):
        if d == 0:

            @pl.when(x != y)
            def _():
                st2(0).start()

            @pl.when(x == y)
            def _():
                own2().start()
        else:
            st2(d).start()
    for d in (2, 1, 3):
        xsend(d).start()
    halo_send(0)

    def blk(k, yy, zz, cc):
        if k == 0:
            return w1.at[cc, lax.rem(zz, 4), :, yy, lax.div(zz, 4)]
        return w2.at[yy, lax.rem(zz, 4), cc, pl.ds(pl.multiple_of(48 * lax.div(zz, 4), 16), 48), :]

    def zset(zz):
        return w1.at[1, lax.rem(zz, 4), :, :, lax.div(zz, 4)]

    def zz(s):
        return lax.rem(z + 8 + s, 8)

    WAY = {1: 0, -1: 1, 2: 2, -2: 3, 3: 4, -3: 5, 4: 6, -4: 7, 0: 8}
    AROUND = (2, -2, 1, -1)
    B_RELAYS = {2: ((-2, 4), (-2, 3)), -2: ((2, -3),)}

    def yy_of(e):
        return lax.rem(y + e, 4)

    def zi_of(origin):
        return lax.rem(z + 8 + origin, 4)

    def when_b(origin, f):
        k = zi_of(origin)

        @pl.when(jnp.logical_or(c == 0, k <= 2))
        def _():
            f()

    def on_core(core, f):
        @pl.when(c == core)
        def _():
            f()

    def a_relays(e, total):
        if total == 2:
            return ((-2, 3), (-2, 4)) if e < 2 else ((-2, 3),)
        return ((2, -3), (2, -4)) if e >= 2 else ((2, -3),)

    def b_z(origin, total):
        ref = blk(0, y, zz(origin), c)
        i = WAY[total]
        return rc(ref, ref, w1zs.at[0], w1zr.at[i], dev(y, zz(origin + total), c))

    def b_got(total):
        got(blk(0, y, zz(-total), c), w1zr.at[WAY[total]])

    UP = (0, -2, 1, 3)

    def b_y(d, s):
        ref = blk(0, y, zz(s), c)
        return rc(ref, ref, ysend.at[0], yrecv.at[5 + d - 1], dev(yy_of(d), z, c))

    def b_sib(core, d):
        yy = lax.rem(y + d, 4)
        ref = w1.at[0, :, :, yy] if core == 0 else w1.at[1, 0:3, :, yy]
        return rc(ref, ref, bsend.at[0], brecv.at[0], dev(y, z, 1 - core))

    def y_all(origin):
        for d in (2, 1, 3):
            b_y(d, origin).start()

    def first():
        def send():
            for total in AROUND:
                b_z(0, total).start()
            y_all(0)

        when_b(0, send)

    def step(n):
        if n == 1:
            for total in (2, -2):

                def take(total=total):
                    b_got(total)
                    for origin, far in B_RELAYS[total]:
                        b_z(origin, far).start()
                    y_all(-total)

                when_b(-total, take)
        if n == 2 or n == 3:
            for total in ((1, -1) if n == 2 else (3, -3)):

                def take(total=total):
                    b_got(total)
                    y_all(-total)

                when_b(-total, take)
        if n == 3:

            def take4():
                b_got(4)
                y_all(4)

            when_b(4, take4)
            on_core(0, lambda: b_sib(0, 0).start())
            on_core(1, lambda: b_sib(1, 0).start())
        if n == 4:

            def arrived(core, count):
                for d in (1, 3, 2):
                    came(count * 144, yrecv.at[5 + d - 1])
                    b_sib(core, 4 - d).start()

            on_core(0, lambda: arrived(0, 8))
            on_core(1, lambda: arrived(1, 6))
        if n == 5:
            on_core(0, lambda: came(24 * 144, brecv.at[0]))
            on_core(1, lambda: came(32 * 144, brecv.at[0]))

    def step_sent():
        def core0():
            gone(7 * 144, w1zs.at[0])
            gone(24 * 144, ysend.at[0])
            gone(32 * 144, bsend.at[0])

        on_core(0, core0)
        for k, along_z in enumerate((7, 4, 7, 3)):

            @pl.when(jnp.logical_and(c == 1, zi == k))
            def _():
                gone(along_z * 144, w1zs.at[0])

        on_core(1, lambda: gone(18 * 144, ysend.at[0]))
        on_core(1, lambda: gone(24 * 144, bsend.at[0]))

    def wset(yy, cc):
        return w2.at[yy, :, cc, 0:96, :]

    def z2_send(origin, total):
        ref = blk(1, y, zz(origin), c)
        i = WAY[total]
        return rc(ref, ref, rsend.at[0], rrecv.at[i], dev(y, zz(origin + total), c))

    def z2_got(total):
        got(blk(1, y, zz(-total), c), rrecv.at[WAY[total]])

    EARLY = (0, 2, -2)
    LATE = (1, -1, 3, -3, 4)

    def y2_one(d, origin, step):
        ref = blk(1, yy_of(4 + origin), zz(step), 0)
        k = 4 if origin else 2 * (d // 2) + (step in LATE)
        return rc(ref, ref, ysend.at[1], yrecv.at[k], dev(yy_of(d), z, 0))

    def y2_send(origin):
        for d in (1, 3):
            y2_one(d, 0, origin).start()

    def y2_relay(group):
        steps = LATE if group else EARLY
        for k, (d, back) in enumerate(((1, -1), (3, 1))):
            came(len(steps) * 144, yrecv.at[2 * k + group])
            for step in steps:
                if (step in UP) == (d == 1):
                    y2_one(d, back, step).start()

    def sib2_send(d):
        ref = wset(lax.rem(y + d, 4), c)
        return rc(ref, ref, bsend.at[1], brecv.at[1], dev(y, z, 1 - c))

    Z2 = ((0, 2), (0, -2), (0, 1), (0, -1), (-2, 4), (-2, 3), (2, -3))

    def col(origin):
        zo = zz(origin)
        return w2.at[:, lax.rem(zo, 4), 1, pl.ds(pl.multiple_of(48 * lax.div(zo, 4), 16), 48), :]

    def y2_own(d):
        ref = blk(1, y, z, 1)
        return rc(ref, ref, ysend.at[1], yrecv.at[4], dev(yy_of(d), z, 1))

    def z2_col(e, origin, total):
        ref = blk(1, yy_of(e), zz(origin), 1)
        i = WAY[total]
        k = 9 + 4 * (i - 2) + e if total in (2, -2) else i
        return rc(ref, ref, rsend.at[0], rrecv.at[k], dev(y, zz(origin + total), 1))

    def when_used(e, origin, f):
        @pl.when(jnp.logical_not(jnp.logical_and(yy_of(e) == 3, zi_of(origin) > 0)))
        def _():
            f()

    def col_came(total):
        k = WAY[total]

        @pl.when(zi_of(-total) > 0)
        def _():
            came(3 * 144, rrecv.at[k])

        @pl.when(zi_of(-total) == 0)
        def _():
            came(4 * 144, rrecv.at[k])

    def col_sib(origin):
        ref = col(origin)
        return rc(ref, ref, bsend.at[1], brecv.at[1], dev(y, z, 0))

    def step2(n):
        def core0():
            if n == 0:
                for origin, total in Z2[:4]:
                    z2_send(origin, total).start()
            if n == 1:
                z2_got(2)
                z2_send(-2, 4).start()
                z2_send(-2, 3).start()
                z2_got(-2)
                z2_send(2, -3).start()
            if n == 2:
                for origin in EARLY:
                    y2_send(origin)
            if n == 8:
                for total, origin in ((1, -1), (-1, 1), (3, -3), (-3, 3), (4, 4)):
                    z2_got(total)
                    y2_send(origin)
                sib2_send(0).start()
            if n == 4:
                y2_relay(0)
            if n == 5:
                y2_relay(1)
                sib2_send(1).start()
                sib2_send(3).start()
            if n == 6:
                came(8 * 144, yrecv.at[4])
                sib2_send(2).start()

        def core1():
            if n == 0:
                for d in (2, 1, 3):
                    y2_own(d).start()
            if n == 1:
                came(3 * 144, yrecv.at[4])
                for e in (0, 1, 3, 2):

                    def send(e=e):
                        for total in AROUND:
                            z2_col(e, 0, total).start()

                    when_used(e, 0, send)
                col_sib(0).start()
            if n == 3:
                for total in (2, -2):
                    for e in (0, 1, 3, 2):

                        def relay(e=e, total=total):
                            got(blk(1, yy_of(e), zz(-total), 1), rrecv.at[9 + 4 * (WAY[total] - 2) + e])
                            for origin, far in a_relays(e, total):
                                z2_col(e, origin, far).start()

                        when_used(e, -total, relay)
                    col_sib(-total).start()
                for total in (1, -1):
                    col_came(total)
                    col_sib(-total).start()
            if n == 5:
                for total in (3, -3):
                    col_came(total)
                    col_sib(-total).start()
                for way, rows in ((4, (0, 1)), (-4, (2, 3))):
                    short = jnp.logical_and(zi_of(4) > 0, jnp.logical_or(yy_of(rows[0]) == 3, yy_of(rows[1]) == 3))

                    @pl.when(short)
                    def _():
                        came(144, rrecv.at[WAY[way]])

                    @pl.when(jnp.logical_not(short))
                    def _():
                        came(2 * 144, rrecv.at[WAY[way]])

                col_sib(4).start()

        on_core(0, core0)
        on_core(1, core1)
        if n == 7:
            came(32 * 144, brecv.at[1])

    def step2_sent():
        def core0():
            gone(7 * 144, rsend.at[0])
            gone(24 * 144, ysend.at[1])

        def core1():
            for k in range(4):

                @pl.when(zi == k)
                def _():
                    gone(((16 if k == 0 else 12) + (12 if k == 2 else 9)) * 144, rsend.at[0])

            gone(3 * 144, ysend.at[1])

        on_core(0, core0)
        on_core(1, core1)
        gone(32 * 144, bsend.at[1])

    own1.wait()

    @pl.when(j != 7)
    def _():
        came(7 * 32, st1r.at[0])
        for dy in range(3):
            for m in range(8):
                two = r1[m, 16 * (dy // 2):16 * (dy // 2) + 16].astype(F32)
                stack[m * 6:m * 6 + 6, 0:128] = two[(dy % 2) * 8:(dy % 2) * 8 + 6]
            w1[c, zi, dy, y, h] = stack[:, 0:128].astype(BF16)

    first()
    step(1)
    @pl.when(x != y)
    def _():
        came(8 * 48, st2r.at[0])

    @pl.when(x == y)
    def _():
        own2().wait()
        came(7 * 48, st2r.at[0])

    for m in range(8):
        stack[m * 6:m * 6 + 6] = r2[m].astype(F32)[0:6]
    w2[y, zi, c, pl.ds(pl.multiple_of(48 * h, 16), 48), :] = stack[...].astype(BF16)
    step2(0)
    step(2)
    xstep(1)
    xstep(3)
    step2(1)
    xstep(2)
    step(3)
    step2(2)
    step(4)
    step2(8)
    step2(3)
    halo_wait()
    step(5)

    def conv1():
        rows = []
        for yy in range(2):
            rows.append(jnp.concatenate(
                [abuf[:, :, yy + dy].reshape(512, 384) for dy in range(3)], axis=1))
        lhs = jnp.concatenate(rows, axis=0)

        def tile(n, carry):
            rhs = jnp.concatenate(
                [w1[0, n].reshape(1152, 128), w1[1, n].reshape(1152, 128)], axis=1)
            res = jnp.dot(lhs, rhs, preferred_element_type=F32)
            for yy in range(2):
                pbuf[n, 2:10, yy] = res[yy * 512:yy * 512 + 512].reshape(8, 64, 256)
            return carry

        tile(0, 0)
        tile(1, 0)
        step2(4)
        tile(2, 0)
        tile(3, 0)

    conv1()
    step2(5)

    lane = lax.broadcasted_iota(jnp.int32, (64, 128), 1)
    row = lax.broadcasted_iota(jnp.int32, (64, 128), 0)

    def shift_down(v):
        return jnp.where(row > 0, pltpu.roll(v, 1, 0), 0.0)

    def shift_up(v):
        return jnp.where(row < 63, pltpu.roll(v, 63, 0), 0.0)

    def combine(f, carry):
        both = []
        for yy in range(2):
            def p(dt, n):
                return pbuf[n // 2, f + dt, yy, :, (n % 2) * 128:(n % 2) * 128 + 128]

            m1 = p(0, 0) + p(1, 3) + p(2, 6)
            a_lo = p(0, 0) + p(1, 3)
            mid = p(0, 1) + p(1, 4)
            b_hi = p(0, 2) + p(1, 5)
            m0 = pltpu.roll(jnp.where(lane >= 96, a_lo, mid), 32, 1) + pltpu.roll(p(2, 2), 96, 1)
            m2 = pltpu.roll(jnp.where(lane >= 64, mid, b_hi), 64, 1) + pltpu.roll(p(2, 5), 96, 1)
            hid = m1 + shift_down(m0) + shift_up(m2) + bias1
            hid = jnp.where(lane < 96, hid, 0.0)
            hbuf[f, yy] = hid
            hedge[f, yy] = hid.astype(BF16)
            both.append(hid * hid)
        sums = jnp.sum(jnp.transpose(jnp.concatenate(both, axis=0)), axis=0, keepdims=True)
        ssbuf[0, pl.ds(f, 1)] = sums
        return carry

    lax.fori_loop(0, 8, combine, 0, unroll=2)

    def ss_send(d):
        return rc(ssbuf.at[0], ssbuf.at[d], sss.at[0], ssr.at[0], (lax.rem(x + d, 4), t))

    def ss_up(d):
        return rc(ssbuf.at[0], ssbuf.at[8 + d], sss.at[1], ssr.at[2], (lax.rem(x + d, 4), t - 1))

    def ss_down(d):
        return rc(ssbuf.at[0], ssbuf.at[4 + d], sss.at[2], ssr.at[1], (lax.rem(x + d, 4), t + 1))

    def h2up():
        return rc(hedge.at[:, 0], a2h.at[1], h2s.at[0], h2r.at[0], (x, t - 1))

    def h2down():
        return rc(hedge.at[:, 1], a2h.at[0], h2s.at[1], h2r.at[1], (x, t + 1))

    for d in (2, 1, 3):
        ss_send(d).start()

    @pl.when(t > 0)
    def _():
        for d in (2, 1, 3, 0):
            ss_up(d).start()
        h2up().start()

    @pl.when(t < 63)
    def _():
        for d in (2, 1, 3, 0):
            ss_down(d).start()
        h2down().start()

    @pl.when(t == 0)
    def _():
        a2h[0] = jnp.zeros((8, 64, 128), BF16)
        ssbuf[4:8] = jnp.zeros((4, 8, 128), F32)

    @pl.when(t == 63)
    def _():
        a2h[1] = jnp.zeros((8, 64, 128), BF16)
        ssbuf[8:12] = jnp.zeros((4, 8, 128), F32)

    step2(6)
    sizes = ssbuf.at[1:4]
    got(sizes, ssr.at[0])
    ssbuf[12] = (ssbuf[0] + ssbuf[1]) + (ssbuf[2] + ssbuf[3])

    def spread(f, where, v):
        a2s[0, f + 2, where] = shift_down(v).astype(BF16)
        a2s[1, f + 2, where] = v.astype(BF16)
        a2s[2, f + 2, where] = shift_up(v).astype(BF16)

    def act2(f, carry):
        ms = jnp.transpose(jnp.broadcast_to(ssbuf[12, pl.ds(f, 1)], (128, 128))) * (1.0 / 384.0)
        u = hbuf[f].reshape(128, 128) * lax.rsqrt(ms + 1e-6) * gain2
        v = silu(u)
        for yy in range(2):
            spread(f, 1 + yy, v[64 * yy:64 * yy + 64])
        return carry

    lax.fori_loop(0, 8, act2, 0, unroll=2)

    @pl.when(t > 0)
    def _():
        got(ssbuf.at[4:8], ssr.at[1])
        got(a2h.at[0], h2r.at[1])

    @pl.when(t < 63)
    def _():
        got(ssbuf.at[8:12], ssr.at[2])
        got(a2h.at[1], h2r.at[0])

    above = (ssbuf[4] + ssbuf[5]) + (ssbuf[6] + ssbuf[7])
    below = (ssbuf[8] + ssbuf[9]) + (ssbuf[10] + ssbuf[11])
    ssbuf[13] = jnp.where(lane8 >= 64, above, below)

    def halo2(f, carry):
        ms = jnp.transpose(jnp.broadcast_to(ssbuf[13, pl.ds(f, 1)], (128, 128))) * (1.0 / 384.0)
        hv = jnp.concatenate([a2h[1, f], a2h[0, f]], axis=0).astype(F32)
        v = silu(hv * lax.rsqrt(ms + 1e-6) * gain2)
        spread(f, 0, v[64:128])
        spread(f, 3, v[0:64])
        return carry

    def halo_pair(d):
        first_frame = 2 * lax.rem(x + d, 4)
        for f in range(2):
            halo2(first_frame + f, 0)

    halo_pair(1)
    halo_pair(2)
    step2(7)

    def conv2(q):
        acc = None
        for dt in range(3):
            lhs, rhs = [], []
            for dy in range(3):
                for dx in range(3):
                    tap = dt * 9 + dy * 3 + dx
                    lhs.append(a2s[dx, pl.ds(2 * q + dt, 2), dy:dy + 2].reshape(256, 128))
                    rhs.append(w2[tap // 8, (tap % 8) // 2, tap % 2])
            part = jnp.dot(
                jnp.concatenate(lhs, axis=1), jnp.concatenate(rhs, axis=0),
                preferred_element_type=F32,
            )
            acc = part if acc is None else acc + part
        return acc

    def far_send(k):
        ref = sendb.at[1, k]
        return rc(ref, hop.at[k], fs.at[0], fr.at[k], (lax.rem(x + (1, 3)[k], 4), t))

    def out_send(k, f):
        return rc(sendb.at[2 * k, f], recvb.at[k, f], fs.at[0], fr.at[2 + k], (lax.rem(x + (1, 3)[k], 4), t))

    sendb[1] = conv2(lax.rem(x + 2, 4)).astype(BF16).reshape(2, 2, 64, 384)
    for k in range(2):
        far_send(k).start()
    halo_pair(3)
    part = conv2(lax.rem(x + 3, 4))
    sendb[2, 0] = part[0:128].astype(BF16).reshape(2, 64, 384)
    out_send(1, 0).start()
    keep[1] = part[128:256]
    halo_pair(0)
    part = conv2(lax.rem(x + 1, 4))
    sendb[0, 1] = part[128:256].astype(BF16).reshape(2, 64, 384)
    out_send(0, 1).start()
    keep[0] = part[0:128]
    mine = conv2(x) + bias2 + lat[...].reshape(256, 384).astype(F32)
    for k in range(2):
        got(hop.at[k], fr.at[k])
        sendb[2 * k, k] = (keep[k] + hop[k].reshape(128, 384).astype(F32)).astype(BF16).reshape(2, 64, 384)
        out_send(k, k).start()
    for k in range(2):
        got(recvb.at[k], fr.at[2 + k])
        mine = mine + recvb[k].reshape(256, 384).astype(F32)
    out[...] = mine.astype(BF16).reshape(2, 2, 64, 384)

    @pl.when(j == 7)
    def _():
        gone(7 * 32, st1s.at[0])

    @pl.when(j != 7)
    def _():
        gone(6 * 32, st1s.at[0])

    @pl.when(x != y)
    def _():
        gone(8 * 48, st2s.at[0])

    @pl.when(x == y)
    def _():
        gone(7 * 48, st2s.at[0])

    gone(3 * 768, xs.at[0])
    def ss_gone(count, i):
        size = ssbuf.at[0:count]
        rc(size, size, sss.at[i], loc.at[2], (x, t)).wait_send()

    ss_gone(3, 0)
    gone(3 * 768, fs.at[0])

    @pl.when(t > 0)
    def _():
        gone(4 * 384, ups.at[0])
        ss_gone(4, 1)
        h2up().wait_send()

    @pl.when(t < 63)
    def _():
        gone(4 * 384, dns.at[0])
        ss_gone(4, 2)
        h2down().wait_send()

    step2_sent()

    step_sent()


def per_device(latents, gain_first, conv_first, bias_first, gain_second, conv_second, bias_second):
    vm = pl.BlockSpec(memory_space=pltpu.VMEM)
    dma = pltpu.SemaphoreType.DMA
    return pl.pallas_call(
        kernel,
        out_shape=jax.ShapeDtypeStruct((2, 2, 64, 384), BF16),
        in_specs=[pl.BlockSpec(memory_space=pltpu.HBM)] * 7,
        out_specs=vm,
        scratch_shapes=[
            pltpu.VMEM((2, 2, 64, 384), BF16),
            pltpu.VMEM((4, 384), F32),
            pltpu.VMEM((27, 6, 384), BF16),
            pltpu.VMEM((27, 6, 384), BF16),
            pltpu.VMEM((8, 32, 128), BF16),
            pltpu.VMEM((8, 16, 384), BF16),
            pltpu.VMEM((48, 384), F32),
            pltpu.VMEM((4608, 128), BF16),
            pltpu.VMEM((8, 32, 128), BF16),
            pltpu.VMEM((8, 16, 384), BF16),
            pltpu.VMEM((2, 4, 3, 4, 2, 48, 128), BF16),
            pltpu.VMEM((4, 4, 2, 128, 384), BF16),
            pltpu.VMEM((4, 2, 4, 64, 384), BF16),
            pltpu.VMEM((4, 10, 2, 64, 256), F32),
            pltpu.VMEM((8, 2, 64, 128), F32),
            pltpu.VMEM((8, 2, 64, 128), BF16),
            pltpu.VMEM((14, 8, 128), F32),
            pltpu.VMEM((3, 10, 4, 64, 128), BF16),
            pltpu.VMEM((2, 8, 64, 128), BF16),
            pltpu.VMEM((3, 2, 2, 64, 384), BF16),
            pltpu.VMEM((2, 2, 2, 64, 384), BF16),
            pltpu.VMEM((2, 2, 64, 384), BF16),
            pltpu.VMEM((2, 128, 384), F32),
            dma((7,)), dma((1,)), dma((1,)), dma((1,)), dma((1,)), dma((3,)),
            dma((1,)), dma((9,)), dma((2,)), dma((8,)), dma((1,)), dma((17,)), dma((2,)), dma((2,)),
            dma((1,)), dma((4,)), dma((1,)), dma((1,)), dma((1,)), dma((1,)),
            dma((3,)), dma((3,)), dma((2,)), dma((2,)), dma((1,)), dma((4,)),
        ],
        compiler_params=pltpu.CompilerParams(
            collective_id=0, has_side_effects=True, vmem_limit_bytes=63 * 1024 * 1024
        ),
        cost_estimate=pl.CostEstimate(flops=4_000_000_000, bytes_accessed=8_000_000, transcendentals=400_000),
    )(
        latents, gain_first, bias_first, gain_second, bias_second,
        conv_first.reshape(27, 6, 384), conv_second.reshape(27, 6, 384),
    )


def solution(mesh):
    in_specs = (
        P("span", "tile", None, None),
        P(),
        P(None, None, None, "tile", None),
        P(),
        P(),
        P(None, None, None, "tile", None),
        P(),
    )
    out_specs = P("span", "tile", None, None)
    return jax.shard_map(
        per_device, mesh=mesh, in_specs=in_specs, out_specs=out_specs, check_vma=False
    )
```

```python
import jax
import jax.numpy as jnp
from jax import lax
from jax.experimental import pallas as pl
from jax.experimental.pallas import tpu as pltpu
from jax.sharding import PartitionSpec as P

MESH = pl.DeviceIdType.MESH
F32 = jnp.float32
BF16 = jnp.bfloat16

SLOTS = ((0, 1), (0, 0), (0, 2), (2, 0), (1, 1), (1, 0), (1, 2), (2, 2), (2, 1))


def silu(u):
    return u / (1.0 + jnp.exp(-u))


def kernel(
    lat_hbm, gain1_hbm, bias1_hbm, gain2_hbm, bias2_hbm, k1_hbm, k2_hbm, out,
    lat, vec, k1, k2, s1, s2, stack,
    ruler, r1, r2, w1, w2, abuf, pbuf, hbuf, hedge, ssbuf, a2s, a2h, sendb, recvb, hop, keep,
    ins, st1s, st1r, st2s, st2r, loc,
    w1zs, w1zr, ysend, yrecv, rsend, rrecv, bsend, brecv,
    xs, xr, ups, upr, dns, dnr, sss, ssr, h2s, h2r, fs, fr,
):
    x = lax.axis_index("span")
    t = lax.axis_index("tile")
    c = lax.rem(t, 2)
    z = lax.rem(lax.div(t, 2), 8)
    y = lax.div(t, 16)
    zi = lax.rem(z, 4)
    h = lax.div(z, 4)
    j = lax.rem(t, 8)
    g = lax.div(t, 8)

    def dev(yy, zz, cc):
        return (x, yy * 16 + zz * 2 + cc)

    def rc(src, dst, ssem, rsem, device):
        return pltpu.make_async_remote_copy(
            src_ref=src, dst_ref=dst, send_sem=ssem, recv_sem=rsem,
            device_id=device, device_id_type=MESH,
        )

    def got(ref, rsem):
        rc(ref, ref, loc.at[2], rsem, (x, t)).wait_recv()

    def gone(rows, ssem):
        size = ruler.at[0:rows]
        rc(size, size, ssem, loc.at[2], (x, t)).wait_send()

    def came(rows, rsem):
        got(ruler.at[0:rows], rsem)

    loads = [
        pltpu.make_async_copy(k1_hbm, k1, ins.at[0]),
        pltpu.make_async_copy(lat_hbm, lat, ins.at[1]),
        pltpu.make_async_copy(k2_hbm, k2, ins.at[2]),
        pltpu.make_async_copy(gain1_hbm, vec.at[0], ins.at[3]),
        pltpu.make_async_copy(bias1_hbm, vec.at[1], ins.at[4]),
        pltpu.make_async_copy(gain2_hbm, vec.at[2], ins.at[5]),
        pltpu.make_async_copy(bias2_hbm, vec.at[3], ins.at[6]),
    ]
    for load in loads:
        load.start()

    barrier = pltpu.get_barrier_semaphore()

    def hail(device):
        pl.semaphore_signal(barrier, inc=1, device_id=device, device_id_type=MESH)

    for d in range(1, 8):
        hail((x, g * 8 + lax.rem(j + d, 8)))
    for d in range(1, 4):
        hail(dev(lax.rem(y + d, 4), z, c))

    @pl.when(x != y)
    def _():
        for d in range(8):
            hail((y, x * 16 + h * 8 + lax.rem(j + d, 8)))

    for d in range(1, 4):
        hail((lax.rem(x + d, 4), t))
    for d in (1, 2, 6, 7):
        hail(dev(y, lax.rem(z + d, 8), c))

    @pl.when(t > 0)
    def _():
        for d in range(4):
            hail((lax.rem(x + d, 4), t - 1))

    @pl.when(t < 63)
    def _():
        for d in range(4):
            hail((lax.rem(x + d, 4), t + 1))

    lane8 = lax.broadcasted_iota(jnp.int32, (8, 128), 1)
    turn = lax.rem(384 - 96 * x, 384)

    def mine96(v):
        return pltpu.roll(v, turn, 1)[:, 0:128]

    loads[0].wait()
    pad2 = jnp.zeros((2, 384), F32)
    tiles = []
    for dy in range(3):
        got_slots = []
        for dt, dx in SLOTS:
            got_slots.append(mine96(jnp.concatenate([k1[dt * 9 + dy * 3 + dx].astype(F32), pad2], axis=0)))

        def at(n, by):
            return pltpu.roll(got_slots[n], by, 1) if by else got_slots[n]

        row = [
            jnp.where(lane8 < 96, at(0, 0), at(1, 96)),
            jnp.where(lane8 < 64, at(1, 96), at(2, 64)),
            jnp.where(lane8 < 32, at(2, 64), at(3, 32)),
            jnp.where(lane8 < 96, at(4, 0), at(5, 96)),
            jnp.where(lane8 < 64, at(5, 96), at(6, 64)),
            jnp.where(lane8 < 32, at(6, 64), at(7, 32)),
            jnp.where(lane8 < 96, at(8, 0), 0.0),
            jnp.zeros((8, 128), F32),
        ]
        tiles.append(row)
    for n in range(8):
        s1[n, 0:16] = jnp.concatenate([tiles[0][n], tiles[1][n]], axis=0).astype(BF16)
        s1[n, 16:32] = jnp.concatenate([tiles[2][n], jnp.zeros((8, 128), F32)], axis=0).astype(BF16)
    loads[2].wait()
    for n in range(8):
        tap = jnp.minimum(8 * x + n, 26)
        s2[n] = jnp.concatenate([k2[tap].astype(F32), jnp.zeros((10, 384), F32)], axis=0).astype(BF16)
    for load in loads[3:]:
        load.wait()
    loads[1].wait()
    gain1 = vec[0:1]
    bias2 = vec[3:4]
    bias1 = jnp.where(lane8[0:1] < 96, mine96(jnp.broadcast_to(vec[1:2], (8, 384)))[0:1], 0.0)
    gain2 = jnp.where(lane8[0:1] < 96, mine96(jnp.broadcast_to(vec[2:3], (8, 384)))[0:1], 0.0)

    w1[1, 3] = jnp.zeros((3, 4, 2, 48, 128), BF16)
    w2[:, :, :, 96:128, :] = jnp.zeros((4, 4, 2, 32, 384), BF16)
    a2s[:, 0:2] = jnp.zeros((3, 2, 4, 64, 128), BF16)

    def zero_p(i, carry):
        pbuf[i, 0:2] = jnp.zeros((2, 2, 64, 256), F32)
        return carry

    lax.fori_loop(0, 4, zero_p, 0)

    def act1(i, carry):
        v = lat[i].reshape(128, 384).astype(F32)
        ms = jnp.mean(v * v, axis=-1, keepdims=True)
        u = v * lax.rsqrt(ms + 1e-6) * gain1
        abuf[x, i, 1:3] = silu(u).astype(BF16).reshape(2, 64, 384)
        return carry

    lax.fori_loop(0, 2, act1, 0)

    many = jnp.where(x != y, 8, 0) + jnp.where(t > 0, 4, 0) + jnp.where(t < 63, 4, 0) + 17
    pl.semaphore_wait(barrier, many)

    def st1(d):
        jj = lax.rem(j + d, 8)
        return rc(s1.at[jj], r1.at[j], st1s.at[0], st1r.at[0], (x, g * 8 + jj))

    def st2(d):
        jj = lax.rem(j + d, 8)
        return rc(s2.at[jj], r2.at[j], st2s.at[0], st2r.at[0], (y, x * 16 + h * 8 + jj))

    def own2():
        return pltpu.make_async_copy(s2.at[j], r2.at[j], loc.at[1])

    for d in range(1, 8):

        @pl.when(lax.rem(j + d, 8) != 7)
        def _():
            st1(d).start()

    own1 = pltpu.make_async_copy(s1.at[j], r1.at[j], loc.at[0])
    own1.start()

    def xsend(d):
        return rc(
            abuf.at[x, :, 1:3], abuf.at[x, :, 1:3], xs.at[0], xr.at[d], (lax.rem(x + d, 4), t)
        )

    def up(src, d):
        return rc(abuf.at[src, :, 1], abuf.at[src, :, 3], ups.at[0], upr.at[0], (x, t - 1))

    def down(src, d):
        return rc(abuf.at[src, :, 2], abuf.at[src, :, 0], dns.at[0], dnr.at[0], (x, t + 1))

    def halo_send(d):
        src = lax.rem(x + 4 - d, 4)

        @pl.when(t > 0)
        def _():
            up(src, d).start()

        @pl.when(t < 63)
        def _():
            down(src, d).start()

    def xstep(d):
        src = lax.rem(x + 4 - d, 4)
        land = abuf.at[src, :, 1:3]
        got(land, xr.at[d])
        halo_send(d)

    def halo_wait():
        @pl.when(t > 0)
        def _():
            came(4 * 384, dnr.at[0])

        @pl.when(t < 63)
        def _():
            came(4 * 384, upr.at[0])

        @pl.when(t == 0)
        def _():
            abuf[:, :, 0] = jnp.zeros((4, 2, 64, 384), BF16)

        @pl.when(t == 63)
        def _():
            abuf[:, :, 3] = jnp.zeros((4, 2, 64, 384), BF16)

    for d in range(8):
        if d == 0:

            @pl.when(x != y)
            def _():
                st2(0).start()

            @pl.when(x == y)
            def _():
                own2().start()
        else:
            st2(d).start()
    for d in (2, 1, 3):
        xsend(d).start()
    halo_send(0)

    def blk(k, yy, zz, cc):
        if k == 0:
            return w1.at[cc, lax.rem(zz, 4), :, yy, lax.div(zz, 4)]
        return w2.at[yy, lax.rem(zz, 4), cc, pl.ds(pl.multiple_of(48 * lax.div(zz, 4), 16), 48), :]

    def zset(zz):
        return w1.at[1, lax.rem(zz, 4), :, :, lax.div(zz, 4)]

    def zz(s):
        return lax.rem(z + 8 + s, 8)

    WAY = {1: 0, -1: 1, 2: 2, -2: 3, 3: 4, -3: 5, 4: 6, -4: 7, 0: 8}
    AROUND = (2, -2, 1, -1)
    B_RELAYS = {2: ((-2, 4), (-2, 3)), -2: ((2, -3),)}

    def yy_of(e):
        return lax.rem(y + e, 4)

    def zi_of(origin):
        return lax.rem(z + 8 + origin, 4)

    def when_b(origin, f):
        k = zi_of(origin)

        @pl.when(jnp.logical_or(c == 0, k <= 2))
        def _():
            f()

    def on_core(core, f):
        @pl.when(c == core)
        def _():
            f()

    def a_relays(e, total):
        if total == 2:
            return ((-2, 3), (-2, 4)) if e < 2 else ((-2, 3),)
        return ((2, -3), (2, -4)) if e >= 2 else ((2, -3),)

    def b_z(origin, total):
        ref = blk(0, y, zz(origin), c)
        i = WAY[total]
        return rc(ref, ref, w1zs.at[0], w1zr.at[i], dev(y, zz(origin + total), c))

    def b_got(total):
        got(blk(0, y, zz(-total), c), w1zr.at[WAY[total]])

    UP = (0, -2, 1, 3)

    def b_y(d, s):
        ref = blk(0, y, zz(s), c)
        return rc(ref, ref, ysend.at[0], yrecv.at[5 + d - 1], dev(yy_of(d), z, c))

    def b_sib(core, d):
        yy = lax.rem(y + d, 4)
        ref = w1.at[0, :, :, yy] if core == 0 else w1.at[1, 0:3, :, yy]
        return rc(ref, ref, bsend.at[0], brecv.at[0], dev(y, z, 1 - core))

    def y_all(origin):
        for d in (2, 1, 3):
            b_y(d, origin).start()

    def first():
        def send():
            for total in AROUND:
                b_z(0, total).start()
            y_all(0)

        when_b(0, send)

    def step(n):
        if n == 1:
            for total in (2, -2):

                def take(total=total):
                    b_got(total)
                    for origin, far in B_RELAYS[total]:
                        b_z(origin, far).start()
                    y_all(-total)

                when_b(-total, take)
        if n == 2 or n == 3:
            for total in ((1, -1) if n == 2 else (3, -3)):

                def take(total=total):
                    b_got(total)
                    y_all(-total)

                when_b(-total, take)
        if n == 3:

            def take4():
                b_got(4)
                y_all(4)

            when_b(4, take4)
            on_core(0, lambda: b_sib(0, 0).start())
            on_core(1, lambda: b_sib(1, 0).start())
        if n == 4:

            def arrived(core, count):
                for d in (1, 3, 2):
                    came(count * 144, yrecv.at[5 + d - 1])
                    b_sib(core, 4 - d).start()

            on_core(0, lambda: arrived(0, 8))
            on_core(1, lambda: arrived(1, 6))
        if n == 5:
            on_core(0, lambda: came(24 * 144, brecv.at[0]))
            on_core(1, lambda: came(32 * 144, brecv.at[0]))

    def step_sent():
        def core0():
            gone(7 * 144, w1zs.at[0])
            gone(24 * 144, ysend.at[0])
            gone(32 * 144, bsend.at[0])

        on_core(0, core0)
        for k, along_z in enumerate((7, 4, 7, 3)):

            @pl.when(jnp.logical_and(c == 1, zi == k))
            def _():
                gone(along_z * 144, w1zs.at[0])

        on_core(1, lambda: gone(18 * 144, ysend.at[0]))
        on_core(1, lambda: gone(24 * 144, bsend.at[0]))

    def wset(yy, cc):
        return w2.at[yy, :, cc, 0:96, :]

    def z2_send(origin, total):
        ref = blk(1, y, zz(origin), c)
        i = WAY[total]
        return rc(ref, ref, rsend.at[0], rrecv.at[i], dev(y, zz(origin + total), c))

    def z2_got(total):
        got(blk(1, y, zz(-total), c), rrecv.at[WAY[total]])

    EARLY = (0, 2, -2)
    LATE = (1, -1, 3, -3, 4)

    def y2_one(d, origin, step):
        ref = blk(1, yy_of(4 + origin), zz(step), 0)
        k = 4 if origin else 2 * (d // 2) + (step in LATE)
        return rc(ref, ref, ysend.at[1], yrecv.at[k], dev(yy_of(d), z, 0))

    def y2_send(origin):
        for d in (1, 3):
            y2_one(d, 0, origin).start()

    def y2_relay(group):
        steps = LATE if group else EARLY
        for k, (d, back) in enumerate(((1, -1), (3, 1))):
            came(len(steps) * 144, yrecv.at[2 * k + group])
            for step in steps:
                if (step in UP) == (d == 1):
                    y2_one(d, back, step).start()

    def sib2_send(d):
        ref = wset(lax.rem(y + d, 4), c)
        return rc(ref, ref, bsend.at[1], brecv.at[1], dev(y, z, 1 - c))

    Z2 = ((0, 2), (0, -2), (0, 1), (0, -1), (-2, 4), (-2, 3), (2, -3))

    def col(origin):
        zo = zz(origin)
        return w2.at[:, lax.rem(zo, 4), 1, pl.ds(pl.multiple_of(48 * lax.div(zo, 4), 16), 48), :]

    def y2_own(d):
        ref = blk(1, y, z, 1)
        return rc(ref, ref, ysend.at[1], yrecv.at[4], dev(yy_of(d), z, 1))

    def z2_col(e, origin, total):
        ref = blk(1, yy_of(e), zz(origin), 1)
        i = WAY[total]
        k = 9 + 4 * (i - 2) + e if total in (2, -2) else i
        return rc(ref, ref, rsend.at[0], rrecv.at[k], dev(y, zz(origin + total), 1))

    def when_used(e, origin, f):
        @pl.when(jnp.logical_not(jnp.logical_and(yy_of(e) == 3, zi_of(origin) > 0)))
        def _():
            f()

    def col_came(total):
        k = WAY[total]

        @pl.when(zi_of(-total) > 0)
        def _():
            came(3 * 144, rrecv.at[k])

        @pl.when(zi_of(-total) == 0)
        def _():
            came(4 * 144, rrecv.at[k])

    def col_sib(origin):
        ref = col(origin)
        return rc(ref, ref, bsend.at[1], brecv.at[1], dev(y, z, 0))

    def step2(n):
        def core0():
            if n == 0:
                for origin, total in Z2[:4]:
                    z2_send(origin, total).start()
            if n == 1:
                z2_got(2)
                z2_send(-2, 4).start()
                z2_send(-2, 3).start()
                z2_got(-2)
                z2_send(2, -3).start()
            if n == 2:
                for origin in EARLY:
                    y2_send(origin)
            if n == 8:
                for total, origin in ((1, -1), (-1, 1), (3, -3), (-3, 3), (4, 4)):
                    z2_got(total)
                    y2_send(origin)
                sib2_send(0).start()
            if n == 4:
                y2_relay(0)
            if n == 5:
                y2_relay(1)
                sib2_send(1).start()
                sib2_send(3).start()
            if n == 6:
                came(8 * 144, yrecv.at[4])
                sib2_send(2).start()

        def core1():
            if n == 0:
                for d in (2, 1, 3):
                    y2_own(d).start()
            if n == 1:
                came(3 * 144, yrecv.at[4])
                for e in (0, 1, 3, 2):

                    def send(e=e):
                        for total in AROUND:
                            z2_col(e, 0, total).start()

                    when_used(e, 0, send)
                col_sib(0).start()
            if n == 3:
                for total in (2, -2):
                    for e in (0, 1, 3, 2):

                        def relay(e=e, total=total):
                            got(blk(1, yy_of(e), zz(-total), 1), rrecv.at[9 + 4 * (WAY[total] - 2) + e])
                            for origin, far in a_relays(e, total):
                                z2_col(e, origin, far).start()

                        when_used(e, -total, relay)
                    col_sib(-total).start()
                for total in (1, -1):
                    col_came(total)
                    col_sib(-total).start()
            if n == 5:
                for total in (3, -3):
                    col_came(total)
                    col_sib(-total).start()
                for way, rows in ((4, (0, 1)), (-4, (2, 3))):
                    short = jnp.logical_and(zi_of(4) > 0, jnp.logical_or(yy_of(rows[0]) == 3, yy_of(rows[1]) == 3))

                    @pl.when(short)
                    def _():
                        came(144, rrecv.at[WAY[way]])

                    @pl.when(jnp.logical_not(short))
                    def _():
                        came(2 * 144, rrecv.at[WAY[way]])

                col_sib(4).start()

        on_core(0, core0)
        on_core(1, core1)
        if n == 7:
            came(32 * 144, brecv.at[1])

    def step2_sent():
        def core0():
            gone(7 * 144, rsend.at[0])
            gone(24 * 144, ysend.at[1])

        def core1():
            for k in range(4):

                @pl.when(zi == k)
                def _():
                    gone(((16 if k == 0 else 12) + (12 if k == 2 else 9)) * 144, rsend.at[0])

            gone(3 * 144, ysend.at[1])

        on_core(0, core0)
        on_core(1, core1)
        gone(32 * 144, bsend.at[1])

    own1.wait()

    @pl.when(j != 7)
    def _():
        came(7 * 32, st1r.at[0])
        for dy in range(3):
            for m in range(8):
                two = r1[m, 16 * (dy // 2):16 * (dy // 2) + 16].astype(F32)
                stack[m * 6:m * 6 + 6, 0:128] = two[(dy % 2) * 8:(dy % 2) * 8 + 6]
            w1[c, zi, dy, y, h] = stack[:, 0:128].astype(BF16)

    first()
    step(1)
    @pl.when(x != y)
    def _():
        came(8 * 48, st2r.at[0])

    @pl.when(x == y)
    def _():
        own2().wait()
        came(7 * 48, st2r.at[0])

    for m in range(8):
        stack[m * 6:m * 6 + 6] = r2[m].astype(F32)[0:6]
    w2[y, zi, c, pl.ds(pl.multiple_of(48 * h, 16), 48), :] = stack[...].astype(BF16)
    step2(0)
    step(2)
    xstep(1)
    xstep(3)
    step2(1)
    xstep(2)
    step(3)
    step2(2)
    step(4)
    step2(8)
    step2(3)
    halo_wait()
    step(5)

    def conv1():
        rows = []
        for yy in range(2):
            rows.append(jnp.concatenate(
                [abuf[:, :, yy + dy].reshape(512, 384) for dy in range(3)], axis=1))
        lhs = jnp.concatenate(rows, axis=0)

        def tile(n, carry):
            rhs = jnp.concatenate(
                [w1[0, n].reshape(1152, 128), w1[1, n].reshape(1152, 128)], axis=1)
            res = jnp.dot(lhs, rhs, preferred_element_type=F32)
            for yy in range(2):
                pbuf[n, 2:10, yy] = res[yy * 512:yy * 512 + 512].reshape(8, 64, 256)
            return carry

        tile(0, 0)
        tile(1, 0)
        step2(4)
        tile(2, 0)
        tile(3, 0)

    conv1()
    step2(5)

    lane = lax.broadcasted_iota(jnp.int32, (64, 128), 1)
    row = lax.broadcasted_iota(jnp.int32, (64, 128), 0)

    def shift_down(v):
        return jnp.where(row > 0, pltpu.roll(v, 1, 0), 0.0)

    def shift_up(v):
        return jnp.where(row < 63, pltpu.roll(v, 63, 0), 0.0)

    def combine(f, carry):
        both = []
        for yy in range(2):
            def p(dt, n):
                return pbuf[n // 2, f + dt, yy, :, (n % 2) * 128:(n % 2) * 128 + 128]

            m1 = p(0, 0) + p(1, 3) + p(2, 6)
            a_lo = p(0, 0) + p(1, 3)
            mid = p(0, 1) + p(1, 4)
            b_hi = p(0, 2) + p(1, 5)
            m0 = pltpu.roll(jnp.where(lane >= 96, a_lo, mid), 32, 1) + pltpu.roll(p(2, 2), 96, 1)
            m2 = pltpu.roll(jnp.where(lane >= 64, mid, b_hi), 64, 1) + pltpu.roll(p(2, 5), 96, 1)
            hid = m1 + shift_down(m0) + shift_up(m2) + bias1
            hid = jnp.where(lane < 96, hid, 0.0)
            hbuf[f, yy] = hid
            hedge[f, yy] = hid.astype(BF16)
            both.append(hid * hid)
        sums = jnp.sum(jnp.transpose(jnp.concatenate(both, axis=0)), axis=0, keepdims=True)
        ssbuf[0, pl.ds(f, 1)] = sums
        return carry

    lax.fori_loop(0, 8, combine, 0, unroll=8)

    def ss_send(d):
        return rc(ssbuf.at[0], ssbuf.at[d], sss.at[0], ssr.at[0], (lax.rem(x + d, 4), t))

    def ss_up(d):
        return rc(ssbuf.at[0], ssbuf.at[8 + d], sss.at[1], ssr.at[2], (lax.rem(x + d, 4), t - 1))

    def ss_down(d):
        return rc(ssbuf.at[0], ssbuf.at[4 + d], sss.at[2], ssr.at[1], (lax.rem(x + d, 4), t + 1))

    def h2up():
        return rc(hedge.at[:, 0], a2h.at[1], h2s.at[0], h2r.at[0], (x, t - 1))

    def h2down():
        return rc(hedge.at[:, 1], a2h.at[0], h2s.at[1], h2r.at[1], (x, t + 1))

    for d in (2, 1, 3):
        ss_send(d).start()

    @pl.when(t > 0)
    def _():
        for d in (2, 1, 3, 0):
            ss_up(d).start()
        h2up().start()

    @pl.when(t < 63)
    def _():
        for d in (2, 1, 3, 0):
            ss_down(d).start()
        h2down().start()

    @pl.when(t == 0)
    def _():
        a2h[0] = jnp.zeros((8, 64, 128), BF16)
        ssbuf[4:8] = jnp.zeros((4, 8, 128), F32)

    @pl.when(t == 63)
    def _():
        a2h[1] = jnp.zeros((8, 64, 128), BF16)
        ssbuf[8:12] = jnp.zeros((4, 8, 128), F32)

    step2(6)
    sizes = ssbuf.at[1:4]
    got(sizes, ssr.at[0])
    ssbuf[12] = (ssbuf[0] + ssbuf[1]) + (ssbuf[2] + ssbuf[3])

    def spread(f, where, v):
        a2s[0, f + 2, where] = shift_down(v).astype(BF16)
        a2s[1, f + 2, where] = v.astype(BF16)
        a2s[2, f + 2, where] = shift_up(v).astype(BF16)

    def act2(f, carry):
        ms = jnp.transpose(jnp.broadcast_to(ssbuf[12, pl.ds(f, 1)], (128, 128))) * (1.0 / 384.0)
        u = hbuf[f].reshape(128, 128) * lax.rsqrt(ms + 1e-6) * gain2
        v = silu(u)
        for yy in range(2):
            spread(f, 1 + yy, v[64 * yy:64 * yy + 64])
        return carry

    lax.fori_loop(0, 8, act2, 0, unroll=4)

    @pl.when(t > 0)
    def _():
        got(ssbuf.at[4:8], ssr.at[1])
        got(a2h.at[0], h2r.at[1])

    @pl.when(t < 63)
    def _():
        got(ssbuf.at[8:12], ssr.at[2])
        got(a2h.at[1], h2r.at[0])

    above = (ssbuf[4] + ssbuf[5]) + (ssbuf[6] + ssbuf[7])
    below = (ssbuf[8] + ssbuf[9]) + (ssbuf[10] + ssbuf[11])
    ssbuf[13] = jnp.where(lane8 >= 64, above, below)

    def halo2(f, carry):
        ms = jnp.transpose(jnp.broadcast_to(ssbuf[13, pl.ds(f, 1)], (128, 128))) * (1.0 / 384.0)
        hv = jnp.concatenate([a2h[1, f], a2h[0, f]], axis=0).astype(F32)
        v = silu(hv * lax.rsqrt(ms + 1e-6) * gain2)
        spread(f, 0, v[64:128])
        spread(f, 3, v[0:64])
        return carry

    def halo_pair(d):
        first_frame = 2 * lax.rem(x + d, 4)
        for f in range(2):
            halo2(first_frame + f, 0)

    halo_pair(1)
    halo_pair(2)
    step2(7)

    def conv2(q):
        acc = None
        for dt in range(3):
            lhs, rhs = [], []
            for dy in range(3):
                for dx in range(3):
                    tap = dt * 9 + dy * 3 + dx
                    lhs.append(a2s[dx, pl.ds(2 * q + dt, 2), dy:dy + 2].reshape(256, 128))
                    rhs.append(w2[tap // 8, (tap % 8) // 2, tap % 2])
            part = jnp.dot(
                jnp.concatenate(lhs, axis=1), jnp.concatenate(rhs, axis=0),
                preferred_element_type=F32,
            )
            acc = part if acc is None else acc + part
        return acc

    def far_send(k):
        ref = sendb.at[1, k]
        return rc(ref, hop.at[k], fs.at[0], fr.at[k], (lax.rem(x + (1, 3)[k], 4), t))

    def out_send(k, f):
        return rc(sendb.at[2 * k, f], recvb.at[k, f], fs.at[0], fr.at[2 + k], (lax.rem(x + (1, 3)[k], 4), t))

    sendb[1] = conv2(lax.rem(x + 2, 4)).astype(BF16).reshape(2, 2, 64, 384)
    for k in range(2):
        far_send(k).start()
    halo_pair(3)
    part = conv2(lax.rem(x + 3, 4))
    sendb[2, 0] = part[0:128].astype(BF16).reshape(2, 64, 384)
    out_send(1, 0).start()
    keep[1] = part[128:256]
    halo_pair(0)
    part = conv2(lax.rem(x + 1, 4))
    sendb[0, 1] = part[128:256].astype(BF16).reshape(2, 64, 384)
    out_send(0, 1).start()
    keep[0] = part[0:128]
    mine = conv2(x) + bias2 + lat[...].reshape(256, 384).astype(F32)
    for k in range(2):
        got(hop.at[k], fr.at[k])
        sendb[2 * k, k] = (keep[k] + hop[k].reshape(128, 384).astype(F32)).astype(BF16).reshape(2, 64, 384)
        out_send(k, k).start()
    for k in range(2):
        got(recvb.at[k], fr.at[2 + k])
        mine = mine + recvb[k].reshape(256, 384).astype(F32)
    out[...] = mine.astype(BF16).reshape(2, 2, 64, 384)

    @pl.when(j == 7)
    def _():
        gone(7 * 32, st1s.at[0])

    @pl.when(j != 7)
    def _():
        gone(6 * 32, st1s.at[0])

    @pl.when(x != y)
    def _():
        gone(8 * 48, st2s.at[0])

    @pl.when(x == y)
    def _():
        gone(7 * 48, st2s.at[0])

    gone(3 * 768, xs.at[0])
    def ss_gone(count, i):
        size = ssbuf.at[0:count]
        rc(size, size, sss.at[i], loc.at[2], (x, t)).wait_send()

    ss_gone(3, 0)
    gone(3 * 768, fs.at[0])

    @pl.when(t > 0)
    def _():
        gone(4 * 384, ups.at[0])
        ss_gone(4, 1)
        h2up().wait_send()

    @pl.when(t < 63)
    def _():
        gone(4 * 384, dns.at[0])
        ss_gone(4, 2)
        h2down().wait_send()

    step2_sent()

    step_sent()


def per_device(latents, gain_first, conv_first, bias_first, gain_second, conv_second, bias_second):
    vm = pl.BlockSpec(memory_space=pltpu.VMEM)
    dma = pltpu.SemaphoreType.DMA
    return pl.pallas_call(
        kernel,
        out_shape=jax.ShapeDtypeStruct((2, 2, 64, 384), BF16),
        in_specs=[pl.BlockSpec(memory_space=pltpu.HBM)] * 7,
        out_specs=vm,
        scratch_shapes=[
            pltpu.VMEM((2, 2, 64, 384), BF16),
            pltpu.VMEM((4, 384), F32),
            pltpu.VMEM((27, 6, 384), BF16),
            pltpu.VMEM((27, 6, 384), BF16),
            pltpu.VMEM((8, 32, 128), BF16),
            pltpu.VMEM((8, 16, 384), BF16),
            pltpu.VMEM((48, 384), F32),
            pltpu.VMEM((4608, 128), BF16),
            pltpu.VMEM((8, 32, 128), BF16),
            pltpu.VMEM((8, 16, 384), BF16),
            pltpu.VMEM((2, 4, 3, 4, 2, 48, 128), BF16),
            pltpu.VMEM((4, 4, 2, 128, 384), BF16),
            pltpu.VMEM((4, 2, 4, 64, 384), BF16),
            pltpu.VMEM((4, 10, 2, 64, 256), F32),
            pltpu.VMEM((8, 2, 64, 128), F32),
            pltpu.VMEM((8, 2, 64, 128), BF16),
            pltpu.VMEM((14, 8, 128), F32),
            pltpu.VMEM((3, 10, 4, 64, 128), BF16),
            pltpu.VMEM((2, 8, 64, 128), BF16),
            pltpu.VMEM((3, 2, 2, 64, 384), BF16),
            pltpu.VMEM((2, 2, 2, 64, 384), BF16),
            pltpu.VMEM((2, 2, 64, 384), BF16),
            pltpu.VMEM((2, 128, 384), F32),
            dma((7,)), dma((1,)), dma((1,)), dma((1,)), dma((1,)), dma((3,)),
            dma((1,)), dma((9,)), dma((2,)), dma((8,)), dma((1,)), dma((17,)), dma((2,)), dma((2,)),
            dma((1,)), dma((4,)), dma((1,)), dma((1,)), dma((1,)), dma((1,)),
            dma((3,)), dma((3,)), dma((2,)), dma((2,)), dma((1,)), dma((4,)),
        ],
        compiler_params=pltpu.CompilerParams(
            collective_id=0, has_side_effects=True, vmem_limit_bytes=63 * 1024 * 1024
        ),
        cost_estimate=pl.CostEstimate(flops=4_000_000_000, bytes_accessed=8_000_000, transcendentals=400_000),
    )(
        latents, gain_first, bias_first, gain_second, bias_second,
        conv_first.reshape(27, 6, 384), conv_second.reshape(27, 6, 384),
    )


def solution(mesh):
    in_specs = (
        P("span", "tile", None, None),
        P(),
        P(None, None, None, "tile", None),
        P(),
        P(),
        P(None, None, None, "tile", None),
        P(),
    )
    out_specs = P("span", "tile", None, None)
    return jax.shard_map(
        per_device, mesh=mesh, in_specs=in_specs, out_specs=out_specs, check_vma=False
    )
```

```python
import jax
import jax.numpy as jnp
from jax import lax
from jax.experimental import pallas as pl
from jax.experimental.pallas import tpu as pltpu
from jax.sharding import PartitionSpec as P

MESH = pl.DeviceIdType.MESH
F32 = jnp.float32
BF16 = jnp.bfloat16

SLOTS = ((0, 1), (0, 0), (0, 2), (2, 0), (1, 1), (1, 0), (1, 2), (2, 2), (2, 1))


def silu(u):
    return u / (1.0 + jnp.exp(-u))


def kernel(
    lat_hbm, gain1_hbm, bias1_hbm, gain2_hbm, bias2_hbm, k1_hbm, k2_hbm, out,
    lat, vec, k1, k2, s1, s2, stack,
    ruler, r1, r2, w1, w2, abuf, pbuf, hbuf, hedge, ssbuf, a2s, a2h, sendb, recvb, hop, keep,
    ins, st1s, st1r, st2s, st2r, loc,
    w1zs, w1zr, ysend, yrecv, rsend, rrecv, bsend, brecv,
    xs, xr, ups, upr, dns, dnr, sss, ssr, h2s, h2r, fs, fr,
):
    x = lax.axis_index("span")
    t = lax.axis_index("tile")
    c = lax.rem(t, 2)
    z = lax.rem(lax.div(t, 2), 8)
    y = lax.div(t, 16)
    zi = lax.rem(z, 4)
    h = lax.div(z, 4)
    j = lax.rem(t, 8)
    g = lax.div(t, 8)

    def dev(yy, zz, cc):
        return (x, yy * 16 + zz * 2 + cc)

    def rc(src, dst, ssem, rsem, device):
        return pltpu.make_async_remote_copy(
            src_ref=src, dst_ref=dst, send_sem=ssem, recv_sem=rsem,
            device_id=device, device_id_type=MESH,
        )

    def got(ref, rsem):
        rc(ref, ref, loc.at[2], rsem, (x, t)).wait_recv()

    def gone(rows, ssem):
        size = ruler.at[0:rows]
        rc(size, size, ssem, loc.at[2], (x, t)).wait_send()

    def came(rows, rsem):
        got(ruler.at[0:rows], rsem)

    loads = [
        pltpu.make_async_copy(k1_hbm, k1, ins.at[0]),
        pltpu.make_async_copy(lat_hbm, lat, ins.at[1]),
        pltpu.make_async_copy(k2_hbm, k2, ins.at[2]),
        pltpu.make_async_copy(gain1_hbm, vec.at[0], ins.at[3]),
        pltpu.make_async_copy(bias1_hbm, vec.at[1], ins.at[4]),
        pltpu.make_async_copy(gain2_hbm, vec.at[2], ins.at[5]),
        pltpu.make_async_copy(bias2_hbm, vec.at[3], ins.at[6]),
    ]
    for load in loads:
        load.start()

    barrier = pltpu.get_barrier_semaphore()

    def hail(device):
        pl.semaphore_signal(barrier, inc=1, device_id=device, device_id_type=MESH)

    for d in range(1, 8):
        hail((x, g * 8 + lax.rem(j + d, 8)))
    for d in range(1, 4):
        hail(dev(lax.rem(y + d, 4), z, c))

    @pl.when(x != y)
    def _():
        for d in range(8):
            hail((y, x * 16 + h * 8 + lax.rem(j + d, 8)))

    for d in range(1, 4):
        hail((lax.rem(x + d, 4), t))
    for d in (1, 2, 6, 7):
        hail(dev(y, lax.rem(z + d, 8), c))

    @pl.when(t > 0)
    def _():
        for d in range(4):
            hail((lax.rem(x + d, 4), t - 1))

    @pl.when(t < 63)
    def _():
        for d in range(4):
            hail((lax.rem(x + d, 4), t + 1))

    lane8 = lax.broadcasted_iota(jnp.int32, (8, 128), 1)
    turn = lax.rem(384 - 96 * x, 384)

    def mine96(v):
        return pltpu.roll(v, turn, 1)[:, 0:128]

    loads[0].wait()
    pad2 = jnp.zeros((2, 384), F32)
    tiles = []
    for dy in range(3):
        got_slots = []
        for dt, dx in SLOTS:
            got_slots.append(mine96(jnp.concatenate([k1[dt * 9 + dy * 3 + dx].astype(F32), pad2], axis=0)))

        def at(n, by):
            return pltpu.roll(got_slots[n], by, 1) if by else got_slots[n]

        row = [
            jnp.where(lane8 < 96, at(0, 0), at(1, 96)),
            jnp.where(lane8 < 64, at(1, 96), at(2, 64)),
            jnp.where(lane8 < 32, at(2, 64), at(3, 32)),
            jnp.where(lane8 < 96, at(4, 0), at(5, 96)),
            jnp.where(lane8 < 64, at(5, 96), at(6, 64)),
            jnp.where(lane8 < 32, at(6, 64), at(7, 32)),
            jnp.where(lane8 < 96, at(8, 0), 0.0),
            jnp.zeros((8, 128), F32),
        ]
        tiles.append(row)
    for n in range(8):
        s1[n, 0:16] = jnp.concatenate([tiles[0][n], tiles[1][n]], axis=0).astype(BF16)
        s1[n, 16:32] = jnp.concatenate([tiles[2][n], jnp.zeros((8, 128), F32)], axis=0).astype(BF16)
    loads[2].wait()
    for n in range(8):
        tap = jnp.minimum(8 * x + n, 26)
        s2[n] = jnp.concatenate([k2[tap].astype(F32), jnp.zeros((10, 384), F32)], axis=0).astype(BF16)
    for load in loads[3:]:
        load.wait()
    loads[1].wait()
    gain1 = vec[0:1]
    bias2 = vec[3:4]
    bias1 = jnp.where(lane8[0:1] < 96, mine96(jnp.broadcast_to(vec[1:2], (8, 384)))[0:1], 0.0)
    gain2 = jnp.where(lane8[0:1] < 96, mine96(jnp.broadcast_to(vec[2:3], (8, 384)))[0:1], 0.0)

    w1[1, 3] = jnp.zeros((3, 4, 2, 48, 128), BF16)
    w2[:, :, :, 96:128, :] = jnp.zeros((4, 4, 2, 32, 384), BF16)
    a2s[:, 0:2] = jnp.zeros((3, 2, 4, 64, 128), BF16)

    def zero_p(i, carry):
        pbuf[i, 0:2] = jnp.zeros((2, 2, 64, 256), F32)
        return carry

    lax.fori_loop(0, 4, zero_p, 0)

    def act1(i, carry):
        v = lat[i].reshape(128, 384).astype(F32)
        ms = jnp.mean(v * v, axis=-1, keepdims=True)
        u = v * lax.rsqrt(ms + 1e-6) * gain1
        abuf[x, i, 1:3] = silu(u).astype(BF16).reshape(2, 64, 384)
        return carry

    lax.fori_loop(0, 2, act1, 0)

    many = jnp.where(x != y, 8, 0) + jnp.where(t > 0, 4, 0) + jnp.where(t < 63, 4, 0) + 17
    pl.semaphore_wait(barrier, many)

    def st1(d):
        jj = lax.rem(j + d, 8)
        return rc(s1.at[jj], r1.at[j], st1s.at[0], st1r.at[0], (x, g * 8 + jj))

    def st2(d):
        jj = lax.rem(j + d, 8)
        return rc(s2.at[jj], r2.at[j], st2s.at[0], st2r.at[0], (y, x * 16 + h * 8 + jj))

    def own2():
        return pltpu.make_async_copy(s2.at[j], r2.at[j], loc.at[1])

    for d in range(1, 8):

        @pl.when(lax.rem(j + d, 8) != 7)
        def _():
            st1(d).start()

    own1 = pltpu.make_async_copy(s1.at[j], r1.at[j], loc.at[0])
    own1.start()

    def xsend(d):
        return rc(
            abuf.at[x, :, 1:3], abuf.at[x, :, 1:3], xs.at[0], xr.at[d], (lax.rem(x + d, 4), t)
        )

    def up(src, d):
        return rc(abuf.at[src, :, 1], abuf.at[src, :, 3], ups.at[0], upr.at[0], (x, t - 1))

    def down(src, d):
        return rc(abuf.at[src, :, 2], abuf.at[src, :, 0], dns.at[0], dnr.at[0], (x, t + 1))

    def halo_send(d):
        src = lax.rem(x + 4 - d, 4)

        @pl.when(t > 0)
        def _():
            up(src, d).start()

        @pl.when(t < 63)
        def _():
            down(src, d).start()

    def xstep(d):
        src = lax.rem(x + 4 - d, 4)
        land = abuf.at[src, :, 1:3]
        got(land, xr.at[d])
        halo_send(d)

    def halo_wait():
        @pl.when(t > 0)
        def _():
            came(4 * 384, dnr.at[0])

        @pl.when(t < 63)
        def _():
            came(4 * 384, upr.at[0])

        @pl.when(t == 0)
        def _():
            abuf[:, :, 0] = jnp.zeros((4, 2, 64, 384), BF16)

        @pl.when(t == 63)
        def _():
            abuf[:, :, 3] = jnp.zeros((4, 2, 64, 384), BF16)

    for d in range(8):
        if d == 0:

            @pl.when(x != y)
            def _():
                st2(0).start()

            @pl.when(x == y)
            def _():
                own2().start()
        else:
            st2(d).start()
    for d in (2, 1, 3):
        xsend(d).start()
    halo_send(0)

    def blk(k, yy, zz, cc):
        if k == 0:
            return w1.at[cc, lax.rem(zz, 4), :, yy, lax.div(zz, 4)]
        return w2.at[yy, lax.rem(zz, 4), cc, pl.ds(pl.multiple_of(48 * lax.div(zz, 4), 16), 48), :]

    def zset(zz):
        return w1.at[1, lax.rem(zz, 4), :, :, lax.div(zz, 4)]

    def zz(s):
        return lax.rem(z + 8 + s, 8)

    WAY = {1: 0, -1: 1, 2: 2, -2: 3, 3: 4, -3: 5, 4: 6, -4: 7, 0: 8}
    AROUND = (2, -2, 1, -1)
    B_RELAYS = {2: ((-2, 4), (-2, 3)), -2: ((2, -3),)}

    def yy_of(e):
        return lax.rem(y + e, 4)

    def zi_of(origin):
        return lax.rem(z + 8 + origin, 4)

    def when_b(origin, f):
        k = zi_of(origin)

        @pl.when(jnp.logical_or(c == 0, k <= 2))
        def _():
            f()

    def on_core(core, f):
        @pl.when(c == core)
        def _():
            f()

    def a_relays(e, total):
        if total == 2:
            return ((-2, 3), (-2, 4)) if e < 2 else ((-2, 3),)
        return ((2, -3), (2, -4)) if e >= 2 else ((2, -3),)

    def b_z(origin, total):
        ref = blk(0, y, zz(origin), c)
        i = WAY[total]
        return rc(ref, ref, w1zs.at[0], w1zr.at[i], dev(y, zz(origin + total), c))

    def b_got(total):
        got(blk(0, y, zz(-total), c), w1zr.at[WAY[total]])

    UP = (0, -2, 1, 3)

    def b_y(d, s):
        ref = blk(0, y, zz(s), c)
        return rc(ref, ref, ysend.at[0], yrecv.at[5 + d - 1], dev(yy_of(d), z, c))

    def b_sib(core, d):
        yy = lax.rem(y + d, 4)
        ref = w1.at[0, :, :, yy] if core == 0 else w1.at[1, 0:3, :, yy]
        return rc(ref, ref, bsend.at[0], brecv.at[0], dev(y, z, 1 - core))

    def y_all(origin):
        for d in (2, 1, 3):
            b_y(d, origin).start()

    def first():
        def send():
            for total in AROUND:
                b_z(0, total).start()
            y_all(0)

        when_b(0, send)

    def step(n):
        if n == 1:
            for total in (2, -2):

                def take(total=total):
                    b_got(total)
                    for origin, far in B_RELAYS[total]:
                        b_z(origin, far).start()
                    y_all(-total)

                when_b(-total, take)
        if n == 2 or n == 3:
            for total in ((1, -1) if n == 2 else (3, -3)):

                def take(total=total):
                    b_got(total)
                    y_all(-total)

                when_b(-total, take)
        if n == 3:

            def take4():
                b_got(4)
                y_all(4)

            when_b(4, take4)
            on_core(0, lambda: b_sib(0, 0).start())
            on_core(1, lambda: b_sib(1, 0).start())
        if n == 4:

            def arrived(core, count):
                for d in (1, 3, 2):
                    came(count * 144, yrecv.at[5 + d - 1])
                    b_sib(core, 4 - d).start()

            on_core(0, lambda: arrived(0, 8))
            on_core(1, lambda: arrived(1, 6))
        if n == 5:
            on_core(0, lambda: came(24 * 144, brecv.at[0]))
            on_core(1, lambda: came(32 * 144, brecv.at[0]))

    def step_sent():
        def core0():
            gone(7 * 144, w1zs.at[0])
            gone(24 * 144, ysend.at[0])
            gone(32 * 144, bsend.at[0])

        on_core(0, core0)
        for k, along_z in enumerate((7, 4, 7, 3)):

            @pl.when(jnp.logical_and(c == 1, zi == k))
            def _():
                gone(along_z * 144, w1zs.at[0])

        on_core(1, lambda: gone(18 * 144, ysend.at[0]))
        on_core(1, lambda: gone(24 * 144, bsend.at[0]))

    def wset(yy, cc):
        return w2.at[yy, :, cc, 0:96, :]

    def z2_send(origin, total):
        ref = blk(1, y, zz(origin), c)
        i = WAY[total]
        return rc(ref, ref, rsend.at[0], rrecv.at[i], dev(y, zz(origin + total), c))

    def z2_got(total):
        got(blk(1, y, zz(-total), c), rrecv.at[WAY[total]])

    EARLY = (0, 2, -2)
    LATE = (1, -1, 3, -3, 4)

    def y2_one(d, origin, step):
        ref = blk(1, yy_of(4 + origin), zz(step), 0)
        k = 4 if origin else 2 * (d // 2) + (step in LATE)
        return rc(ref, ref, ysend.at[1], yrecv.at[k], dev(yy_of(d), z, 0))

    def y2_send(origin):
        for d in (1, 3):
            y2_one(d, 0, origin).start()

    def y2_relay(group):
        steps = LATE if group else EARLY
        for k, (d, back) in enumerate(((1, -1), (3, 1))):
            came(len(steps) * 144, yrecv.at[2 * k + group])
            for step in steps:
                if (step in UP) == (d == 1):
                    y2_one(d, back, step).start()

    def sib2_send(d):
        ref = wset(lax.rem(y + d, 4), c)
        return rc(ref, ref, bsend.at[1], brecv.at[1], dev(y, z, 1 - c))

    Z2 = ((0, 2), (0, -2), (0, 1), (0, -1), (-2, 4), (-2, 3), (2, -3))

    def col(origin):
        zo = zz(origin)
        return w2.at[:, lax.rem(zo, 4), 1, pl.ds(pl.multiple_of(48 * lax.div(zo, 4), 16), 48), :]

    def y2_own(d):
        ref = blk(1, y, z, 1)
        return rc(ref, ref, ysend.at[1], yrecv.at[4], dev(yy_of(d), z, 1))

    def z2_col(e, origin, total):
        ref = blk(1, yy_of(e), zz(origin), 1)
        i = WAY[total]
        k = 9 + 4 * (i - 2) + e if total in (2, -2) else i
        return rc(ref, ref, rsend.at[0], rrecv.at[k], dev(y, zz(origin + total), 1))

    def when_used(e, origin, f):
        @pl.when(jnp.logical_not(jnp.logical_and(yy_of(e) == 3, zi_of(origin) > 0)))
        def _():
            f()

    def col_came(total):
        k = WAY[total]

        @pl.when(zi_of(-total) > 0)
        def _():
            came(3 * 144, rrecv.at[k])

        @pl.when(zi_of(-total) == 0)
        def _():
            came(4 * 144, rrecv.at[k])

    def col_sib(origin):
        ref = col(origin)
        return rc(ref, ref, bsend.at[1], brecv.at[1], dev(y, z, 0))

    def step2(n):
        def core0():
            if n == 0:
                for origin, total in Z2[:4]:
                    z2_send(origin, total).start()
            if n == 1:
                z2_got(2)
                z2_send(-2, 4).start()
                z2_send(-2, 3).start()
                z2_got(-2)
                z2_send(2, -3).start()
            if n == 2:
                for origin in EARLY:
                    y2_send(origin)
            if n == 8:
                for total, origin in ((1, -1), (-1, 1), (3, -3), (-3, 3), (4, 4)):
                    z2_got(total)
                    y2_send(origin)
                sib2_send(0).start()
            if n == 4:
                y2_relay(0)
            if n == 5:
                y2_relay(1)
                sib2_send(1).start()
                sib2_send(3).start()
            if n == 6:
                came(8 * 144, yrecv.at[4])
                sib2_send(2).start()

        def core1():
            if n == 0:
                for d in (2, 1, 3):
                    y2_own(d).start()
            if n == 1:
                came(3 * 144, yrecv.at[4])
                for e in (0, 1, 3, 2):

                    def send(e=e):
                        for total in AROUND:
                            z2_col(e, 0, total).start()

                    when_used(e, 0, send)
                col_sib(0).start()
            if n == 3:
                for total in (2, -2):
                    for e in (0, 1, 3, 2):

                        def relay(e=e, total=total):
                            got(blk(1, yy_of(e), zz(-total), 1), rrecv.at[9 + 4 * (WAY[total] - 2) + e])
                            for origin, far in a_relays(e, total):
                                z2_col(e, origin, far).start()

                        when_used(e, -total, relay)
                    col_sib(-total).start()
                for total in (1, -1):
                    col_came(total)
                    col_sib(-total).start()
            if n == 5:
                for total in (3, -3):
                    col_came(total)
                    col_sib(-total).start()
                for way, rows in ((4, (0, 1)), (-4, (2, 3))):
                    short = jnp.logical_and(zi_of(4) > 0, jnp.logical_or(yy_of(rows[0]) == 3, yy_of(rows[1]) == 3))

                    @pl.when(short)
                    def _():
                        came(144, rrecv.at[WAY[way]])

                    @pl.when(jnp.logical_not(short))
                    def _():
                        came(2 * 144, rrecv.at[WAY[way]])

                col_sib(4).start()

        on_core(0, core0)
        on_core(1, core1)
        if n == 7:
            came(32 * 144, brecv.at[1])

    def step2_sent():
        def core0():
            gone(7 * 144, rsend.at[0])
            gone(24 * 144, ysend.at[1])

        def core1():
            for k in range(4):

                @pl.when(zi == k)
                def _():
                    gone(((16 if k == 0 else 12) + (12 if k == 2 else 9)) * 144, rsend.at[0])

            gone(3 * 144, ysend.at[1])

        on_core(0, core0)
        on_core(1, core1)
        gone(32 * 144, bsend.at[1])

    own1.wait()

    @pl.when(j != 7)
    def _():
        came(7 * 32, st1r.at[0])
        for dy in range(3):
            for m in range(8):
                two = r1[m, 16 * (dy // 2):16 * (dy // 2) + 16].astype(F32)
                stack[m * 6:m * 6 + 6, 0:128] = two[(dy % 2) * 8:(dy % 2) * 8 + 6]
            w1[c, zi, dy, y, h] = stack[:, 0:128].astype(BF16)

    first()
    step(1)
    @pl.when(x != y)
    def _():
        came(8 * 48, st2r.at[0])

    @pl.when(x == y)
    def _():
        own2().wait()
        came(7 * 48, st2r.at[0])

    for m in range(8):
        stack[m * 6:m * 6 + 6] = r2[m].astype(F32)[0:6]
    w2[y, zi, c, pl.ds(pl.multiple_of(48 * h, 16), 48), :] = stack[...].astype(BF16)
    step2(0)
    step(2)
    xstep(1)
    xstep(3)
    step2(1)
    xstep(2)
    step(3)
    step2(2)
    step(4)
    step2(8)
    step2(3)
    halo_wait()
    step(5)

    def conv1():
        rows = []
        for yy in range(2):
            rows.append(jnp.concatenate(
                [abuf[:, :, yy + dy].reshape(512, 384) for dy in range(3)], axis=1))
        lhs = jnp.concatenate(rows, axis=0)

        def tile(n, carry):
            rhs = jnp.concatenate(
                [w1[0, n].reshape(1152, 128), w1[1, n].reshape(1152, 128)], axis=1)
            res = jnp.dot(lhs, rhs, preferred_element_type=F32)
            for yy in range(2):
                pbuf[n, 2:10, yy] = res[yy * 512:yy * 512 + 512].reshape(8, 64, 256)
            return carry

        tile(0, 0)
        tile(1, 0)
        step2(4)
        tile(2, 0)
        tile(3, 0)

    conv1()
    step2(5)

    lane = lax.broadcasted_iota(jnp.int32, (64, 128), 1)
    row = lax.broadcasted_iota(jnp.int32, (64, 128), 0)

    def shift_down(v):
        return jnp.where(row > 0, pltpu.roll(v, 1, 0), 0.0)

    def shift_up(v):
        return jnp.where(row < 63, pltpu.roll(v, 63, 0), 0.0)

    def combine(f, carry):
        both = []
        for yy in range(2):
            def p(dt, n):
                return pbuf[n // 2, f + dt, yy, :, (n % 2) * 128:(n % 2) * 128 + 128]

            m1 = p(0, 0) + p(1, 3) + p(2, 6)
            a_lo = p(0, 0) + p(1, 3)
            mid = p(0, 1) + p(1, 4)
            b_hi = p(0, 2) + p(1, 5)
            m0 = pltpu.roll(jnp.where(lane >= 96, a_lo, mid), 32, 1) + pltpu.roll(p(2, 2), 96, 1)
            m2 = pltpu.roll(jnp.where(lane >= 64, mid, b_hi), 64, 1) + pltpu.roll(p(2, 5), 96, 1)
            hid = m1 + shift_down(m0) + shift_up(m2) + bias1
            hid = jnp.where(lane < 96, hid, 0.0)
            hbuf[f, yy] = hid
            hedge[f, yy] = hid.astype(BF16)
            both.append(hid * hid)
        sums = jnp.sum(jnp.transpose(jnp.concatenate(both, axis=0)), axis=0, keepdims=True)
        ssbuf[0, pl.ds(f, 1)] = sums
        return carry

    lax.fori_loop(0, 8, combine, 0, unroll=8)

    def ss_send(d):
        return rc(ssbuf.at[0], ssbuf.at[d], sss.at[0], ssr.at[0], (lax.rem(x + d, 4), t))

    def ss_up(d):
        return rc(ssbuf.at[0], ssbuf.at[8 + d], sss.at[1], ssr.at[2], (lax.rem(x + d, 4), t - 1))

    def ss_down(d):
        return rc(ssbuf.at[0], ssbuf.at[4 + d], sss.at[2], ssr.at[1], (lax.rem(x + d, 4), t + 1))

    def h2up():
        return rc(hedge.at[:, 0], a2h.at[1], h2s.at[0], h2r.at[0], (x, t - 1))

    def h2down():
        return rc(hedge.at[:, 1], a2h.at[0], h2s.at[1], h2r.at[1], (x, t + 1))

    for d in (2, 1, 3):
        ss_send(d).start()

    @pl.when(t > 0)
    def _():
        for d in (2, 1, 3, 0):
            ss_up(d).start()
        h2up().start()

    @pl.when(t < 63)
    def _():
        for d in (2, 1, 3, 0):
            ss_down(d).start()
        h2down().start()

    @pl.when(t == 0)
    def _():
        a2h[0] = jnp.zeros((8, 64, 128), BF16)
        ssbuf[4:8] = jnp.zeros((4, 8, 128), F32)

    @pl.when(t == 63)
    def _():
        a2h[1] = jnp.zeros((8, 64, 128), BF16)
        ssbuf[8:12] = jnp.zeros((4, 8, 128), F32)

    step2(6)
    sizes = ssbuf.at[1:4]
    got(sizes, ssr.at[0])
    ssbuf[12] = (ssbuf[0] + ssbuf[1]) + (ssbuf[2] + ssbuf[3])

    def spread(f, where, v):
        a2s[0, f + 2, where] = shift_down(v).astype(BF16)
        a2s[1, f + 2, where] = v.astype(BF16)
        a2s[2, f + 2, where] = shift_up(v).astype(BF16)

    def act2(f, carry):
        ms = jnp.transpose(jnp.broadcast_to(ssbuf[12, pl.ds(f, 1)], (128, 128))) * (1.0 / 384.0)
        u = hbuf[f].reshape(128, 128) * lax.rsqrt(ms + 1e-6) * gain2
        v = silu(u)
        for yy in range(2):
            spread(f, 1 + yy, v[64 * yy:64 * yy + 64])
        return carry

    lax.fori_loop(0, 8, act2, 0, unroll=8)

    @pl.when(t > 0)
    def _():
        got(ssbuf.at[4:8], ssr.at[1])
        got(a2h.at[0], h2r.at[1])

    @pl.when(t < 63)
    def _():
        got(ssbuf.at[8:12], ssr.at[2])
        got(a2h.at[1], h2r.at[0])

    above = (ssbuf[4] + ssbuf[5]) + (ssbuf[6] + ssbuf[7])
    below = (ssbuf[8] + ssbuf[9]) + (ssbuf[10] + ssbuf[11])
    ssbuf[13] = jnp.where(lane8 >= 64, above, below)

    def halo2(f, carry):
        ms = jnp.transpose(jnp.broadcast_to(ssbuf[13, pl.ds(f, 1)], (128, 128))) * (1.0 / 384.0)
        hv = jnp.concatenate([a2h[1, f], a2h[0, f]], axis=0).astype(F32)
        v = silu(hv * lax.rsqrt(ms + 1e-6) * gain2)
        spread(f, 0, v[64:128])
        spread(f, 3, v[0:64])
        return carry

    def halo_pair(d):
        first_frame = 2 * lax.rem(x + d, 4)
        for f in range(2):
            halo2(first_frame + f, 0)

    halo_pair(1)
    halo_pair(2)
    step2(7)

    def conv2(q):
        acc = None
        for dt in range(3):
            lhs, rhs = [], []
            for dy in range(3):
                for dx in range(3):
                    tap = dt * 9 + dy * 3 + dx
                    lhs.append(a2s[dx, pl.ds(2 * q + dt, 2), dy:dy + 2].reshape(256, 128))
                    rhs.append(w2[tap // 8, (tap % 8) // 2, tap % 2])
            part = jnp.dot(
                jnp.concatenate(lhs, axis=1), jnp.concatenate(rhs, axis=0),
                preferred_element_type=F32,
            )
            acc = part if acc is None else acc + part
        return acc

    def far_send(k):
        ref = sendb.at[1, k]
        return rc(ref, hop.at[k], fs.at[0], fr.at[k], (lax.rem(x + (1, 3)[k], 4), t))

    def out_send(k, f):
        return rc(sendb.at[2 * k, f], recvb.at[k, f], fs.at[0], fr.at[2 + k], (lax.rem(x + (1, 3)[k], 4), t))

    sendb[1] = conv2(lax.rem(x + 2, 4)).astype(BF16).reshape(2, 2, 64, 384)
    for k in range(2):
        far_send(k).start()
    halo_pair(3)
    part = conv2(lax.rem(x + 3, 4))
    sendb[2, 0] = part[0:128].astype(BF16).reshape(2, 64, 384)
    out_send(1, 0).start()
    keep[1] = part[128:256]
    halo_pair(0)
    part = conv2(lax.rem(x + 1, 4))
    sendb[0, 1] = part[128:256].astype(BF16).reshape(2, 64, 384)
    out_send(0, 1).start()
    keep[0] = part[0:128]
    mine = conv2(x) + bias2 + lat[...].reshape(256, 384).astype(F32)
    for k in range(2):
        got(hop.at[k], fr.at[k])
        sendb[2 * k, k] = (keep[k] + hop[k].reshape(128, 384).astype(F32)).astype(BF16).reshape(2, 64, 384)
        out_send(k, k).start()
    for k in range(2):
        got(recvb.at[k], fr.at[2 + k])
        mine = mine + recvb[k].reshape(256, 384).astype(F32)
    out[...] = mine.astype(BF16).reshape(2, 2, 64, 384)

    @pl.when(j == 7)
    def _():
        gone(7 * 32, st1s.at[0])

    @pl.when(j != 7)
    def _():
        gone(6 * 32, st1s.at[0])

    @pl.when(x != y)
    def _():
        gone(8 * 48, st2s.at[0])

    @pl.when(x == y)
    def _():
        gone(7 * 48, st2s.at[0])

    gone(3 * 768, xs.at[0])
    def ss_gone(count, i):
        size = ssbuf.at[0:count]
        rc(size, size, sss.at[i], loc.at[2], (x, t)).wait_send()

    ss_gone(3, 0)
    gone(3 * 768, fs.at[0])

    @pl.when(t > 0)
    def _():
        gone(4 * 384, ups.at[0])
        ss_gone(4, 1)
        h2up().wait_send()

    @pl.when(t < 63)
    def _():
        gone(4 * 384, dns.at[0])
        ss_gone(4, 2)
        h2down().wait_send()

    step2_sent()

    step_sent()


def per_device(latents, gain_first, conv_first, bias_first, gain_second, conv_second, bias_second):
    vm = pl.BlockSpec(memory_space=pltpu.VMEM)
    dma = pltpu.SemaphoreType.DMA
    return pl.pallas_call(
        kernel,
        out_shape=jax.ShapeDtypeStruct((2, 2, 64, 384), BF16),
        in_specs=[pl.BlockSpec(memory_space=pltpu.HBM)] * 7,
        out_specs=vm,
        scratch_shapes=[
            pltpu.VMEM((2, 2, 64, 384), BF16),
            pltpu.VMEM((4, 384), F32),
            pltpu.VMEM((27, 6, 384), BF16),
            pltpu.VMEM((27, 6, 384), BF16),
            pltpu.VMEM((8, 32, 128), BF16),
            pltpu.VMEM((8, 16, 384), BF16),
            pltpu.VMEM((48, 384), F32),
            pltpu.VMEM((4608, 128), BF16),
            pltpu.VMEM((8, 32, 128), BF16),
            pltpu.VMEM((8, 16, 384), BF16),
            pltpu.VMEM((2, 4, 3, 4, 2, 48, 128), BF16),
            pltpu.VMEM((4, 4, 2, 128, 384), BF16),
            pltpu.VMEM((4, 2, 4, 64, 384), BF16),
            pltpu.VMEM((4, 10, 2, 64, 256), F32),
            pltpu.VMEM((8, 2, 64, 128), F32),
            pltpu.VMEM((8, 2, 64, 128), BF16),
            pltpu.VMEM((14, 8, 128), F32),
            pltpu.VMEM((3, 10, 4, 64, 128), BF16),
            pltpu.VMEM((2, 8, 64, 128), BF16),
            pltpu.VMEM((3, 2, 2, 64, 384), BF16),
            pltpu.VMEM((2, 2, 2, 64, 384), BF16),
            pltpu.VMEM((2, 2, 64, 384), BF16),
            pltpu.VMEM((2, 128, 384), F32),
            dma((7,)), dma((1,)), dma((1,)), dma((1,)), dma((1,)), dma((3,)),
            dma((1,)), dma((9,)), dma((2,)), dma((8,)), dma((1,)), dma((17,)), dma((2,)), dma((2,)),
            dma((1,)), dma((4,)), dma((1,)), dma((1,)), dma((1,)), dma((1,)),
            dma((3,)), dma((3,)), dma((2,)), dma((2,)), dma((1,)), dma((4,)),
        ],
        compiler_params=pltpu.CompilerParams(
            collective_id=0, has_side_effects=True, vmem_limit_bytes=63 * 1024 * 1024
        ),
        cost_estimate=pl.CostEstimate(flops=4_000_000_000, bytes_accessed=8_000_000, transcendentals=400_000),
    )(
        latents, gain_first, bias_first, gain_second, bias_second,
        conv_first.reshape(27, 6, 384), conv_second.reshape(27, 6, 384),
    )


def solution(mesh):
    in_specs = (
        P("span", "tile", None, None),
        P(),
        P(None, None, None, "tile", None),
        P(),
        P(),
        P(None, None, None, "tile", None),
        P(),
    )
    out_specs = P("span", "tile", None, None)
    return jax.shard_map(
        per_device, mesh=mesh, in_specs=in_specs, out_specs=out_specs, check_vma=False
    )
```
